32 devices in a mesh: seq: 2 (over x), wt: 16 (over z, y, core).
Axes of the slice: x: 2, y: 2, z: 4, core: 2. Of those that a mesh axis runs over, the one named last changes fastest.
Arguments:
- activations: bfloat16 [16, 2048, 1024], P('wt', 'seq'), may hold values from -6 to 6
- w_query: bfloat16 [1024, 1024], P('wt'), may hold values from -0.1875 to 0.1875
- w_key: bfloat16 [1024, 1024], P('wt'), may hold values from -0.1875 to 0.1875
- w_value: bfloat16 [1024, 1024], P('wt'), may hold values from -0.1875 to 0.1875
- w_gate: bfloat16 [1024, 1024], P('wt'), may hold values from -0.1875 to 0.1875
- w_out: bfloat16 [1024, 1024], P('wt'), may hold values from -0.1875 to 0.1875
- w_first: bfloat16 [1024, 2816], P('wt'), may hold values from -0.1875 to 0.1875
- w_second: bfloat16 [1024, 2816], P('wt'), may hold values from -0.1875 to 0.1875
- w_down: bfloat16 [2816, 1024], P('wt'), may hold values from -0.109375 to 0.109375
- decay_rate: float32 [8], replicated, may hold values from 0.0002 to 0.04
- seq_lengths: int32 [16, 2], P('wt'), may hold values from 0 to 2048, as said below
- out_grad: bfloat16 [16, 2048, 1024], P('wt', 'seq'), may hold values from -6 to 6
Outputs:
- layer_out: bfloat16 [16, 2048, 1024], P('wt', 'seq')
- input_grad: bfloat16 [16, 2048, 1024], P('wt', 'seq')
- grad_query: float32 [1024, 1024], P('wt')
- grad_key: float32 [1024, 1024], P('wt')
- grad_value: float32 [1024, 1024], P('wt')
- grad_gate: float32 [1024, 1024], P('wt')
- grad_out: float32 [1024, 1024], P('wt')
- grad_first: float32 [1024, 2816], P('wt')
- grad_second: float32 [1024, 2816], P('wt')
- grad_down: float32 [2816, 1024], P('wt')
The draws below stay inside these ranges and needn't reach their ends.
Inputs may be any that keep to these rules, and one draw needn't show every extreme that they name: `seq_lengths`: row g lists the lengths of group g's sequences in token order, then zeros; each nonzero length is a multiple of 1024, a row sums to 2048, and no sequence crosses a multiple of min(4096, 2048) tokens.
All inputs are finite; a program needn't handle non-finite values.
Results may differ from the reference program's by a relative error of at most 0.02.
Values may be sent and summed in bfloat16 or wider, within the bound.
No kernel may reach another device: no remote copies, remote signals or barrier semaphores. Data moves between devices by JAX's collectives and lax.ppermute only.
A program may use at most 256 MiB of HBM per device.

```python
import math
import jax
import jax.numpy as jnp
from jax import lax

D = 1024
H = 8
FF = 2816
HD = 128
MIN_LEN = 1024
MAX_LEN = 4096
BLK = 512
GROUP_TOK = 2048
GROUPS = 16
UNITS = 2


def draw_seq_lengths(key, part):
    span_units = min(MAX_LEN, GROUP_TOK) // MIN_LEN
    unit_index = jnp.arange(UNITS, dtype=jnp.int32)
    cut_after = jax.random.randint(key, (GROUPS, UNITS), 0, 2, dtype=jnp.int32)
    cut_after = jnp.where(((unit_index + 1) % span_units == 0)[None, :], 1, cut_after)
    opening = (jnp.arange(GROUPS, dtype=jnp.int32)[:, None] == 0) & (unit_index[None, :] < span_units - 1)
    cut_after = jnp.where(opening, 0, cut_after)
    seq_of = (jnp.cumsum(cut_after, axis=1) - cut_after).astype(jnp.int32)
    unit_counts = jnp.sum((seq_of[:, None, :] == unit_index[None, :, None]).astype(jnp.int32), axis=2)
    return (unit_counts * MIN_LEN).astype(jnp.int32)


def raised(entries, rng, source, target, blocks, factor):
    def block_of(dim):
        return (jnp.arange(entries.shape[dim]) // (entries.shape[dim] // blocks)).reshape((-1,) + (1,) * (entries.ndim - 1 - dim))

    near = jax.random.permutation(rng, blocks)[block_of(target)]
    other_side = (block_of(target) + blocks // 2) % blocks
    return jnp.where((block_of(source) == near) | (block_of(source) == other_side), factor * entries, entries)


def block_levels(own_key, shape, split, least, top_value):
    factor_of, own = 1.0, jax.random.fold_in(own_key, 6)
    for dim, parts in split:
        draws = jnp.exp(jax.random.uniform(jax.random.fold_in(own, dim), (parts,), jnp.float32, least / len(split), top_value / len(split)))
        factor_of = factor_of * jnp.repeat(draws, shape[dim] // parts).reshape([-1 if axis == dim else 1 for axis in range(len(shape))])
    return factor_of


def scatter_about(key, extent, deviation, limit, pieces=(), kind=jnp.bfloat16):
    gain = block_levels(key, extent, pieces, -0.22, 0.18) if pieces else 1.0
    result = jax.random.normal(key, extent, jnp.float32) * deviation * gain
    return jnp.minimum(jnp.maximum(result, -limit), limit).astype(kind)


def gaussian_with(rng, extent, scale, most, cuts, heavy, kind=jnp.bfloat16):
    drawn = scale * jax.random.normal(rng, extent, jnp.float32)
    if cuts:
        drawn = drawn * block_levels(rng, extent, cuts, -0.22, 0.18)
    return jnp.clip(raised(drawn, jax.random.fold_in(rng, 3), *heavy), -most, most).astype(kind)


def setup_inputs(seed: int = 0) -> dict:
    splits = jax.random.split(jax.random.key(seed), 13)
    return {
        "activations": gaussian_with(splits[0], (GROUPS, GROUP_TOK, D), 1.0, 6.0, ((0, 16), (1, 2)), (0, 2, 16, 2.0)),
        "w_query": scatter_about(splits[1], (D, D), D ** -0.5, 0.1875, ((0, 16),)),
        "w_key": scatter_about(splits[2], (D, D), D ** -0.5, 0.1875, ((0, 16),)),
        "w_value": scatter_about(splits[3], (D, D), D ** -0.5, 0.1875, ((0, 16),)),
        "w_gate": scatter_about(splits[4], (D, D), D ** -0.5, 0.1875, ((0, 16),)),
        "w_out": scatter_about(splits[5], (D, D), D ** -0.5, 0.1875, ((0, 16),)),
        "w_first": scatter_about(splits[6], (D, FF), D ** -0.5, 0.1875, ((0, 16),)),
        "w_second": scatter_about(splits[7], (D, FF), D ** -0.5, 0.1875, ((0, 16),)),
        "w_down": scatter_about(splits[8], (FF, D), FF ** -0.5, 0.109375, ((0, 16),)),
        "decay_rate": jnp.clip(jnp.exp(jax.random.uniform(splits[9], (H,), jnp.float32, math.log(0.0002), math.log(0.04))), 0.0002, 0.04),
        "seq_lengths": draw_seq_lengths(jax.random.fold_in(splits[12], 71), 0),
        "out_grad": scatter_about(splits[11], (GROUPS, GROUP_TOK, D), 1.0, 6.0, ((0, 16), (1, 2))),
    }


@jax.custom_vjp
def low(v):
    return lax.optimization_barrier(v.astype(jnp.bfloat16)).astype(jnp.float32)

@jax.custom_vjp
def low_back(v):
    return v

def low_keep(v):
    return (low(v), None)

def low_pass(kept, grad):
    return (grad,)

def back_keep(v):
    return (v, None)

def back_low(kept, grad):
    return (low(grad),)
low.defvjp(low_keep, low_pass)
low_back.defvjp(back_keep, back_low)
epsilon = 1e-06
head_floor = 1.0
highest = lax.Precision.HIGHEST

def matmul(left, right):
    return jnp.dot(left, right, precision=highest, preferred_element_type=jnp.float32)

def simple_norm(tensor, added=epsilon):
    return tensor * lax.rsqrt(lax.optimization_barrier(jnp.mean(tensor * tensor, axis=-1, keepdims=True)) + added)

def swish_act(tensor):
    return tensor * jax.nn.sigmoid(tensor)

def seq_layout(lengths, row_count):
    starts = (jnp.cumsum(lengths) - lengths).astype(jnp.int32)
    live_slot = lengths > 0
    token_index = jnp.arange(row_count, dtype=jnp.int32)
    has_begun = (starts[None, :] <= token_index[:, None]) & live_slot[None, :]
    first_token = lax.optimization_barrier(jnp.max(jnp.where(has_begun, starts[None, :], 0), axis=1)).astype(jnp.int32)
    position = (token_index - first_token).astype(jnp.float32)
    block_first = jnp.arange(row_count // BLK, dtype=jnp.int32) * BLK
    is_start = jnp.any((starts[None, :] == block_first[:, None]) & live_slot[None, :], axis=1)
    return (position, is_start)

def decay_tables(head_rates):
    offsets = jnp.arange(BLK, dtype=jnp.float32)
    distance = offsets[:, None] - offsets[None, :]
    decay_mask = jnp.where(distance[None] >= 0, jnp.exp(-head_rates[:, None, None] * jnp.maximum(distance, 0.0)[None]), 0.0)
    decay_in = jnp.exp(-head_rates[None, :] * (offsets[:, None] + 1.0))
    decay_out = jnp.exp(-head_rates[None, :] * (BLK - 1.0 - offsets[:, None]))
    across = jnp.exp(-head_rates * BLK)
    return (decay_mask, decay_in, decay_out, across)

def rotate(heads, position):
    frequency = 10000.0 ** (-jnp.arange(HD, dtype=jnp.float32) / HD)
    angles = position[:, None] * frequency[None, :]
    cosine = jnp.cos(angles)[:, None, :]
    sine_table = jnp.sin(angles)[:, None, :]
    return low(jnp.concatenate([heads * cosine, heads * sine_table], axis=-1))

def mixer(query_heads, key_heads, value_heads, head_rates, position, is_start):
    query_rot = rotate(query_heads, position)
    key_rot = rotate(key_heads, position)
    decay_mask, decay_in, decay_out, across = decay_tables(head_rates)
    nblocks = query_rot.shape[0] // BLK
    keep_next = 1.0 - jnp.concatenate([is_start[1:], jnp.ones((1,), dtype=bool)]).astype(jnp.float32)

    def blocked(tensor):
        return tensor.reshape((nblocks, BLK) + tensor.shape[1:])

    def one_block(carried, item):
        query_block, key_block, value_block, keep_flag = item
        scores = low_back(jnp.einsum('ihc,jhc->hij', query_block, key_block, precision=highest))
        weights = low(scores * decay_mask)
        inner_part = jnp.einsum('hij,jhd->ihd', weights, value_block, precision=highest)
        outer_part = jnp.einsum('ihc,hcd->ihd', query_block, carried, precision=highest) * decay_in[:, :, None]
        fresh_sum = jnp.einsum('jhc,jhd->hcd', key_block * decay_out[:, :, None], value_block, precision=highest)
        carried = keep_flag * (across[:, None, None] * carried + fresh_sum)
        return (carried, inner_part + outer_part)
    zero_state = jnp.zeros((H, 2 * HD, HD), jnp.float32)
    final_state, mixed = lax.scan(jax.checkpoint(one_block), zero_state, (blocked(query_rot), blocked(key_rot), blocked(value_heads), keep_next))
    return mixed.reshape(query_heads.shape)

def forward(x_float, w_query, w_key, w_value, w_gate, w_out, w_first, w_second, w_down, head_rates, position, is_start):
    row_count = x_float.shape[0]
    head_shape = (row_count, H, HD)
    normed_in = low(simple_norm(x_float))
    query_act = low_back(low(swish_act(low_back(matmul(normed_in, w_query)))))
    key_act = low_back(low(swish_act(low_back(matmul(normed_in, w_key)))))
    value_act = low_back(low(matmul(normed_in, w_value)))
    gate_act = low_back(low(matmul(normed_in, w_gate)))
    mixed = low_back(mixer(query_act.reshape(head_shape), key_act.reshape(head_shape), value_act.reshape(head_shape), head_rates, position, is_start))
    gated = low_back(low(simple_norm(mixed, head_floor) * gate_act.reshape(head_shape))).reshape(row_count, D)
    residual = x_float + low_back(matmul(gated, w_out))
    normed_mid = low(simple_norm(residual))
    first_proj = low_back(matmul(normed_mid, w_first))
    second_proj = low_back(matmul(normed_mid, w_second))
    middle = low_back(low(first_proj * second_proj))
    return residual + low_back(matmul(middle, w_down))

def reference(activations, w_query, w_key, w_value, w_gate, w_out, w_first, w_second, w_down, decay_rate, seq_lengths, out_grad):
    weights = (w_query.astype(jnp.float32), w_key.astype(jnp.float32), w_value.astype(jnp.float32), w_gate.astype(jnp.float32), w_out.astype(jnp.float32), w_first.astype(jnp.float32), w_second.astype(jnp.float32), w_down.astype(jnp.float32))

    def one_group(totals, item):
        x_group, grad_group, lengths = item
        position, is_start = seq_layout(lengths, x_group.shape[0])

        def run(x_float, weight_set):
            return forward(x_float, weight_set[0], weight_set[1], weight_set[2], weight_set[3], weight_set[4], weight_set[5], weight_set[6], weight_set[7], decay_rate, position, is_start)
        layer_value, pullback = jax.vjp(run, x_group.astype(jnp.float32), weights)
        grad_x, grad_weights = pullback(grad_group.astype(jnp.float32))
        totals = jax.tree.map(lambda total, extra: total + extra, totals, grad_weights)
        return (totals, (layer_value.astype(jnp.bfloat16), grad_x.astype(jnp.bfloat16)))
    zero_totals = jax.tree.map(jnp.zeros_like, weights)
    totals, outputs = lax.scan(one_group, zero_totals, (activations, out_grad, seq_lengths))
    return (outputs[0], outputs[1], totals[0], totals[1], totals[2], totals[3], totals[4], totals[5], totals[6], totals[7])
```

```python
import jax
import jax.numpy as jnp
from jax import lax
from jax.experimental import pallas as pl
from jax.experimental.pallas import tpu as pltpu
from jax.sharding import PartitionSpec as P

H = 8
HD = 128
CH = 256
TILE = 256
MIN_LEN = 1024
VMEM_LIMIT = 60 << 20

epsilon = 1e-06
head_floor = 1.0
bf16 = jnp.bfloat16
f32 = jnp.float32


def nn(left, right):
    return jnp.dot(left, right, preferred_element_type=f32)


def nt(left, right):
    return lax.dot_general(left, right, (((1,), (1,)), ((), ())), preferred_element_type=f32)


def tn(left, right):
    return lax.dot_general(left, right, (((0,), (0,)), ((), ())), preferred_element_type=f32)


def struct(shape, dtype):
    return jax.ShapeDtypeStruct(shape, dtype)


def fixed(shape):
    zeros = (0,) * len(shape)
    return pl.BlockSpec(shape, lambda i: zeros, pipeline_mode=pl.Buffered(1))


def columns(rows, width):
    return pl.BlockSpec((rows, width), lambda i: (0, i))


def row_tiles(height, cols):
    return pl.BlockSpec((height, cols), lambda i: (i, 0))


def smem():
    return pl.BlockSpec(memory_space=pltpu.SMEM)


def params():
    return pltpu.CompilerParams(vmem_limit_bytes=VMEM_LIMIT)


def cost(flops, moved):
    return pl.CostEstimate(flops=flops, bytes_accessed=moved, transcendentals=0)


def decay_in_of(rate):
    row = lax.broadcasted_iota(jnp.int32, (CH, HD), 0).astype(f32)
    return jnp.exp(-rate * (row + 1.0))


def decay_out_of(rate):
    row = lax.broadcasted_iota(jnp.int32, (CH, HD), 0).astype(f32)
    return jnp.exp(-rate * (CH - 1.0 - row))


def double(table):
    return jnp.concatenate([table, table], axis=1)


def rotated(heads, cosine, sine):
    return jnp.concatenate([heads * cosine, heads * sine], axis=1)


def swish(raw):
    return raw * jax.nn.sigmoid(raw)


def swish_slope(raw):
    sig = jax.nn.sigmoid(raw)
    return sig * (1.0 + raw * (1.0 - sig))


def head_columns(s):
    return slice(s * HD, (s + 1) * HD)


def key_value_kernel(rates, across, a, wk, wv, cosine, sine, kraw_out, v_out, state_out):
    step = pl.program_id(0)
    rows = a.shape[0]
    kraw = nn(a[...], wk[...])
    v_out[...] = nn(a[...], wv[...]).astype(bf16)
    kraw_out[...] = kraw.astype(bf16)
    for s in range(TILE // HD):
        head = step * (TILE // HD) + s
        cols = head_columns(s)
        tail = double(decay_out_of(rates[head]))
        state = jnp.zeros((HD, 2 * HD), f32)
        for c in range(rows // CH):
            span = slice(c * CH, (c + 1) * CH)
            key = swish(kraw[span, cols])
            faded = rotated(key, cosine[span, :], sine[span, :]) * tail
            state = across[head] * state + tn(v_out[span, cols], faded.astype(bf16))
        state_out[s] = state


def key_value(rates, across, a, wk, wv, cosine, sine):
    rows, depth = a.shape
    width = wk.shape[1]
    return pl.pallas_call(
        key_value_kernel,
        grid=(width // TILE,),
        in_specs=[
            smem(),
            smem(),
            fixed((rows, depth)),
            columns(depth, TILE),
            columns(depth, TILE),
            fixed((rows, HD)),
            fixed((rows, HD)),
        ],
        out_specs=[
            columns(rows, TILE),
            columns(rows, TILE),
            pl.BlockSpec((TILE // HD, HD, 2 * HD), lambda i: (i, 0, 0)),
        ],
        out_shape=[
            struct((rows, width), bf16),
            struct((rows, width), bf16),
            struct((H, HD, 2 * HD), f32),
        ],
        compiler_params=params(),
        cost_estimate=cost(4 * rows * depth * width, 2 * (3 * rows * depth + 2 * depth * width)),
        name="key_value",
    )(rates, across, a, wk, wv, cosine, sine)


def mix_kernel(
    rates, across, a, wq, wg, kraw, v, cosine, sine, state_in, qraw_out, u_out, o_out, gated_out
):
    step = pl.program_id(0)
    rows = a.shape[0]
    qraw = nn(a[...], wq[...])
    qraw_out[...] = qraw.astype(bf16)
    u_out[...] = nn(a[...], wg[...]).astype(bf16)
    row = lax.broadcasted_iota(jnp.int32, (CH, CH), 0)
    col = lax.broadcasted_iota(jnp.int32, (CH, CH), 1)
    distance = (row - col).astype(f32)
    for s in range(TILE // HD):
        head = step * (TILE // HD) + s
        cols = head_columns(s)
        rate = rates[head]
        tail = double(decay_out_of(rate))
        lead = decay_in_of(rate)
        mask = jnp.where(distance >= 0, jnp.exp(-rate * jnp.maximum(distance, 0.0)), 0.0)
        state = state_in[s]
        for c in range(rows // CH):
            span = slice(c * CH, (c + 1) * CH)
            cos_c, sin_c = cosine[span, :], sine[span, :]
            query = rotated(swish(qraw[span, cols]), cos_c, sin_c).astype(bf16)
            key_float = rotated(swish(kraw[span, cols].astype(f32)), cos_c, sin_c)
            key = key_float.astype(bf16)
            value = v[span, cols]
            weights = (nt(query, key) * mask).astype(bf16)
            o = nn(weights, value) + lead * nt(query, state.astype(bf16))
            state = across[head] * state + tn(value, (key_float * tail).astype(bf16))
            o_out[span, cols] = o.astype(bf16)
            scale = lax.rsqrt(jnp.mean(o * o, axis=1, keepdims=True) + head_floor)
            gated_out[span, cols] = (o * scale * u_out[span, cols].astype(f32)).astype(bf16)


def mix(rates, across, a, wq, wg, kraw, v, cosine, sine, state_in):
    rows, depth = a.shape
    width = wq.shape[1]
    return pl.pallas_call(
        mix_kernel,
        grid=(width // TILE,),
        in_specs=[
            smem(),
            smem(),
            fixed((rows, depth)),
            columns(depth, TILE),
            columns(depth, TILE),
            columns(rows, TILE),
            columns(rows, TILE),
            fixed((rows, HD)),
            fixed((rows, HD)),
            pl.BlockSpec((TILE // HD, HD, 2 * HD), lambda i: (i, 0, 0)),
        ],
        out_specs=[columns(rows, TILE)] * 4,
        out_shape=[struct((rows, width), bf16)] * 4,
        compiler_params=params(),
        cost_estimate=cost(8 * rows * depth * width, 2 * (7 * rows * depth + 2 * depth * width)),
        name="mix",
    )(rates, across, a, wq, wg, kraw, v, cosine, sine, state_in)


def residual_kernel(x, gated, wo, h1_out, bn_out, bnt_out):
    h1 = x[...].astype(f32) + nn(gated[...], wo[...])
    h1_out[...] = h1
    normed = h1 * lax.rsqrt(jnp.mean(h1 * h1, axis=1, keepdims=True) + epsilon)
    low = normed.astype(bf16)
    bn_out[...] = low
    bnt_out[...] = low.T


def residual(x, gated, wo):
    rows, depth = x.shape
    part = 512
    return pl.pallas_call(
        residual_kernel,
        grid=(rows // part,),
        in_specs=[row_tiles(part, depth), row_tiles(part, depth), fixed(wo.shape)],
        out_specs=[row_tiles(part, depth), row_tiles(part, depth), columns(depth, part)],
        out_shape=[
            struct((rows, depth), f32),
            struct((rows, depth), bf16),
            struct((depth, rows), bf16),
        ],
        compiler_params=params(),
        cost_estimate=cost(2 * rows * depth * depth, 14 * rows * depth),
        name="residual",
    )(x, gated, wo)


def feed_kernel(
    h1, bn, bnt, og, w1, w2, wd, g1_out, g2_out, gd_out, y_out, dh1_out, dattn_out, total, dbn
):
    step = pl.program_id(0)

    @pl.when(step == 0)
    def _():
        total[...] = h1[...]
        dbn[...] = jnp.zeros_like(dbn)

    first = nn(bn[...], w1[...])
    second = nn(bn[...], w2[...])
    middle = (first * second).astype(bf16)
    dmid = nt(og[...], wd[...])
    total[...] += nn(middle, wd[...])
    d_first = (dmid * second).astype(bf16)
    d_second = (dmid * first).astype(bf16)
    dbn[...] += nt(d_first, w1[...]) + nt(d_second, w2[...])
    g1_out[...] = nn(bnt[...], d_first).astype(bf16)
    g2_out[...] = nn(bnt[...], d_second).astype(bf16)
    gd_out[...] = tn(middle, og[...]).astype(bf16)

    @pl.when(step == pl.num_programs(0) - 1)
    def _():
        y_out[...] = total[...].astype(bf16)
        hidden = h1[...]
        scale = lax.rsqrt(jnp.mean(hidden * hidden, axis=1, keepdims=True) + epsilon)
        normed = hidden * scale
        incoming = dbn[...]
        dh1 = og[...].astype(f32) + scale * (
            incoming - normed * jnp.mean(normed * incoming, axis=1, keepdims=True)
        )
        dh1_out[...] = dh1
        dattn_out[...] = dh1.astype(bf16)


def feed(h1, bn, bnt, og, w1, w2, wd):
    rows, depth = h1.shape
    hidden = w1.shape[1]
    return pl.pallas_call(
        feed_kernel,
        grid=(hidden // TILE,),
        in_specs=[
            fixed((rows, depth)),
            fixed((rows, depth)),
            fixed((depth, rows)),
            fixed((rows, depth)),
            columns(depth, TILE),
            columns(depth, TILE),
            row_tiles(TILE, depth),
        ],
        out_specs=[
            columns(depth, TILE),
            columns(depth, TILE),
            row_tiles(TILE, depth),
            fixed((rows, depth)),
            fixed((rows, depth)),
            fixed((rows, depth)),
        ],
        out_shape=[
            struct((depth, hidden), bf16),
            struct((depth, hidden), bf16),
            struct((hidden, depth), bf16),
            struct((rows, depth), bf16),
            struct((rows, depth), f32),
            struct((rows, depth), bf16),
        ],
        scratch_shapes=[pltpu.VMEM((rows, depth), f32), pltpu.VMEM((rows, depth), f32)],
        compiler_params=params(),
        cost_estimate=cost(18 * rows * depth * hidden, 12 * depth * hidden + 20 * rows * depth),
        name="feed",
    )(h1, bn, bnt, og, w1, w2, wd)


def gate_back_kernel(
    rates, across, dattn, wo, o_in, u_in, qraw, cosine, sine, du_out, do_out, back_out
):
    step = pl.program_id(0)
    rows = dattn.shape[0]
    dgated = nt(dattn[...], wo[...]).astype(bf16).astype(f32)
    for s in range(TILE // HD):
        head = step * (TILE // HD) + s
        cols = head_columns(s)
        lead = double(decay_in_of(rates[head]))
        back = jnp.zeros((HD, 2 * HD), f32)
        for c in reversed(range(rows // CH)):
            span = slice(c * CH, (c + 1) * CH)
            o = o_in[span, cols].astype(f32)
            scale = lax.rsqrt(jnp.mean(o * o, axis=1, keepdims=True) + head_floor)
            normed = o * scale
            incoming = dgated[span, cols]
            du_out[span, cols] = (incoming * normed).astype(bf16)
            spread = incoming * u_in[span, cols].astype(f32)
            do = scale * (spread - normed * jnp.mean(normed * spread, axis=1, keepdims=True))
            low = do.astype(bf16)
            do_out[span, cols] = low
            query = rotated(
                swish(qraw[span, cols].astype(f32)), cosine[span, :], sine[span, :]
            )
            back = across[head] * back + tn(low, (query * lead).astype(bf16))
        back_out[s] = back


def gate_back(rates, across, dattn, wo, o_in, u_in, qraw, cosine, sine):
    rows, depth = dattn.shape
    return pl.pallas_call(
        gate_back_kernel,
        grid=(depth // TILE,),
        in_specs=[
            smem(),
            smem(),
            fixed((rows, depth)),
            row_tiles(TILE, depth),
            columns(rows, TILE),
            columns(rows, TILE),
            columns(rows, TILE),
            fixed((rows, HD)),
            fixed((rows, HD)),
        ],
        out_specs=[
            columns(rows, TILE),
            columns(rows, TILE),
            pl.BlockSpec((TILE // HD, HD, 2 * HD), lambda i: (i, 0, 0)),
        ],
        out_shape=[
            struct((rows, depth), bf16),
            struct((rows, depth), bf16),
            struct((H, HD, 2 * HD), f32),
        ],
        compiler_params=params(),
        cost_estimate=cost(3 * rows * depth * depth, 16 * rows * depth),
        name="gate_back",
    )(rates, across, dattn, wo, o_in, u_in, qraw, cosine, sine)


def mix_back_kernel(
    rates,
    across,
    qraw,
    kraw,
    v,
    do_in,
    cosine,
    sine,
    state_in,
    back_in,
    dq_out,
    dk_out,
    dv_out,
    query_s,
    key_s,
):
    step = pl.program_id(0)
    rows = qraw.shape[0]
    count = rows // CH
    row = lax.broadcasted_iota(jnp.int32, (CH, CH), 0)
    col = lax.broadcasted_iota(jnp.int32, (CH, CH), 1)
    distance = (row - col).astype(f32)
    for s in range(TILE // HD):
        head = step * (TILE // HD) + s
        cols = head_columns(s)
        rate = rates[head]
        lead = double(decay_in_of(rate))
        tail = double(decay_out_of(rate))
        mask = jnp.where(distance >= 0, jnp.exp(-rate * jnp.maximum(distance, 0.0)), 0.0)
        mask_t = jnp.where(distance <= 0, jnp.exp(rate * jnp.minimum(distance, 0.0)), 0.0)
        state = state_in[s]
        states = []
        for c in range(count):
            span = slice(c * CH, (c + 1) * CH)
            key_float = rotated(
                swish(kraw[span, cols].astype(f32)), cosine[span, :], sine[span, :]
            )
            key_s[span, :] = key_float.astype(bf16)
            states.append(state.astype(bf16))
            if c < count - 1:
                state = across[head] * state + tn(v[span, cols], (key_float * tail).astype(bf16))
        back = back_in[s]
        for c in reversed(range(count)):
            span = slice(c * CH, (c + 1) * CH)
            cos_c, sin_c = cosine[span, :], sine[span, :]
            query_raw = qraw[span, cols].astype(f32)
            query_float = rotated(swish(query_raw), cos_c, sin_c)
            query = query_float.astype(bf16)
            key = key_s[span, :]
            value = v[span, cols]
            do = do_in[span, cols]
            back_low = back.astype(bf16)
            weights_t = (nt(key, query) * mask_t).astype(bf16)
            dscore = (nt(do, value) * mask).astype(bf16)
            dscore_t = (nt(value, do) * mask_t).astype(bf16)
            dqr = nn(dscore, key) + lead * nn(do, states[c])
            dkr = nn(dscore_t, query) + tail * nn(value, back_low)
            dv = nn(weights_t, do) + tail[:, :HD] * nt(key, back_low)
            back = across[head] * back + tn(do, (query_float * lead).astype(bf16))
            dq = dqr[:, :HD] * cos_c + dqr[:, HD:] * sin_c
            dk = dkr[:, :HD] * cos_c + dkr[:, HD:] * sin_c
            dq_out[span, cols] = (dq * swish_slope(query_raw)).astype(bf16)
            dk_out[span, cols] = (dk * swish_slope(kraw[span, cols].astype(f32))).astype(bf16)
            dv_out[span, cols] = dv.astype(bf16)


def mix_back(rates, across, qraw, kraw, v, do_in, cosine, sine, state_in, back_in):
    rows, width = qraw.shape
    heads = pl.BlockSpec((TILE // HD, HD, 2 * HD), lambda i: (i, 0, 0))
    return pl.pallas_call(
        mix_back_kernel,
        grid=(width // TILE,),
        in_specs=[
            smem(),
            smem(),
            columns(rows, TILE),
            columns(rows, TILE),
            columns(rows, TILE),
            columns(rows, TILE),
            fixed((rows, HD)),
            fixed((rows, HD)),
            heads,
            heads,
        ],
        out_specs=[columns(rows, TILE)] * 3,
        out_shape=[struct((rows, width), bf16)] * 3,
        scratch_shapes=[pltpu.VMEM((rows, 2 * HD), bf16), pltpu.VMEM((rows, 2 * HD), bf16)],
        compiler_params=params(),
        cost_estimate=cost(4 * rows * width * width, 16 * rows * width),
        name="mix_back",
    )(rates, across, qraw, kraw, v, do_in, cosine, sine, state_in, back_in)


def weight_grads_kernel(left_t, *refs):
    half = len(refs) // 2
    for incoming, out in zip(refs[:half], refs[half:]):
        out[...] = nn(left_t[...], incoming[...]).astype(bf16)


def weight_grads(left_t, *incoming):
    depth, rows = left_t.shape
    count = len(incoming)
    width = incoming[0].shape[1]
    return pl.pallas_call(
        weight_grads_kernel,
        grid=(width // TILE,),
        in_specs=[fixed((depth, rows))] + [columns(rows, TILE)] * count,
        out_specs=[columns(depth, TILE)] * count,
        out_shape=[struct((depth, width), bf16)] * count,
        compiler_params=params(),
        cost_estimate=cost(
            2 * count * rows * depth * width, 2 * count * (rows + depth) * width
        ),
        name="weight_grads",
    )(left_t, *incoming)


def input_back_kernel(x, dh1, dq, dk, dv, du, wq, wk, wv, wg, out, total):
    step = pl.program_id(0)
    part = nt(dq[...], wq[...]) + nt(dk[...], wk[...]) + nt(dv[...], wv[...]) + nt(du[...], wg[...])

    @pl.when(step == 0)
    def _():
        total[...] = part

    @pl.when(step > 0)
    def _():
        total[...] += part

    @pl.when(step == pl.num_programs(0) - 1)
    def _():
        hidden = x[...].astype(f32)
        scale = lax.rsqrt(jnp.mean(hidden * hidden, axis=1, keepdims=True) + epsilon)
        normed = hidden * scale
        incoming = total[...]
        out[...] = (
            dh1[...]
            + scale * (incoming - normed * jnp.mean(normed * incoming, axis=1, keepdims=True))
        ).astype(bf16)


def input_back(x, dh1, grads, weights):
    rows, depth = x.shape
    width = weights[0].shape[1]
    return pl.pallas_call(
        input_back_kernel,
        grid=(width // TILE,),
        in_specs=[fixed((rows, depth)), fixed((rows, depth))]
        + [columns(rows, TILE)] * 4
        + [columns(depth, TILE)] * 4,
        out_specs=fixed((rows, depth)),
        out_shape=struct((rows, depth), bf16),
        scratch_shapes=[pltpu.VMEM((rows, depth), f32)],
        compiler_params=params(),
        cost_estimate=cost(8 * rows * depth * width, 8 * rows * depth + 16 * width * depth),
        name="input_back",
    )(x, dh1, *grads, *weights)


def body(
    activations,
    w_query,
    w_key,
    w_value,
    w_gate,
    w_out,
    w_first,
    w_second,
    w_down,
    decay_rate,
    seq_lengths,
    out_grad,
):
    seq_count = lax.axis_size("seq")
    seq_index = lax.axis_index("seq")
    x = activations[0]
    og = out_grad[0]
    rows = x.shape[0]
    assert MIN_LEN % rows == 0

    def gathered(w):
        return lax.all_gather(w, "wt", axis=0, tiled=True)

    full_key, full_value = gathered(w_key), gathered(w_value)
    full_query, full_gate = gathered(w_query), gathered(w_gate)
    full_out, full_first = gathered(w_out), gathered(w_first)
    full_second, full_down = gathered(w_second), gathered(w_down)

    lengths = seq_lengths[0]
    starts = jnp.cumsum(lengths) - lengths
    begin = seq_index * rows
    begun = (starts <= begin) & (lengths > 0)
    first_token = jnp.max(jnp.where(begun, starts, 0))
    keep = jnp.where(begin == first_token, 0.0, 1.0).astype(f32)
    position = (begin - first_token + jnp.arange(rows, dtype=jnp.int32)).astype(f32)
    frequency = 10000.0 ** (-jnp.arange(HD, dtype=f32) / HD)
    angles = position[:, None] * frequency[None, :]
    cosine, sine = jnp.cos(angles), jnp.sin(angles)
    across = jnp.exp(-decay_rate * CH)
    whole = jnp.exp(-decay_rate * rows)[:, None, None]

    x_float = x.astype(f32)
    a = (
        x_float * lax.rsqrt(jnp.mean(x_float * x_float, axis=-1, keepdims=True) + epsilon)
    ).astype(bf16)
    a_t = a.T

    kraw, v, own_state = key_value(decay_rate, across, a, full_key, full_value, cosine, sine)
    ahead = [(i, i + 1) for i in range(seq_count - 1)]
    state_in = jnp.zeros_like(own_state)
    for _ in range(seq_count - 1):
        sent = (whole * state_in + own_state).astype(bf16)
        state_in = keep * lax.ppermute(sent, "seq", ahead).astype(f32)

    qraw, u, o, gated = mix(
        decay_rate, across, a, full_query, full_gate, kraw, v, cosine, sine, state_in
    )
    h1, bn, bn_t = residual(x, gated, full_out)
    g_first, g_second, g_down, layer_out, dh1, dattn = feed(
        h1, bn, bn_t, og, full_first, full_second, full_down
    )
    du, do, own_back = gate_back(
        decay_rate, across, dattn, full_out, o, u, qraw, cosine, sine
    )
    behind = [(i + 1, i) for i in range(seq_count - 1)]
    back_in = jnp.zeros_like(own_back)
    for _ in range(seq_count - 1):
        sent = (keep * (whole * back_in + own_back)).astype(bf16)
        back_in = lax.ppermute(sent, "seq", behind).astype(f32)
    (g_out,) = weight_grads(gated.T, dattn)
    dq, dk, dv = mix_back(
        decay_rate, across, qraw, kraw, v, do, cosine, sine, state_in, back_in
    )
    g_query, g_key, g_value, g_gate = weight_grads(a_t, dq, dk, dv, du)
    input_grad = input_back(
        x, dh1, (dq, dk, dv, du), (full_query, full_key, full_value, full_gate)
    )

    def owned(g):
        return lax.psum_scatter(g, "wt", scatter_dimension=0, tiled=True)

    shares = [
        owned(g)
        for g in (g_query, g_key, g_value, g_gate, g_out, g_first, g_second, g_down)
    ]
    totals = [lax.psum(share, "seq").astype(f32) for share in shares]
    return (layer_out[None], input_grad[None], *totals)


def solution(mesh):
    weight = P("wt", None)
    tokens = P("wt", "seq", None)
    return jax.shard_map(
        body,
        mesh=mesh,
        in_specs=(tokens,) + (weight,) * 8 + (P(), weight, tokens),
        out_specs=(tokens, tokens) + (weight,) * 8,
        check_vma=False,
    )
```

```python
import jax
import jax.numpy as jnp
from jax import lax
from jax.experimental import pallas as pl
from jax.experimental.pallas import tpu as pltpu
from jax.sharding import PartitionSpec as P

H = 8
HD = 128
CH = 256
TILE = 256
HALF = 128
SHARDS = 16
MIN_LEN = 1024
VMEM_LIMIT = 60 << 20

epsilon = 1e-06
head_floor = 1.0
bf16 = jnp.bfloat16
f32 = jnp.float32


def nn(left, right):
    return jnp.dot(left, right, preferred_element_type=f32)


def nt(left, right):
    return lax.dot_general(left, right, (((1,), (1,)), ((), ())), preferred_element_type=f32)


def tn(left, right):
    return lax.dot_general(left, right, (((0,), (0,)), ((), ())), preferred_element_type=f32)


def struct(shape, dtype):
    return jax.ShapeDtypeStruct(shape, dtype)


def fixed(shape):
    zeros = (0,) * len(shape)
    return pl.BlockSpec(shape, lambda i: zeros, pipeline_mode=pl.Buffered(1))


def columns(rows, width):
    return pl.BlockSpec((rows, width), lambda i: (0, i))


def row_tiles(height, cols):
    return pl.BlockSpec((height, cols), lambda i: (i, 0))


def smem():
    return pl.BlockSpec(memory_space=pltpu.SMEM)


def params():
    return pltpu.CompilerParams(vmem_limit_bytes=VMEM_LIMIT)


def cost(flops, moved):
    return pl.CostEstimate(flops=flops, bytes_accessed=moved, transcendentals=0)


class Gathered:
    def __init__(self, first, second, order):
        self.first, self.second, self.order = first, second, order

    def specs(self, height, index, chips=8):
        def of(core):
            if chips == 8:
                return pl.BlockSpec((8, 1, height, TILE), lambda i: (0, core, index(i), 0))
            return pl.BlockSpec((chips, 1, height, TILE), lambda i: (i, core, index(i), 0))

        return [of(0), of(self.first.shape[1] - 1)]

    def arrays(self):
        return [self.first, self.second]


def join(order, first, second, held, rows=slice(None)):
    held[:, order, rows, :] = first[:, 0]
    held[:, 1 - order, rows, :] = second[:, 0]


def emit(coords, stage, own, other, rows, order):
    z0, y0, c0, x0 = coords[0], coords[1], coords[2], coords[3]
    for x in range(2):
        x_rel = x + x0 - 2 * x * x0
        cols = slice(x * HALF, (x + 1) * HALF)
        for y_rel in range(2):
            y = y_rel + y0 - 2 * y_rel * y0
            for z_rel in range(4):
                z = lax.rem(z0 + z_rel, 4)
                shard = z * 4 + y * 2
                lead = (x_rel, y_rel) if order == "xy" else (y_rel, x_rel)
                own[(*lead, z_rel, rows)] = stage[shard + c0, :, cols]
                other[(*lead, z_rel, rows)] = stage[shard + 1 - c0, :, cols]


def decay_in_of(rate):
    row = lax.broadcasted_iota(jnp.int32, (CH, HD), 0).astype(f32)
    return jnp.exp(-rate * (row + 1.0))


def decay_out_of(rate):
    row = lax.broadcasted_iota(jnp.int32, (CH, HD), 0).astype(f32)
    return jnp.exp(-rate * (CH - 1.0 - row))


def double(table):
    return jnp.concatenate([table, table], axis=1)


def rotated(heads, cosine, sine):
    return jnp.concatenate([heads * cosine, heads * sine], axis=1)


def swish(raw):
    return raw * jax.nn.sigmoid(raw)


def swish_slope(raw):
    sig = jax.nn.sigmoid(raw)
    return sig * (1.0 + raw * (1.0 - sig))


def head_columns(s):
    return slice(s * HD, (s + 1) * HD)


def head_states():
    return pl.BlockSpec((TILE // HD, HD, 2 * HD), lambda i: (i, 0, 0))


def prepare_kernel(x, a_out, at_out):
    value = x[...].astype(f32)
    low = (value * lax.rsqrt(jnp.mean(value * value, axis=1, keepdims=True) + epsilon)).astype(bf16)
    a_out[...] = low
    at_out[...] = low.T


def prepare(x):
    rows, depth = x.shape
    part = 512
    return pl.pallas_call(
        prepare_kernel,
        grid=(rows // part,),
        in_specs=[row_tiles(part, depth)],
        out_specs=[row_tiles(part, depth), columns(depth, part)],
        out_shape=[struct((rows, depth), bf16), struct((depth, rows), bf16)],
        compiler_params=params(),
        cost_estimate=cost(8 * rows * depth, 6 * rows * depth),
        name="prepare",
    )(x)


def key_value_kernel(
    rates, across, order, a, wk0, wk1, wv0, wv1, cosine, sine, kraw_out, v_out, state_out, held
):
    step = pl.program_id(0)
    rows = a.shape[0]
    join(order[0], wk0, wk1, held.at[0])
    join(order[0], wv0, wv1, held.at[1])
    kraw = nn(a[...], held[0].reshape(-1, TILE))
    v_out[...] = nn(a[...], held[1].reshape(-1, TILE)).astype(bf16)
    kraw_out[...] = kraw.astype(bf16)
    for s in range(TILE // HD):
        head = step * (TILE // HD) + s
        cols = head_columns(s)
        tail = double(decay_out_of(rates[head]))
        state = jnp.zeros((HD, 2 * HD), f32)
        for c in range(rows // CH):
            span = slice(c * CH, (c + 1) * CH)
            key = swish(kraw[span, cols])
            faded = rotated(key, cosine[span, :], sine[span, :]) * tail
            state = across[head] * state + tn(v_out[span, cols], faded.astype(bf16))
        state_out[s] = state


def key_value(rates, across, a, keys, values, cosine, sine):
    rows, depth = a.shape
    return pl.pallas_call(
        key_value_kernel,
        grid=(depth // TILE,),
        in_specs=[smem(), smem(), smem(), fixed((rows, depth))]
        + keys.specs(64, lambda i: i)
        + values.specs(64, lambda i: i)
        + [fixed((rows, HD)), fixed((rows, HD))],
        out_specs=[columns(rows, TILE), columns(rows, TILE), head_states()],
        out_shape=[
            struct((rows, depth), bf16),
            struct((rows, depth), bf16),
            struct((H, HD, 2 * HD), f32),
        ],
        scratch_shapes=[pltpu.VMEM((2, 8, 2, 64, TILE), bf16)],
        compiler_params=params(),
        cost_estimate=cost(5 * rows * depth * depth, 10 * rows * depth),
        name="key_value",
    )(rates, across, keys.order, a, *keys.arrays(), *values.arrays(), cosine, sine)


def mix_kernel(
    rates,
    across,
    order,
    a,
    wq0,
    wq1,
    wg0,
    wg1,
    kraw,
    v,
    cosine,
    sine,
    state_in,
    qraw_out,
    u_out,
    o_out,
    gated_out,
    held,
):
    step = pl.program_id(0)
    rows = a.shape[0]
    join(order[0], wq0, wq1, held.at[0])
    join(order[0], wg0, wg1, held.at[1])
    qraw = nn(a[...], held[0].reshape(-1, TILE))
    qraw_out[...] = qraw.astype(bf16)
    u_out[...] = nn(a[...], held[1].reshape(-1, TILE)).astype(bf16)
    row = lax.broadcasted_iota(jnp.int32, (CH, CH), 0)
    col = lax.broadcasted_iota(jnp.int32, (CH, CH), 1)
    distance = (row - col).astype(f32)
    for s in range(TILE // HD):
        head = step * (TILE // HD) + s
        cols = head_columns(s)
        rate = rates[head]
        tail = double(decay_out_of(rate))
        lead = decay_in_of(rate)
        mask = jnp.where(distance >= 0, jnp.exp(-rate * jnp.maximum(distance, 0.0)), 0.0)
        state = state_in[s]
        for c in range(rows // CH):
            span = slice(c * CH, (c + 1) * CH)
            cos_c, sin_c = cosine[span, :], sine[span, :]
            query = rotated(swish(qraw[span, cols]), cos_c, sin_c).astype(bf16)
            key_float = rotated(swish(kraw[span, cols].astype(f32)), cos_c, sin_c)
            key = key_float.astype(bf16)
            value = v[span, cols]
            weights = (nt(query, key) * mask).astype(bf16)
            o = nn(weights, value) + lead * nt(query, state.astype(bf16))
            state = across[head] * state + tn(value, (key_float * tail).astype(bf16))
            o_out[span, cols] = o.astype(bf16)
            scale = lax.rsqrt(jnp.mean(o * o, axis=1, keepdims=True) + head_floor)
            gated_out[span, cols] = (o * scale * u_out[span, cols].astype(f32)).astype(bf16)


def mix(rates, across, a, queries, gates, kraw, v, cosine, sine, state_in):
    rows, depth = a.shape
    return pl.pallas_call(
        mix_kernel,
        grid=(depth // TILE,),
        in_specs=[smem(), smem(), smem(), fixed((rows, depth))]
        + queries.specs(64, lambda i: i)
        + gates.specs(64, lambda i: i)
        + [
            columns(rows, TILE),
            columns(rows, TILE),
            fixed((rows, HD)),
            fixed((rows, HD)),
            head_states(),
        ],
        out_specs=[columns(rows, TILE)] * 4,
        out_shape=[struct((rows, depth), bf16)] * 4,
        scratch_shapes=[pltpu.VMEM((2, 8, 2, 64, TILE), bf16)],
        compiler_params=params(),
        cost_estimate=cost(8 * rows * depth * depth, 18 * rows * depth),
        name="mix",
    )(
        rates,
        across,
        queries.order,
        a,
        *queries.arrays(),
        *gates.arrays(),
        kraw,
        v,
        cosine,
        sine,
        state_in,
    )


def residual_kernel(order, x, gated, lo0, lo1, hi0, hi1, h1_out, bn_out, bnt_out, held, h1):
    join(order[0], lo0, lo1, held, slice(0, 128))
    join(order[0], hi0, hi1, held, slice(128, 256))
    for b in range(4):
        cols = slice(b * TILE, (b + 1) * TILE)
        weight = held[:, :, b * 64 : (b + 1) * 64, :].reshape(-1, TILE)
        h1[:, cols] = x[:, cols].astype(f32) + nn(gated[...], weight)
    value = h1[...]
    h1_out[...] = value
    normed = value * lax.rsqrt(jnp.mean(value * value, axis=1, keepdims=True) + epsilon)
    low = normed.astype(bf16)
    bn_out[...] = low
    bnt_out[...] = low.T


def residual(x, gated, out_lo, out_hi):
    rows, depth = x.shape
    part = 512
    return pl.pallas_call(
        residual_kernel,
        grid=(rows // part,),
        in_specs=[smem(), row_tiles(part, depth), row_tiles(part, depth)]
        + out_lo.specs(128, lambda i: 2)
        + out_hi.specs(128, lambda i: 2),
        out_specs=[row_tiles(part, depth), row_tiles(part, depth), columns(depth, part)],
        out_shape=[
            struct((rows, depth), f32),
            struct((rows, depth), bf16),
            struct((depth, rows), bf16),
        ],
        scratch_shapes=[
            pltpu.VMEM((8, 2, 256, TILE), bf16),
            pltpu.VMEM((part, depth), f32),
        ],
        compiler_params=params(),
        cost_estimate=cost(2 * rows * depth * depth, 14 * rows * depth),
        name="residual",
    )(out_lo.order, x, gated, *out_lo.arrays(), *out_hi.arrays())


def feed_tile(bn, bnt, og, held, down, stage, total, dbn):
    w1 = held[:, :, 0:64, :].reshape(-1, TILE)
    w2 = held[:, :, 64:128, :].reshape(-1, TILE)
    for b in range(4):
        rows = slice(128 + 16 * b, 144 + 16 * b)
        down[:, b * TILE : (b + 1) * TILE] = held[:, :, rows, :].reshape(TILE, TILE)
    first = nn(bn[...], w1)
    second = nn(bn[...], w2)
    middle = (first * second).astype(bf16)
    dmid = nt(og[...], down[...])
    total[...] += nn(middle, down[...])
    d_first = (dmid * second).astype(bf16)
    d_second = (dmid * first).astype(bf16)
    dbn[...] += nt(d_first, w1) + nt(d_second, w2)
    stage[:, 0:64, :] = nn(bnt[...], d_first).astype(bf16).reshape(SHARDS, 64, TILE)
    stage[:, 64:128, :] = nn(bnt[...], d_second).astype(bf16).reshape(SHARDS, 64, TILE)
    g_down = tn(middle, og[...]).astype(bf16)
    for b in range(4):
        rows = slice(128 + 16 * b, 144 + 16 * b)
        stage[:, rows, :] = g_down[:, b * TILE : (b + 1) * TILE].reshape(SHARDS, 16, TILE)


def feed_start_kernel(bn, bnt, og, w, g_out, y_out, dbn_out, down, total, dbn):
    step = pl.program_id(0)

    @pl.when(step == 0)
    def _():
        total[...] = jnp.zeros_like(total)
        dbn[...] = jnp.zeros_like(dbn)

    feed_tile(bn, bnt, og, w, down, g_out, total, dbn)

    @pl.when(step == pl.num_programs(0) - 1)
    def _():
        y_out[...] = total[...].astype(bf16)
        dbn_out[...] = dbn[...].astype(bf16)


def feed_start(bn, bnt, og, weights, base, tiles):
    rows, depth = bn.shape
    return pl.pallas_call(
        feed_start_kernel,
        grid=(tiles,),
        in_specs=[
            fixed((rows, depth)),
            fixed((depth, rows)),
            fixed((rows, depth)),
            pl.BlockSpec((8, 2, 192, TILE), lambda i: (0, 0, base + i, 0)),
        ],
        out_specs=[
            pl.BlockSpec((SHARDS, 192, TILE), lambda i: (0, i, 0)),
            fixed((rows, depth)),
            fixed((rows, depth)),
        ],
        out_shape=[
            struct((SHARDS, tiles * 192, TILE), bf16),
            struct((rows, depth), bf16),
            struct((rows, depth), bf16),
        ],
        scratch_shapes=[
            pltpu.VMEM((TILE, depth), bf16),
            pltpu.VMEM((rows, depth), f32),
            pltpu.VMEM((rows, depth), f32),
        ],
        compiler_params=params(),
        cost_estimate=cost(
            18 * rows * depth * tiles * TILE, 12 * depth * tiles * TILE + 10 * rows * depth
        ),
        name="feed_start",
    )(bn, bnt, og, weights)


def feed_end_kernel(
    coords,
    h1,
    bn,
    bnt,
    og,
    y_part,
    dbn_part,
    w,
    own_out,
    other_out,
    y_out,
    dh1_out,
    dattn_out,
    down,
    stage,
    total,
    dbn,
):
    step = pl.program_id(0)

    @pl.when(step == 0)
    def _():
        total[...] = h1[...] + y_part[...].astype(f32)
        dbn[...] = dbn_part[...].astype(f32)

    feed_tile(bn, bnt, og, w, down, stage, total, dbn)
    emit(coords, stage, own_out, other_out, slice(0, 192), "xy")

    @pl.when(step == pl.num_programs(0) - 1)
    def _():
        y_out[...] = total[...].astype(bf16)
        hidden = h1[...]
        scale = lax.rsqrt(jnp.mean(hidden * hidden, axis=1, keepdims=True) + epsilon)
        normed = hidden * scale
        incoming = dbn[...]
        dh1 = og[...].astype(f32) + scale * (
            incoming - normed * jnp.mean(normed * incoming, axis=1, keepdims=True)
        )
        dh1_out[...] = dh1
        dattn_out[...] = dh1.astype(bf16)


def grad_block(height):
    return pl.BlockSpec((2, 2, 4, height, HALF), lambda i: (0, 0, 0, i, 0))


def feed_end(coords, h1, bn, bnt, og, y_part, dbn_part, weights, base, tiles):
    rows, depth = bn.shape
    grads = struct((2, 2, 4, tiles * 192, HALF), bf16)
    return pl.pallas_call(
        feed_end_kernel,
        grid=(tiles,),
        in_specs=[
            smem(),
            fixed((rows, depth)),
            fixed((rows, depth)),
            fixed((depth, rows)),
            fixed((rows, depth)),
            fixed((rows, depth)),
            fixed((rows, depth)),
            pl.BlockSpec((8, 2, 192, TILE), lambda i: (0, 0, base + i, 0)),
        ],
        out_specs=[
            grad_block(192),
            grad_block(192),
            fixed((rows, depth)),
            fixed((rows, depth)),
            fixed((rows, depth)),
        ],
        out_shape=[
            grads,
            grads,
            struct((rows, depth), bf16),
            struct((rows, depth), f32),
            struct((rows, depth), bf16),
        ],
        scratch_shapes=[
            pltpu.VMEM((TILE, depth), bf16),
            pltpu.VMEM((SHARDS, 192, TILE), bf16),
            pltpu.VMEM((rows, depth), f32),
            pltpu.VMEM((rows, depth), f32),
        ],
        compiler_params=params(),
        cost_estimate=cost(
            18 * rows * depth * tiles * TILE, 12 * depth * tiles * TILE + 20 * rows * depth
        ),
        name="feed_end",
    )(coords, h1, bn, bnt, og, y_part, dbn_part, weights)


def gate_back_kernel(
    rates,
    across,
    order,
    dattn,
    lo0,
    lo1,
    hi0,
    hi1,
    o_in,
    u_in,
    qraw,
    cosine,
    sine,
    du_out,
    do_out,
    back_out,
    held,
):
    step = pl.program_id(0)
    rows = dattn.shape[0]
    join(order[0], lo0, lo1, held, slice(0, 128))
    join(order[0], hi0, hi1, held, slice(128, 256))
    dgated = jnp.zeros((rows, TILE), f32)
    for b in range(4):
        weight = held[:, :, b * 64 : (b + 1) * 64, :].reshape(TILE, TILE)
        dgated = dgated + nt(dattn[:, b * TILE : (b + 1) * TILE], weight)
    dgated = dgated.astype(bf16).astype(f32)
    for s in range(TILE // HD):
        head = step * (TILE // HD) + s
        cols = head_columns(s)
        lead = double(decay_in_of(rates[head]))
        back = jnp.zeros((HD, 2 * HD), f32)
        for c in reversed(range(rows // CH)):
            span = slice(c * CH, (c + 1) * CH)
            o = o_in[span, cols].astype(f32)
            scale = lax.rsqrt(jnp.mean(o * o, axis=1, keepdims=True) + head_floor)
            normed = o * scale
            incoming = dgated[span, cols]
            du_out[span, cols] = (incoming * normed).astype(bf16)
            spread = incoming * u_in[span, cols].astype(f32)
            do = scale * (spread - normed * jnp.mean(normed * spread, axis=1, keepdims=True))
            low = do.astype(bf16)
            do_out[span, cols] = low
            query = rotated(swish(qraw[span, cols].astype(f32)), cosine[span, :], sine[span, :])
            back = across[head] * back + tn(low, (query * lead).astype(bf16))
        back_out[s] = back


def gate_back(rates, across, dattn, out_lo, out_hi, o_in, u_in, qraw, cosine, sine):
    rows, depth = dattn.shape
    return pl.pallas_call(
        gate_back_kernel,
        grid=(depth // TILE,),
        in_specs=[smem(), smem(), smem(), fixed((rows, depth))]
        + out_lo.specs(128, lambda i: 2, chips=2)
        + out_hi.specs(128, lambda i: 2, chips=2)
        + [
            columns(rows, TILE),
            columns(rows, TILE),
            columns(rows, TILE),
            fixed((rows, HD)),
            fixed((rows, HD)),
        ],
        out_specs=[columns(rows, TILE), columns(rows, TILE), head_states()],
        out_shape=[
            struct((rows, depth), bf16),
            struct((rows, depth), bf16),
            struct((H, HD, 2 * HD), f32),
        ],
        scratch_shapes=[pltpu.VMEM((2, 2, 256, TILE), bf16)],
        compiler_params=params(),
        cost_estimate=cost(3 * rows * depth * depth, 16 * rows * depth),
        name="gate_back",
    )(
        rates,
        across,
        out_lo.order,
        dattn,
        *out_lo.arrays(),
        *out_hi.arrays(),
        o_in,
        u_in,
        qraw,
        cosine,
        sine,
    )


def out_gate_grads_kernel(
    coords, a_t, du, gated, dattn, own_out, other_out, stage, stage_out
):
    step = pl.program_id(0)
    z0, y0, c0, x0 = coords[0], coords[1], coords[2], coords[3]
    stage[...] = nn(a_t[...], du[...]).astype(bf16).reshape(SHARDS, 64, TILE)
    rows = pl.ds(pl.multiple_of(256 + step * 64, 64), 64)
    emit(coords, stage, own_out, other_out, rows, "yx")
    g = tn(gated[...], dattn[...]).astype(bf16)
    z_rel = lax.rem(step + 4 - z0, 4)
    for b in range(4):
        stage_out[b] = g[:, b * TILE : (b + 1) * TILE].reshape(4, 64, TILE)
        rows = slice(b * 64, (b + 1) * 64)
        for x in range(2):
            x_rel = x + x0 - 2 * x * x0
            cols = slice(x * HALF, (x + 1) * HALF)
            for y_rel in range(2):
                y = y_rel + y0 - 2 * y_rel * y0
                own_out[y_rel, x_rel, z_rel, rows, :] = stage_out[b, 2 * y + c0, :, cols]
                other_out[y_rel, x_rel, z_rel, rows, :] = stage_out[
                    b, 2 * y + 1 - c0, :, cols
                ]


def out_gate_grads(coords, a_t, du, gated, dattn):
    depth, rows = a_t.shape
    grads = struct((2, 2, 4, 512, HALF), bf16)
    return pl.pallas_call(
        out_gate_grads_kernel,
        grid=(depth // TILE,),
        in_specs=[
            smem(),
            fixed((depth, rows)),
            columns(rows, TILE),
            columns(rows, TILE),
            fixed((rows, depth)),
        ],
        out_specs=[fixed(grads.shape), fixed(grads.shape)],
        out_shape=[grads, grads],
        scratch_shapes=[
            pltpu.VMEM((SHARDS, 64, TILE), bf16),
            pltpu.VMEM((4, 4, 64, TILE), bf16),
        ],
        compiler_params=params(),
        cost_estimate=cost(4 * rows * depth * depth, 12 * rows * depth),
        name="out_gate_grads",
    )(coords, a_t, du, gated, dattn)


def mix_back_kernel(
    rates,
    across,
    qraw,
    kraw,
    v,
    do_in,
    cosine,
    sine,
    state_in,
    back_in,
    dq_out,
    dk_out,
    dv_out,
    key_s,
):
    step = pl.program_id(0)
    rows = qraw.shape[0]
    count = rows // CH
    row = lax.broadcasted_iota(jnp.int32, (CH, CH), 0)
    col = lax.broadcasted_iota(jnp.int32, (CH, CH), 1)
    distance = (row - col).astype(f32)
    for s in range(TILE // HD):
        head = step * (TILE // HD) + s
        cols = head_columns(s)
        rate = rates[head]
        lead = double(decay_in_of(rate))
        tail = double(decay_out_of(rate))
        mask = jnp.where(distance >= 0, jnp.exp(-rate * jnp.maximum(distance, 0.0)), 0.0)
        mask_t = jnp.where(distance <= 0, jnp.exp(rate * jnp.minimum(distance, 0.0)), 0.0)
        state = state_in[s]
        states = []
        for c in range(count):
            span = slice(c * CH, (c + 1) * CH)
            key_float = rotated(
                swish(kraw[span, cols].astype(f32)), cosine[span, :], sine[span, :]
            )
            key_s[span, :] = key_float.astype(bf16)
            states.append(state.astype(bf16))
            if c < count - 1:
                state = across[head] * state + tn(v[span, cols], (key_float * tail).astype(bf16))
        back = back_in[s]
        for c in reversed(range(count)):
            span = slice(c * CH, (c + 1) * CH)
            cos_c, sin_c = cosine[span, :], sine[span, :]
            query_raw = qraw[span, cols].astype(f32)
            query_float = rotated(swish(query_raw), cos_c, sin_c)
            query = query_float.astype(bf16)
            key = key_s[span, :]
            value = v[span, cols]
            do = do_in[span, cols]
            back_low = back.astype(bf16)
            weights_t = (nt(key, query) * mask_t).astype(bf16)
            dscore = (nt(do, value) * mask).astype(bf16)
            dscore_t = (nt(value, do) * mask_t).astype(bf16)
            dqr = nn(dscore, key) + lead * nn(do, states[c])
            dkr = nn(dscore_t, query) + tail * nn(value, back_low)
            dv = nn(weights_t, do) + tail[:, :HD] * nt(key, back_low)
            back = across[head] * back + tn(do, (query_float * lead).astype(bf16))
            dq = dqr[:, :HD] * cos_c + dqr[:, HD:] * sin_c
            dk = dkr[:, :HD] * cos_c + dkr[:, HD:] * sin_c
            dq_out[span, cols] = (dq * swish_slope(query_raw)).astype(bf16)
            dk_out[span, cols] = (dk * swish_slope(kraw[span, cols].astype(f32))).astype(bf16)
            dv_out[span, cols] = dv.astype(bf16)


def mix_back(rates, across, qraw, kraw, v, do_in, cosine, sine, state_in, back_in):
    rows, width = qraw.shape
    return pl.pallas_call(
        mix_back_kernel,
        grid=(width // TILE,),
        in_specs=[smem(), smem()]
        + [columns(rows, TILE)] * 4
        + [fixed((rows, HD)), fixed((rows, HD)), head_states(), head_states()],
        out_specs=[columns(rows, TILE)] * 3,
        out_shape=[struct((rows, width), bf16)] * 3,
        scratch_shapes=[pltpu.VMEM((rows, 2 * HD), bf16)],
        compiler_params=params(),
        cost_estimate=cost(8 * rows * width * width, 16 * rows * width),
        name="mix_back",
    )(rates, across, qraw, kraw, v, do_in, cosine, sine, state_in, back_in)


def query_grads_kernel(coords, a_t, dq, dk, dv, own_out, other_out, stage):
    for n, incoming in enumerate((dq, dk, dv)):
        stage[:, n * 64 : (n + 1) * 64, :] = (
            nn(a_t[...], incoming[...]).astype(bf16).reshape(SHARDS, 64, TILE)
        )
    emit(coords, stage, own_out, other_out, slice(0, 192), "xy")


def query_grads(coords, a_t, dq, dk, dv):
    depth, rows = a_t.shape
    grads = struct((2, 2, 4, 3 * 256, HALF), bf16)
    return pl.pallas_call(
        query_grads_kernel,
        grid=(depth // TILE,),
        in_specs=[smem(), fixed((depth, rows))] + [columns(rows, TILE)] * 3,
        out_specs=[grad_block(192), grad_block(192)],
        out_shape=[grads, grads],
        scratch_shapes=[pltpu.VMEM((SHARDS, 192, TILE), bf16)],
        compiler_params=params(),
        cost_estimate=cost(6 * rows * depth * depth, 14 * rows * depth),
        name="query_grads",
    )(coords, a_t, dq, dk, dv)


def input_back_kernel(order, x, dh1, dq, dk, dv, du, *refs):
    weights, (out, total, held) = refs[:8], refs[8:]
    step = pl.program_id(0)

    @pl.when(step == 0)
    def _():
        total[...] = jnp.zeros_like(total)

    part = None
    for n, incoming in enumerate((dq, dk, dv, du)):
        join(order[0], weights[2 * n], weights[2 * n + 1], held.at[n])
        term = nt(incoming[...], held[n].reshape(-1, TILE))
        part = term if part is None else part + term
    total[...] += part

    @pl.when(step == pl.num_programs(0) - 1)
    def _():
        hidden = x[...].astype(f32)
        scale = lax.rsqrt(jnp.mean(hidden * hidden, axis=1, keepdims=True) + epsilon)
        normed = hidden * scale
        incoming = total[...]
        out[...] = (
            dh1[...]
            + scale * (incoming - normed * jnp.mean(normed * incoming, axis=1, keepdims=True))
        ).astype(bf16)


def input_back(x, dh1, grads, weights):
    rows, depth = x.shape
    specs, arrays = [], []
    for weight in weights:
        specs += weight.specs(64, lambda i: i)
        arrays += weight.arrays()
    return pl.pallas_call(
        input_back_kernel,
        grid=(depth // TILE,),
        in_specs=[smem(), fixed((rows, depth)), fixed((rows, depth))]
        + [columns(rows, TILE)] * 4
        + specs,
        out_specs=fixed((rows, depth)),
        out_shape=struct((rows, depth), bf16),
        scratch_shapes=[
            pltpu.VMEM((rows, depth), f32),
            pltpu.VMEM((4, 8, 2, 64, TILE), bf16),
        ],
        compiler_params=params(),
        cost_estimate=cost(8 * rows * depth * depth, 24 * rows * depth),
        name="input_back",
    )(weights[0].order, x, dh1, *grads, *arrays)


def square_blocks(w, shards):
    return w.reshape(shards, 64, 4, TILE).transpose(0, 2, 1, 3).reshape(shards, 256, TILE)


def square_back(blocks, shards):
    return blocks.reshape(shards, 4, 64, TILE).transpose(0, 2, 1, 3).reshape(shards * 64, 1024)


def feed_blocks(first, second, down, shards):
    hidden = first.shape[1]
    tiles = hidden // TILE

    def wide(w):
        return w.reshape(shards, 64, SHARDS, tiles, 16).transpose(0, 3, 1, 2, 4).reshape(
            shards, tiles, 64, TILE
        )

    low = down.reshape(shards, tiles, 16, 4, TILE).transpose(0, 1, 3, 2, 4)
    return jnp.concatenate(
        [wide(first), wide(second), low.reshape(shards, tiles, 64, TILE)], axis=2
    ).reshape(shards, tiles * 192, TILE)


def feed_back(blocks, shards):
    tiles = blocks.shape[1] // 192
    blocks = blocks.reshape(shards, tiles, 192, TILE)

    def wide(part):
        return part.reshape(shards, tiles, 64, SHARDS, 16).transpose(0, 2, 3, 1, 4).reshape(
            shards * 64, tiles * TILE
        )

    low = blocks[:, :, 128:].reshape(shards, tiles, 4, 16, TILE).transpose(0, 1, 3, 2, 4)
    return wide(blocks[:, :, :64]), wide(blocks[:, :, 64:128]), low.reshape(-1, 1024)


class Grid:
    def __init__(self):
        index = lax.axis_index("wt")
        self.z, self.y, self.core = index // 4, (index // 2) % 2, index % 2
        self.x = lax.axis_index("seq")

    def coords(self):
        return jnp.stack([self.z, self.y, self.core, self.x]).astype(jnp.int32)

    def over(self, axis, value):
        if axis == "x":
            return lax.ppermute(value, "seq", [(0, 1), (1, 0)])
        step = {"y": 2, "core": 1}[axis]
        return lax.ppermute(value, "wt", [(i, i ^ step) for i in range(SHARDS)])

    def shift_z(self, value, k):
        return lax.ppermute(value, "wt", [(i, (i + 4 * k) % SHARDS) for i in range(SHARDS)])

    def in_order(self, flag, own, received, axis):
        near = jnp.concatenate([own, received], axis=axis)
        far = jnp.concatenate([received, own], axis=axis)
        return jnp.where(flag == 0, near, far)

    def gather(self, y_first, x_first):
        split = y_first.shape[0]
        both = jnp.concatenate([y_first, x_first], axis=0)
        own = lax.dynamic_slice_in_dim(both, self.x * HALF, HALF, axis=1)
        parts = [own] + [self.shift_z(own, k) for k in (1, 2, 3)]
        ring = jnp.stack(parts[::-1] + parts[::-1])
        ring = lax.dynamic_slice_in_dim(ring, (3 - self.z) % 4, 4, axis=0)
        one, two = ring[:, None, :split], ring[:, None, split:]
        one_y, two_x = self.over("y", one), self.over("x", two)
        one = self.in_order(self.y, one, one_y, 1)
        two = self.in_order(self.x, two, two_x, 3)
        one_x, two_y = self.over("x", one), self.over("y", two)
        one = self.in_order(self.x, one, one_x, 3).reshape(8, 1, -1, TILE)
        two = self.in_order(self.y, two, two_y, 1).reshape(8, 1, -1, TILE)
        order = self.core.astype(jnp.int32)[None]
        return (
            Gathered(one, self.over("core", one), order),
            Gathered(two, self.over("core", two), order),
        )

    def scatter(self, own, other, first, second):
        got = self.over("core", other)
        far = (own[1].astype(f32) + got[1].astype(f32)).astype(bf16)
        got_first = self.over(first, far)
        near = own[0].astype(f32) + got[0].astype(f32) + got_first.astype(f32)
        got_second = self.over(second, near[1].astype(bf16))
        total = near[0] + got_second.astype(f32)
        result = total[0]
        for k in (1, 2, 3):
            result = result + self.shift_z(total[k].astype(bf16), k).astype(f32)
        return result.astype(bf16)

    def both_halves(self, half):
        return self.in_order(self.x, half, self.over("x", half), 1)


class Plain:
    def coords(self):
        return jnp.zeros((4,), jnp.int32)


def natural(own, other, order):
    both = jnp.stack([own, other])
    x_axis, y_axis = (1, 2) if order == "xy" else (2, 1)
    both = both.transpose(3, y_axis, 0, 4, x_axis, 5)
    return both.reshape(SHARDS, own.shape[3], TILE)


def body(
    activations,
    w_query,
    w_key,
    w_value,
    w_gate,
    w_out,
    w_first,
    w_second,
    w_down,
    decay_rate,
    seq_lengths,
    out_grad,
):
    seq_count = lax.axis_size("seq")
    seq_index = lax.axis_index("seq")
    direct = seq_count == 2 and lax.axis_size("wt") == SHARDS
    x = activations[0]
    og = out_grad[0]
    rows = x.shape[0]
    assert MIN_LEN % rows == 0

    if direct:
        grid = Grid()
        key_block, value_block, query_block, gate_block, out_block = (
            square_blocks(w, 1)[0] for w in (w_key, w_value, w_query, w_gate, w_out)
        )
        feed_block = feed_blocks(w_first, w_second, w_down, 1)[0]
        feed_weights = lax.all_gather(feed_block, "wt", axis=0, tiled=True)
        feed_weights = feed_weights.reshape(8, 2, -1, TILE)
        keys, values = grid.gather(key_block, value_block)
        queries, gates = grid.gather(
            jnp.concatenate([query_block, out_block[:128]]),
            jnp.concatenate([gate_block, out_block[128:]]),
        )
    else:
        grid = Plain()
        full_key, full_value, full_query, full_gate, full_out = (
            square_blocks(lax.all_gather(w, "wt", axis=0, tiled=True), SHARDS)
            for w in (w_key, w_value, w_query, w_gate, w_out)
        )
        feed_weights = feed_blocks(
            *(lax.all_gather(w, "wt", axis=0, tiled=True) for w in (w_first, w_second, w_down)),
            SHARDS,
        ).reshape(8, 2, -1, TILE)

        def held(block):
            block = block.reshape(8, 2, -1, TILE)
            return Gathered(block, block, jnp.zeros((1,), jnp.int32))

        keys, values = held(full_key), held(full_value)
        queries = held(jnp.concatenate([full_query, full_out[:, :128]], axis=1))
        gates = held(jnp.concatenate([full_gate, full_out[:, 128:]], axis=1))
    coords = grid.coords()

    lengths = seq_lengths[0]
    starts = jnp.cumsum(lengths) - lengths
    begin = seq_index * rows
    begun = (starts <= begin) & (lengths > 0)
    first_token = jnp.max(jnp.where(begun, starts, 0))
    keep = jnp.where(begin == first_token, 0.0, 1.0).astype(f32)
    position = (begin - first_token + jnp.arange(rows, dtype=jnp.int32)).astype(f32)
    frequency = 10000.0 ** (-jnp.arange(HD, dtype=f32) / HD)
    angles = position[:, None] * frequency[None, :]
    cosine, sine = jnp.cos(angles), jnp.sin(angles)
    across = jnp.exp(-decay_rate * CH)
    whole = jnp.exp(-decay_rate * rows)[:, None, None]

    a, a_t = prepare(x)
    kraw, v, own_state = key_value(decay_rate, across, a, keys, values, cosine, sine)
    ahead = [(i, i + 1) for i in range(seq_count - 1)]
    state_in = jnp.zeros_like(own_state)
    for _ in range(seq_count - 1):
        sent = (whole * state_in + own_state).astype(bf16)
        state_in = keep * lax.ppermute(sent, "seq", ahead).astype(f32)

    qraw, u, o, gated = mix(
        decay_rate, across, a, queries, gates, kraw, v, cosine, sine, state_in
    )
    h1, bn, bn_t = residual(x, gated, queries, gates)
    tiles = w_first.shape[1] // TILE
    early = (tiles + 1) // 2
    g_early, y_part, dbn_part = feed_start(bn, bn_t, og, feed_weights, 0, early)
    if direct:
        early_share = lax.psum_scatter(
            g_early.reshape(SHARDS, -1, TILE), "wt", scatter_dimension=0, tiled=True
        )[0]
    own_late, other_late, layer_out, dh1, dattn = feed_end(
        coords, h1, bn, bn_t, og, y_part, dbn_part, feed_weights, early, tiles - early
    )
    du, do, own_back = gate_back(
        decay_rate, across, dattn, queries, gates, o, u, qraw, cosine, sine
    )
    behind = [(i + 1, i) for i in range(seq_count - 1)]
    back_in = jnp.zeros_like(own_back)
    for _ in range(seq_count - 1):
        sent = (keep * (whole * back_in + own_back)).astype(bf16)
        back_in = lax.ppermute(sent, "seq", behind).astype(f32)
    own_og, other_og = out_gate_grads(coords, a_t, du, gated, dattn)
    dq, dk, dv = mix_back(
        decay_rate, across, qraw, kraw, v, do, cosine, sine, state_in, back_in
    )
    own_qkv, other_qkv = query_grads(coords, a_t, dq, dk, dv)
    input_grad = input_back(x, dh1, (dq, dk, dv, du), (queries, keys, values, gates))

    if direct:
        early_total = early_share.astype(f32) + grid.over("x", early_share).astype(f32)
        late_total = grid.both_halves(grid.scatter(own_late, other_late, "x", "y")).astype(f32)
        og_total = grid.both_halves(grid.scatter(own_og, other_og, "y", "x")).astype(f32)
        qkv_total = grid.both_halves(grid.scatter(own_qkv, other_qkv, "x", "y")).astype(f32)
        feed_total = jnp.concatenate([early_total, late_total])[None]
        og_total, qkv_total = og_total[None], qkv_total[None]
        shards = 1
    else:
        feed_total = jnp.concatenate([g_early, natural(own_late, other_late, "xy")], axis=1)
        og_total = natural(own_og, other_og, "yx")
        qkv_total = natural(own_qkv, other_qkv, "xy")
        shards = SHARDS
    qkv_total = qkv_total.reshape(shards, 4, 3, 64, TILE)
    squares = [qkv_total[:, :, n] for n in range(3)] + [og_total[:, 256:], og_total[:, :256]]
    totals = [square_back(g, shards) for g in squares] + list(feed_back(feed_total, shards))
    if not direct:
        totals = [
            lax.psum(lax.psum_scatter(g, "wt", scatter_dimension=0, tiled=True), "seq").astype(f32)
            for g in totals
        ]
    return (layer_out[None], input_grad[None], *totals)


def solution(mesh):
    weight = P("wt", None)
    tokens = P("wt", "seq", None)
    return jax.shard_map(
        body,
        mesh=mesh,
        in_specs=(tokens,) + (weight,) * 8 + (P(), weight, tokens),
        out_specs=(tokens, tokens) + (weight,) * 8,
        check_vma=False,
    )
```

```python
import functools

import jax
import jax.numpy as jnp
from jax import lax
from jax.experimental import pallas as pl
from jax.experimental.pallas import tpu as pltpu
from jax.sharding import PartitionSpec as P

H = 8
HD = 128
CH = 256
TILE = 256
HALF = 128
SHARDS = 16
MIN_LEN = 1024
VMEM_LIMIT = 60 << 20

epsilon = 1e-06
head_floor = 1.0
bf16 = jnp.bfloat16
f32 = jnp.float32


def nn(left, right):
    return jnp.dot(left, right, preferred_element_type=f32)


def nt(left, right):
    return lax.dot_general(left, right, (((1,), (1,)), ((), ())), preferred_element_type=f32)


def tn(left, right):
    return lax.dot_general(left, right, (((0,), (0,)), ((), ())), preferred_element_type=f32)


def struct(shape, dtype):
    return jax.ShapeDtypeStruct(shape, dtype)


def fixed(shape):
    zeros = (0,) * len(shape)
    return pl.BlockSpec(shape, lambda i: zeros, pipeline_mode=pl.Buffered(1))


def columns(rows, width):
    return pl.BlockSpec((rows, width), lambda i: (0, i))


def row_tiles(height, cols):
    return pl.BlockSpec((height, cols), lambda i: (i, 0))


def smem():
    return pl.BlockSpec(memory_space=pltpu.SMEM)


def params():
    return pltpu.CompilerParams(vmem_limit_bytes=VMEM_LIMIT)


def cost(flops, moved):
    return pl.CostEstimate(flops=flops // 10000, bytes_accessed=moved // 10000, transcendentals=0)


class Gathered:
    def __init__(self, kind, arrays):
        self.kind, self.arrays = kind, arrays

    def specs(self, height, index):
        spec = pl.BlockSpec((2, 4, height, HALF), lambda i: (0, 0, index(i), 0))
        return [spec] * 4


def join(coords, kind, refs, held, rows=slice(None)):
    z0, y0, c0, x0 = coords[0], coords[1], coords[2], coords[3]
    for c_rel in range(2):
        core = c_rel + c0 - 2 * c_rel * c0
        pair = refs[2 * c_rel : 2 * c_rel + 2]
        for y_rel in range(2):
            y = y_rel + y0 - 2 * y_rel * y0
            for z_rel in range(4):
                z = lax.rem(z0 + 4 - z_rel, 4)
                if kind == "y":
                    here, there = pair[0][y_rel, z_rel], pair[1][y_rel, z_rel]
                else:
                    here, there = pair[y_rel][0, z_rel], pair[y_rel][1, z_rel]
                near = jnp.concatenate([here, there], axis=1)
                far = jnp.concatenate([there, here], axis=1)
                held[z, y, core, rows, :] = jnp.where(x0 == 0, near, far)


def emit(coords, stage, own, other, rows):
    z0, y0, c0, x0 = coords[0], coords[1], coords[2], coords[3]
    for x in range(2):
        x_rel = x + x0 - 2 * x * x0
        cols = slice(x * HALF, (x + 1) * HALF)
        for y_rel in range(2):
            y = y_rel + y0 - 2 * y_rel * y0
            for z_rel in range(4):
                z = lax.rem(z0 + z_rel, 4)
                shard = z * 4 + y * 2
                own[x_rel, y_rel, z_rel, rows, :] = stage[shard + c0, :, cols]
                other[x_rel, y_rel, z_rel, rows, :] = stage[shard + 1 - c0, :, cols]


def decay_in_of(rate):
    row = lax.broadcasted_iota(jnp.int32, (CH, HD), 0).astype(f32)
    return jnp.exp(-rate * (row + 1.0))


def decay_out_of(rate):
    row = lax.broadcasted_iota(jnp.int32, (CH, HD), 0).astype(f32)
    return jnp.exp(-rate * (CH - 1.0 - row))


def double(table):
    return jnp.concatenate([table, table], axis=1)


def rotated(heads, cosine, sine):
    return jnp.concatenate([heads * cosine, heads * sine], axis=1)


def swish(raw):
    return raw * jax.nn.sigmoid(raw)


def swish_slope(raw):
    sig = jax.nn.sigmoid(raw)
    return sig * (1.0 + raw * (1.0 - sig))


def head_columns(s):
    return slice(s * HD, (s + 1) * HD)


def head_states():
    return pl.BlockSpec((TILE // HD, HD, 2 * HD), lambda i: (i, 0, 0))


def prepare_kernel(x, a_out, at_out):
    value = x[...].astype(f32)
    low = (value * lax.rsqrt(jnp.mean(value * value, axis=1, keepdims=True) + epsilon)).astype(bf16)
    a_out[...] = low
    at_out[...] = low.T


def prepare(x):
    rows, depth = x.shape
    part = 512
    return pl.pallas_call(
        prepare_kernel,
        grid=(rows // part,),
        in_specs=[row_tiles(part, depth)],
        out_specs=[row_tiles(part, depth), columns(depth, part)],
        out_shape=[struct((rows, depth), bf16), struct((depth, rows), bf16)],
        compiler_params=params(),
        cost_estimate=cost(8 * rows * depth, 6 * rows * depth),
        name="prepare",
    )(x)


def key_value_kernel(
    rates, across, coords, a, cosine, sine, *refs
):
    kraw_out, v_out, state_out, held = refs[8:]
    step = pl.program_id(0)
    rows = a.shape[0]
    join(coords, "y", refs[:4], held.at[0])
    join(coords, "x", refs[4:8], held.at[1])
    kraw = nn(a[...], held[0].reshape(-1, TILE))
    v_out[...] = nn(a[...], held[1].reshape(-1, TILE)).astype(bf16)
    kraw_out[...] = kraw.astype(bf16)
    for s in range(TILE // HD):
        head = step * (TILE // HD) + s
        cols = head_columns(s)
        tail = double(decay_out_of(rates[head]))
        state = jnp.zeros((HD, 2 * HD), f32)
        for c in range(rows // CH):
            span = slice(c * CH, (c + 1) * CH)
            key = swish(kraw[span, cols])
            faded = rotated(key, cosine[span, :], sine[span, :]) * tail
            state = across[head] * state + tn(v_out[span, cols], faded.astype(bf16))
        state_out[s] = state.astype(state_out.dtype)


def key_value(rates, across, coords, a, keys, values, cosine, sine, state_type):
    rows, depth = a.shape
    return pl.pallas_call(
        key_value_kernel,
        grid=(depth // TILE,),
        in_specs=[smem(), smem(), smem(), fixed((rows, depth))]
        + [fixed((rows, HD)), fixed((rows, HD))]
        + keys.specs(64, lambda i: i)
        + values.specs(64, lambda i: i),
        out_specs=[columns(rows, TILE), columns(rows, TILE), head_states()],
        out_shape=[
            struct((rows, depth), bf16),
            struct((rows, depth), bf16),
            struct((H, HD, 2 * HD), state_type),
        ],
        scratch_shapes=[pltpu.VMEM((2, 4, 2, 2, 64, TILE), bf16)],
        compiler_params=params(),
        cost_estimate=cost(5 * rows * depth * depth, 10 * rows * depth),
        name="key_value",
    )(rates, across, coords, a, cosine, sine, *keys.arrays, *values.arrays)


def mix_kernel(rates, across, keep, coords, a, kraw, v, cosine, sine, state_in, *refs):
    qraw_out, u_out, o_out, gated_out, held = refs[8:]
    step = pl.program_id(0)
    rows = a.shape[0]
    join(coords, "y", refs[:4], held.at[0])
    join(coords, "x", refs[4:8], held.at[1])
    qraw = nn(a[...], held[0].reshape(-1, TILE))
    qraw_out[...] = qraw.astype(bf16)
    u_out[...] = nn(a[...], held[1].reshape(-1, TILE)).astype(bf16)
    row = lax.broadcasted_iota(jnp.int32, (CH, CH), 0)
    col = lax.broadcasted_iota(jnp.int32, (CH, CH), 1)
    distance = (row - col).astype(f32)
    for s in range(TILE // HD):
        head = step * (TILE // HD) + s
        cols = head_columns(s)
        rate = rates[head]
        tail = double(decay_out_of(rate))
        lead = decay_in_of(rate)
        mask = jnp.where(distance >= 0, jnp.exp(-rate * jnp.maximum(distance, 0.0)), 0.0)
        state = keep[0] * state_in[s].astype(f32)
        for c in range(rows // CH):
            span = slice(c * CH, (c + 1) * CH)
            cos_c, sin_c = cosine[span, :], sine[span, :]
            query = rotated(swish(qraw[span, cols]), cos_c, sin_c).astype(bf16)
            key_float = rotated(swish(kraw[span, cols].astype(f32)), cos_c, sin_c)
            key = key_float.astype(bf16)
            value = v[span, cols]
            weights = (nt(query, key) * mask).astype(bf16)
            o = nn(weights, value) + lead * nt(query, state.astype(bf16))
            state = across[head] * state + tn(value, (key_float * tail).astype(bf16))
            o_out[span, cols] = o.astype(bf16)
            scale = lax.rsqrt(jnp.mean(o * o, axis=1, keepdims=True) + head_floor)
            gated_out[span, cols] = (o * scale * u_out[span, cols].astype(f32)).astype(bf16)


def mix(rates, across, keep, coords, a, queries, gates, kraw, v, cosine, sine, state_in):
    rows, depth = a.shape
    return pl.pallas_call(
        mix_kernel,
        grid=(depth // TILE,),
        in_specs=[smem(), smem(), smem(), smem(), fixed((rows, depth))]
        + [
            columns(rows, TILE),
            columns(rows, TILE),
            fixed((rows, HD)),
            fixed((rows, HD)),
            head_states(),
        ]
        + queries.specs(64, lambda i: i)
        + gates.specs(64, lambda i: i),
        out_specs=[columns(rows, TILE)] * 4,
        out_shape=[struct((rows, depth), bf16)] * 4,
        scratch_shapes=[pltpu.VMEM((2, 4, 2, 2, 64, TILE), bf16)],
        compiler_params=params(),
        cost_estimate=cost(8 * rows * depth * depth, 18 * rows * depth),
        name="mix",
    )(
        rates,
        across,
        keep,
        coords,
        a,
        kraw,
        v,
        cosine,
        sine,
        state_in,
        *queries.arrays,
        *gates.arrays,
    )


def residual_kernel(coords, x, gated, *refs):
    h1_out, bn_out, bnt_out, held, h1 = refs[8:]

    @pl.when(pl.program_id(0) == 0)
    def _():
        join(coords, "y", refs[:4], held, slice(0, 128))
        join(coords, "x", refs[4:8], held, slice(128, 256))

    for b in range(4):
        cols = slice(b * TILE, (b + 1) * TILE)
        weight = held[:, :, :, b * 64 : (b + 1) * 64, :].reshape(-1, TILE)
        h1[:, cols] = x[:, cols].astype(f32) + nn(gated[...], weight)
    value = h1[...]
    h1_out[...] = value
    normed = value * lax.rsqrt(jnp.mean(value * value, axis=1, keepdims=True) + epsilon)
    low = normed.astype(bf16)
    bn_out[...] = low
    bnt_out[...] = low.T


def residual(coords, x, gated, out_lo, out_hi):
    rows, depth = x.shape
    part = 512
    return pl.pallas_call(
        residual_kernel,
        grid=(rows // part,),
        in_specs=[smem(), row_tiles(part, depth), row_tiles(part, depth)]
        + out_lo.specs(128, lambda i: 2)
        + out_hi.specs(128, lambda i: 2),
        out_specs=[row_tiles(part, depth), row_tiles(part, depth), columns(depth, part)],
        out_shape=[
            struct((rows, depth), f32),
            struct((rows, depth), bf16),
            struct((depth, rows), bf16),
        ],
        scratch_shapes=[
            pltpu.VMEM((4, 2, 2, 256, TILE), bf16),
            pltpu.VMEM((part, depth), f32),
        ],
        compiler_params=params(),
        cost_estimate=cost(2 * rows * depth * depth, 14 * rows * depth),
        name="residual",
    )(coords, x, gated, *out_lo.arrays, *out_hi.arrays)


def feed_tile(bn, bnt, og, held, down, stage, total, dbn):
    w1 = held[:, :, :, 0:64, :].reshape(-1, TILE)
    w2 = held[:, :, :, 64:128, :].reshape(-1, TILE)
    for b in range(4):
        rows = slice(128 + 16 * b, 144 + 16 * b)
        down[:, b * TILE : (b + 1) * TILE] = held[:, :, :, rows, :].reshape(TILE, TILE)
    first = nn(bn[...], w1)
    second = nn(bn[...], w2)
    middle = (first * second).astype(bf16)
    dmid = nt(og[...], down[...])
    total[...] += nn(middle, down[...])
    d_first = (dmid * second).astype(bf16)
    d_second = (dmid * first).astype(bf16)
    dbn[...] += nt(d_first, w1) + nt(d_second, w2)
    stage[:, 0:64, :] = nn(bnt[...], d_first).astype(bf16).reshape(SHARDS, 64, TILE)
    stage[:, 64:128, :] = nn(bnt[...], d_second).astype(bf16).reshape(SHARDS, 64, TILE)
    g_down = tn(middle, og[...]).astype(bf16)
    for b in range(4):
        rows = slice(128 + 16 * b, 144 + 16 * b)
        stage[:, rows, :] = g_down[:, b * TILE : (b + 1) * TILE].reshape(SHARDS, 16, TILE)


def feed_start_kernel(bn, bnt, og, w, g_out, y_out, dbn_out, down, total, dbn):
    step = pl.program_id(0)

    @pl.when(step == 0)
    def _():
        total[...] = jnp.zeros_like(total)
        dbn[...] = jnp.zeros_like(dbn)

    feed_tile(bn, bnt, og, w, down, g_out, total, dbn)

    @pl.when(step == pl.num_programs(0) - 1)
    def _():
        y_out[...] = total[...].astype(bf16)
        dbn_out[...] = dbn[...].astype(bf16)


def feed_tiles(base):
    return pl.BlockSpec((4, 2, 2, 192, TILE), lambda i: (0, 0, 0, base + i, 0))


def feed_start(bn, bnt, og, weights, tiles):
    rows, depth = bn.shape
    return pl.pallas_call(
        feed_start_kernel,
        grid=(tiles,),
        in_specs=[
            fixed((rows, depth)),
            fixed((depth, rows)),
            fixed((rows, depth)),
            feed_tiles(0),
        ],
        out_specs=[
            pl.BlockSpec((SHARDS, 192, TILE), lambda i: (0, i, 0)),
            fixed((rows, depth)),
            fixed((rows, depth)),
        ],
        out_shape=[
            struct((SHARDS, tiles * 192, TILE), bf16),
            struct((rows, depth), bf16),
            struct((rows, depth), bf16),
        ],
        scratch_shapes=[
            pltpu.VMEM((TILE, depth), bf16),
            pltpu.VMEM((rows, depth), f32),
            pltpu.VMEM((rows, depth), f32),
        ],
        compiler_params=params(),
        cost_estimate=cost(
            18 * rows * depth * tiles * TILE, 12 * depth * tiles * TILE + 10 * rows * depth
        ),
        name="feed_start",
    )(bn, bnt, og, weights)


def feed_end_kernel(coords, h1, bn, bnt, og, y_part, dbn_part, w, *refs):
    own_out, other_out, y_out, dh1_out, dattn_out, down, stage, total, dbn = refs
    step = pl.program_id(0)

    @pl.when(step == 0)
    def _():
        total[...] = h1[...] + y_part[...].astype(f32)
        dbn[...] = dbn_part[...].astype(f32)

    feed_tile(bn, bnt, og, w, down, stage, total, dbn)
    emit(coords, stage, own_out, other_out, slice(0, 192))

    @pl.when(step == pl.num_programs(0) - 1)
    def _():
        y_out[...] = total[...].astype(bf16)
        hidden = h1[...]
        scale = lax.rsqrt(jnp.mean(hidden * hidden, axis=1, keepdims=True) + epsilon)
        normed = hidden * scale
        incoming = dbn[...]
        dh1 = og[...].astype(f32) + scale * (
            incoming - normed * jnp.mean(normed * incoming, axis=1, keepdims=True)
        )
        dh1_out[...] = dh1
        dattn_out[...] = dh1.astype(bf16)


def grad_block(height):
    return pl.BlockSpec((2, 2, 4, height, HALF), lambda i: (0, 0, 0, i, 0))


def feed_end(coords, h1, bn, bnt, og, y_part, dbn_part, weights, base):
    rows, depth = bn.shape
    tiles = weights.shape[3] // 192 - base
    grads = struct((2, 2, 4, tiles * 192, HALF), bf16)
    return pl.pallas_call(
        feed_end_kernel,
        grid=(tiles,),
        in_specs=[
            smem(),
            fixed((rows, depth)),
            fixed((rows, depth)),
            fixed((depth, rows)),
            fixed((rows, depth)),
            fixed((rows, depth)),
            fixed((rows, depth)),
            feed_tiles(base),
        ],
        out_specs=[
            grad_block(192),
            grad_block(192),
            fixed((rows, depth)),
            fixed((rows, depth)),
            fixed((rows, depth)),
        ],
        out_shape=[
            grads,
            grads,
            struct((rows, depth), bf16),
            struct((rows, depth), f32),
            struct((rows, depth), bf16),
        ],
        scratch_shapes=[
            pltpu.VMEM((TILE, depth), bf16),
            pltpu.VMEM((SHARDS, 192, TILE), bf16),
            pltpu.VMEM((rows, depth), f32),
            pltpu.VMEM((rows, depth), f32),
        ],
        compiler_params=params(),
        cost_estimate=cost(
            18 * rows * depth * tiles * TILE, 12 * depth * tiles * TILE + 20 * rows * depth
        ),
        name="feed_end",
    )(coords, h1, bn, bnt, og, y_part, dbn_part, weights)


def gate_back_kernel(rates, across, keep, coords, dattn, o_in, u_in, qraw, cosine, sine, *refs):
    du_out, do_out, back_out, held = refs[8:]
    step = pl.program_id(0)
    rows = dattn.shape[0]

    @pl.when(step == 0)
    def _():
        join(coords, "y", refs[:4], held, slice(0, 128))
        join(coords, "x", refs[4:8], held, slice(128, 256))

    dgated = jnp.zeros((rows, TILE), f32)
    for b in range(4):
        weight = held[step, :, :, b * 64 : (b + 1) * 64, :].reshape(TILE, TILE)
        dgated = dgated + nt(dattn[:, b * TILE : (b + 1) * TILE], weight)
    dgated = dgated.astype(bf16).astype(f32)
    for s in range(TILE // HD):
        head = step * (TILE // HD) + s
        cols = head_columns(s)
        lead = double(decay_in_of(rates[head]))
        back = jnp.zeros((HD, 2 * HD), f32)
        for c in reversed(range(rows // CH)):
            span = slice(c * CH, (c + 1) * CH)
            o = o_in[span, cols].astype(f32)
            scale = lax.rsqrt(jnp.mean(o * o, axis=1, keepdims=True) + head_floor)
            normed = o * scale
            incoming = dgated[span, cols]
            du_out[span, cols] = (incoming * normed).astype(bf16)
            spread = incoming * u_in[span, cols].astype(f32)
            do = scale * (spread - normed * jnp.mean(normed * spread, axis=1, keepdims=True))
            low = do.astype(bf16)
            do_out[span, cols] = low
            query = rotated(swish(qraw[span, cols].astype(f32)), cosine[span, :], sine[span, :])
            back = across[head] * back + tn(low, (query * lead).astype(bf16))
        back_out[s] = (keep[0] * back).astype(back_out.dtype)


def gate_back(
    rates, across, keep, coords, dattn, out_lo, out_hi, o_in, u_in, qraw, cosine, sine, back_type
):
    rows, depth = dattn.shape
    return pl.pallas_call(
        gate_back_kernel,
        grid=(depth // TILE,),
        in_specs=[smem(), smem(), smem(), smem(), fixed((rows, depth))]
        + [
            columns(rows, TILE),
            columns(rows, TILE),
            columns(rows, TILE),
            fixed((rows, HD)),
            fixed((rows, HD)),
        ]
        + out_lo.specs(128, lambda i: 2)
        + out_hi.specs(128, lambda i: 2),
        out_specs=[columns(rows, TILE), columns(rows, TILE), head_states()],
        out_shape=[
            struct((rows, depth), bf16),
            struct((rows, depth), bf16),
            struct((H, HD, 2 * HD), back_type),
        ],
        scratch_shapes=[pltpu.VMEM((4, 2, 2, 256, TILE), bf16)],
        compiler_params=params(),
        cost_estimate=cost(3 * rows * depth * depth, 16 * rows * depth),
        name="gate_back",
    )(
        rates,
        across,
        keep,
        coords,
        dattn,
        o_in,
        u_in,
        qraw,
        cosine,
        sine,
        *out_lo.arrays,
        *out_hi.arrays,
    )


def out_gate_grads_kernel(
    coords, a_t, du, gated, dattn, own_out, other_out, stage, stage_out
):
    step = pl.program_id(0)
    z0, y0, c0, x0 = coords[0], coords[1], coords[2], coords[3]
    stage[...] = nn(a_t[...], du[...]).astype(bf16).reshape(SHARDS, 64, TILE)
    rows = pl.ds(pl.multiple_of(256 + step * 64, 64), 64)
    emit(coords, stage, own_out, other_out, rows)
    g = tn(gated[...], dattn[...]).astype(bf16)
    z_rel = lax.rem(step + 4 - z0, 4)
    for b in range(4):
        stage_out[b] = g[:, b * TILE : (b + 1) * TILE].reshape(4, 64, TILE)
        rows = slice(b * 64, (b + 1) * 64)
        for x in range(2):
            x_rel = x + x0 - 2 * x * x0
            cols = slice(x * HALF, (x + 1) * HALF)
            for y_rel in range(2):
                y = y_rel + y0 - 2 * y_rel * y0
                own_out[x_rel, y_rel, z_rel, rows, :] = stage_out[b, 2 * y + c0, :, cols]
                other_out[x_rel, y_rel, z_rel, rows, :] = stage_out[
                    b, 2 * y + 1 - c0, :, cols
                ]


def out_gate_grads(coords, a_t, du, gated, dattn):
    depth, rows = a_t.shape
    grads = struct((2, 2, 4, 512, HALF), bf16)
    return pl.pallas_call(
        out_gate_grads_kernel,
        grid=(depth // TILE,),
        in_specs=[
            smem(),
            fixed((depth, rows)),
            columns(rows, TILE),
            columns(rows, TILE),
            fixed((rows, depth)),
        ],
        out_specs=[fixed(grads.shape), fixed(grads.shape)],
        out_shape=[grads, grads],
        scratch_shapes=[
            pltpu.VMEM((SHARDS, 64, TILE), bf16),
            pltpu.VMEM((4, 4, 64, TILE), bf16),
        ],
        compiler_params=params(),
        cost_estimate=cost(4 * rows * depth * depth, 12 * rows * depth),
        name="out_gate_grads",
    )(coords, a_t, du, gated, dattn)


def mix_back_kernel(
    base,
    rates,
    across,
    keep,
    qraw,
    kraw,
    v,
    do_in,
    cosine,
    sine,
    state_in,
    back_in,
    dq_out,
    dk_out,
    dv_out,
    key_s,
):
    step = base + pl.program_id(0)
    rows = qraw.shape[0]
    count = rows // CH
    row = lax.broadcasted_iota(jnp.int32, (CH, CH), 0)
    col = lax.broadcasted_iota(jnp.int32, (CH, CH), 1)
    distance = (row - col).astype(f32)
    for s in range(TILE // HD):
        head = step * (TILE // HD) + s
        cols = head_columns(s)
        rate = rates[head]
        lead = double(decay_in_of(rate))
        tail = double(decay_out_of(rate))
        mask = jnp.where(distance >= 0, jnp.exp(-rate * jnp.maximum(distance, 0.0)), 0.0)
        mask_t = jnp.where(distance <= 0, jnp.exp(rate * jnp.minimum(distance, 0.0)), 0.0)
        state = keep[0] * state_in[s].astype(f32)
        states = []
        for c in range(count):
            span = slice(c * CH, (c + 1) * CH)
            key_float = rotated(
                swish(kraw[span, cols].astype(f32)), cosine[span, :], sine[span, :]
            )
            key_s[span, :] = key_float.astype(bf16)
            states.append(state.astype(bf16))
            if c < count - 1:
                state = across[head] * state + tn(v[span, cols], (key_float * tail).astype(bf16))
        back = back_in[s].astype(f32)
        for c in reversed(range(count)):
            span = slice(c * CH, (c + 1) * CH)
            cos_c, sin_c = cosine[span, :], sine[span, :]
            query_raw = qraw[span, cols].astype(f32)
            query_float = rotated(swish(query_raw), cos_c, sin_c)
            query = query_float.astype(bf16)
            key = key_s[span, :]
            value = v[span, cols]
            do = do_in[span, cols]
            back_low = back.astype(bf16)
            weights_t = (nt(key, query) * mask_t).astype(bf16)
            dscore = (nt(do, value) * mask).astype(bf16)
            dscore_t = (nt(value, do) * mask_t).astype(bf16)
            dqr = nn(dscore, key) + lead * nn(do, states[c])
            dkr = nn(dscore_t, query) + tail * nn(value, back_low)
            dv = nn(weights_t, do) + tail[:, :HD] * nt(key, back_low)
            back = across[head] * back + tn(do, (query_float * lead).astype(bf16))
            dq = dqr[:, :HD] * cos_c + dqr[:, HD:] * sin_c
            dk = dkr[:, :HD] * cos_c + dkr[:, HD:] * sin_c
            dq_out[span, cols] = (dq * swish_slope(query_raw)).astype(bf16)
            dk_out[span, cols] = (dk * swish_slope(kraw[span, cols].astype(f32))).astype(bf16)
            dv_out[span, cols] = dv.astype(bf16)


def mix_back(part, rates, across, keep, qraw, kraw, v, do_in, cosine, sine, state_in, back_in):
    rows, width = qraw.shape
    count = width // TILE // 2
    base = part * count
    cols = pl.BlockSpec((rows, TILE), lambda i: (0, base + i))
    heads = pl.BlockSpec((TILE // HD, HD, 2 * HD), lambda i: (base + i, 0, 0))
    return pl.pallas_call(
        functools.partial(mix_back_kernel, base),
        grid=(count,),
        in_specs=[smem(), smem(), smem()]
        + [cols] * 4
        + [fixed((rows, HD)), fixed((rows, HD)), heads, heads],
        out_specs=[columns(rows, TILE)] * 3,
        out_shape=[struct((rows, width // 2), bf16)] * 3,
        scratch_shapes=[pltpu.VMEM((rows, 2 * HD), bf16)],
        compiler_params=params(),
        cost_estimate=cost(4 * rows * width * width, 8 * rows * width),
        name="mix_back",
    )(rates, across, keep, qraw, kraw, v, do_in, cosine, sine, state_in, back_in)


def query_grads_kernel(coords, a_t, dq, dk, dv, own_out, other_out, stage):
    for n, incoming in enumerate((dq, dk, dv)):
        stage[:, n * 64 : (n + 1) * 64, :] = (
            nn(a_t[...], incoming[...]).astype(bf16).reshape(SHARDS, 64, TILE)
        )
    emit(coords, stage, own_out, other_out, slice(0, 192))


def query_grads(coords, a_t, dq, dk, dv):
    depth, rows = a_t.shape
    count = dq.shape[1] // TILE
    grads = struct((2, 2, 4, count * 192, HALF), bf16)
    return pl.pallas_call(
        query_grads_kernel,
        grid=(count,),
        in_specs=[smem(), fixed((depth, rows))] + [columns(rows, TILE)] * 3,
        out_specs=[grad_block(192), grad_block(192)],
        out_shape=[grads, grads],
        scratch_shapes=[pltpu.VMEM((SHARDS, 192, TILE), bf16)],
        compiler_params=params(),
        cost_estimate=cost(6 * rows * depth * count * TILE, 10 * rows * depth),
        name="query_grads",
    )(coords, a_t, dq, dk, dv)


def input_part(coords, refs, total, held):
    incoming, weights = refs[:4], refs[4:20]
    part = None
    for n, kind in enumerate(("y", "y", "x", "x")):
        join(coords, kind, weights[4 * n : 4 * n + 4], held.at[n])
        term = nt(incoming[n][...], held[n].reshape(-1, TILE))
        part = term if part is None else part + term
    total[...] += part


def input_start_kernel(coords, *refs):
    out, total, held = refs[20:]
    step = pl.program_id(0)

    @pl.when(step == 0)
    def _():
        total[...] = jnp.zeros_like(total)

    input_part(coords, refs, total, held)

    @pl.when(step == pl.num_programs(0) - 1)
    def _():
        out[...] = total[...].astype(bf16)


def input_end_kernel(coords, start, x, dh1, *refs):
    out, total, held = refs[20:]
    step = pl.program_id(0)

    @pl.when(step == 0)
    def _():
        total[...] = start[...].astype(f32)

    input_part(coords, refs, total, held)

    @pl.when(step == pl.num_programs(0) - 1)
    def _():
        hidden = x[...].astype(f32)
        scale = lax.rsqrt(jnp.mean(hidden * hidden, axis=1, keepdims=True) + epsilon)
        normed = hidden * scale
        incoming = total[...]
        out[...] = (
            dh1[...]
            + scale * (incoming - normed * jnp.mean(normed * incoming, axis=1, keepdims=True))
        ).astype(bf16)


def input_back(part, coords, whole, grads, du, weights):
    rows, depth = du.shape
    count = depth // TILE // 2
    base = part * count
    specs, arrays = [], []
    for weight in weights:
        specs += weight.specs(64, lambda i: base + i)
        arrays += weight.arrays
    return pl.pallas_call(
        input_end_kernel if part else input_start_kernel,
        grid=(count,),
        in_specs=[smem()]
        + [fixed((rows, depth))] * len(whole)
        + [columns(rows, TILE)] * 3
        + [pl.BlockSpec((rows, TILE), lambda i: (0, base + i))]
        + specs,
        out_specs=fixed((rows, depth)),
        out_shape=struct((rows, depth), bf16),
        scratch_shapes=[
            pltpu.VMEM((rows, depth), f32),
            pltpu.VMEM((4, 4, 2, 2, 64, TILE), bf16),
        ],
        compiler_params=params(),
        cost_estimate=cost(4 * rows * depth * depth, 16 * rows * depth),
        name="input_back",
    )(coords, *whole, *grads, du, *arrays)


def square_blocks(w, shards):
    return w.reshape(shards, 64, 4, TILE).transpose(0, 2, 1, 3).reshape(shards, 256, TILE)


def square_back(blocks, shards):
    return blocks.reshape(shards, 4, 64, TILE).transpose(0, 2, 1, 3).reshape(shards * 64, 1024)


def feed_blocks(first, second, down, shards):
    hidden = first.shape[1]
    tiles = hidden // TILE

    def wide(w):
        return w.reshape(shards, 64, SHARDS, tiles, 16).transpose(0, 3, 1, 2, 4).reshape(
            shards, tiles, 64, TILE
        )

    low = down.reshape(shards, tiles, 16, 4, TILE).transpose(0, 1, 3, 2, 4)
    return jnp.concatenate(
        [wide(first), wide(second), low.reshape(shards, tiles, 64, TILE)], axis=2
    ).reshape(shards, tiles * 192, TILE)


def feed_back(blocks, shards):
    tiles = blocks.shape[1] // 192
    blocks = blocks.reshape(shards, tiles, 192, TILE)

    def wide(part):
        return part.reshape(shards, tiles, 64, SHARDS, 16).transpose(0, 2, 3, 1, 4).reshape(
            shards * 64, tiles * TILE
        )

    low = blocks[:, :, 128:].reshape(shards, tiles, 4, 16, TILE).transpose(0, 1, 3, 2, 4)
    return wide(blocks[:, :, :64]), wide(blocks[:, :, 64:128]), low.reshape(-1, 1024)


class Grid:
    def __init__(self):
        index = lax.axis_index("wt")
        self.z, self.y, self.core = index // 4, (index // 2) % 2, index % 2
        self.x = lax.axis_index("seq")

    def coords(self):
        return jnp.stack([self.z, self.y, self.core, self.x]).astype(jnp.int32)

    def over(self, axis, value):
        if axis == "x":
            return lax.ppermute(value, "seq", [(0, 1), (1, 0)])
        step = {"y": 2, "core": 1}[axis]
        return lax.ppermute(value, "wt", [(i, i ^ step) for i in range(SHARDS)])

    def corners(self, values):
        both = [(s * SHARDS + w, (1 - s) * SHARDS + (w ^ 2)) for s in range(2) for w in range(SHARDS)]
        return [
            self.over("x", values[0]),
            self.over("y", values[1]),
            lax.ppermute(values[2], ("seq", "wt"), both),
        ]

    def shifts(self, values):
        return [values[0]] + [self.shift_z(values[k], k) for k in (1, 2, 3)]

    def shift_z(self, value, k):
        return lax.ppermute(value, "wt", [(i, (i + 4 * k) % SHARDS) for i in range(SHARDS)])

    def in_order(self, flag, own, received, axis):
        near = jnp.concatenate([own, received], axis=axis)
        far = jnp.concatenate([received, own], axis=axis)
        return jnp.where(flag == 0, near, far)


class Gather:
    def __init__(self, grid, one, two):
        self.grid, self.split = grid, one.shape[0]
        both = jnp.concatenate([one, two], axis=0)
        own = lax.dynamic_slice_in_dim(both, grid.x * HALF, HALF, axis=1)
        self.got = [own] + [grid.shift_z(own, k) for k in (1, 2, 3)]

    def first(self):
        both = jnp.stack(self.got)
        self.one, self.two = both[:, : self.split], both[:, self.split :]

    def first_send(self):
        self.got = [self.grid.over("y", self.one), self.grid.over("x", self.two)]

    def second(self):
        self.one = jnp.stack([self.one, self.got[0]])
        self.two = jnp.stack([self.two, self.got[1]])

    def second_send(self):
        self.got = [self.grid.over("x", self.one), self.grid.over("y", self.two)]

    def last_send(self):
        self.one, self.two = [self.one, self.got[0]], [self.two, self.got[1]]
        self.got = [self.grid.over("core", value) for value in (*self.one, *self.two)]

    def pairs(self):
        return Gathered("y", [*self.one, *self.got[:2]]), Gathered("x", [*self.two, *self.got[2:]])


def far_kernel(count, *refs):
    owns, gots, outs = refs[:count], refs[count : 2 * count], refs[2 * count :]
    first = 0
    for own, got in zip(owns, gots):
        rows = slice(first, first + own.shape[3])
        first += own.shape[3]
        for (x_rel, y_rel), out in zip(((1, 0), (0, 1), (1, 1)), outs):
            total = own[x_rel, y_rel].astype(f32) + got[x_rel, y_rel].astype(f32)
            out[:, rows, :] = total.astype(bf16)


def far(owns, gots):
    rows = sum(own.shape[3] for own in owns)

    def spec(array):
        return pl.BlockSpec((2, 2, 1, array.shape[3], HALF), lambda i: (0, 0, i, 0, 0))

    return pl.pallas_call(
        functools.partial(far_kernel, len(owns)),
        grid=(4,),
        in_specs=[spec(array) for array in (*owns, *gots)],
        out_specs=[pl.BlockSpec((1, rows, HALF), lambda i: (i, 0, 0))] * 3,
        out_shape=[struct((4, rows, HALF), bf16)] * 3,
        compiler_params=params(),
        cost_estimate=cost(0, 0),
        name="far",
    )(*owns, *gots)


def near_kernel(count, *refs):
    owns, gots, received = refs[:count], refs[count : 2 * count], refs[2 * count : 2 * count + 3]
    outs = refs[2 * count + 3 :]
    first = 0
    for own, got in zip(owns, gots):
        rows = slice(first, first + own.shape[3])
        first += own.shape[3]
        for z_rel, out in enumerate(outs):
            total = own[0, 0, z_rel].astype(f32) + got[0, 0, z_rel].astype(f32)
            for other in received:
                total = total + other[z_rel, rows, :].astype(f32)
            out[rows, :] = total.astype(bf16)


def near(owns, gots, received):
    rows = received[0].shape[1]

    def spec(array):
        return pl.BlockSpec((1, 1, 4, array.shape[3], HALF), lambda i: (0, 0, 0, 0, 0))

    return pl.pallas_call(
        functools.partial(near_kernel, len(owns)),
        grid=(1,),
        in_specs=[spec(array) for array in (*owns, *gots)] + [fixed((4, rows, HALF))] * 3,
        out_specs=[fixed((rows, HALF))] * 4,
        out_shape=[struct((rows, HALF), bf16)] * 4,
        compiler_params=params(),
        cost_estimate=cost(0, 0),
        name="near",
    )(*owns, *gots, *received)


def last_kernel(*refs):
    *groups, out = refs
    first = 0
    for n in range(0, len(groups), 4):
        rows = slice(first, first + groups[n].shape[0])
        first += groups[n].shape[0]
        out[rows, :] = sum(part[...].astype(f32) for part in groups[n : n + 4]).astype(bf16)


def last(*groups):
    arrays = [array for group in groups for array in group]
    rows = sum(group[0].shape[0] for group in groups)
    return pl.pallas_call(
        last_kernel,
        grid=(1,),
        in_specs=[fixed(array.shape) for array in arrays],
        out_specs=fixed((rows, HALF)),
        out_shape=struct((rows, HALF), bf16),
        compiler_params=params(),
        cost_estimate=cost(0, 0),
        name="last",
    )(*arrays)


class Order:
    def __init__(self):
        self.token = None

    def point(self, *values):
        kept = values if self.token is None else (*values, self.token)
        done = lax.optimization_barrier(kept)
        self.token = done[0]
        return done[: len(values)]


class Plain:
    def coords(self):
        return jnp.zeros((4,), jnp.int32)


def natural(own, other):
    both = jnp.stack([own, other]).transpose(3, 2, 0, 4, 1, 5)
    return both.reshape(SHARDS, own.shape[3], TILE)


def body(
    activations,
    w_query,
    w_key,
    w_value,
    w_gate,
    w_out,
    w_first,
    w_second,
    w_down,
    decay_rate,
    seq_lengths,
    out_grad,
):
    seq_count = lax.axis_size("seq")
    seq_index = lax.axis_index("seq")
    direct = seq_count == 2 and lax.axis_size("wt") == SHARDS
    x = activations[0]
    og = out_grad[0]
    rows = x.shape[0]
    assert MIN_LEN % rows == 0
    tiles = w_first.shape[1] // TILE
    early = (tiles + 1) // 2

    if direct:
        grid = Grid()
        key_block, value_block, query_block, gate_block, out_block = (
            square_blocks(w, 1)[0] for w in (w_key, w_value, w_query, w_gate, w_out)
        )
        feed_block = feed_blocks(w_first, w_second, w_down, 1)[0]
        kv = Gather(grid, key_block, value_block)
        qg = Gather(
            grid,
            jnp.concatenate([query_block, out_block[:128]]),
            jnp.concatenate([gate_block, out_block[128:]]),
        )
    else:
        grid = Plain()
        full_key, full_value, full_query, full_gate, full_out = (
            square_blocks(lax.all_gather(w, "wt", axis=0, tiled=True), SHARDS)
            for w in (w_key, w_value, w_query, w_gate, w_out)
        )
        feed_weights = feed_blocks(
            *(lax.all_gather(w, "wt", axis=0, tiled=True) for w in (w_first, w_second, w_down)),
            SHARDS,
        )

        def held(block, kind):
            block = block.reshape(4, 2, 2, -1, 2, HALF)[jnp.array([0, 3, 2, 1])]
            block = block.transpose((2, 4, 1, 0, 3, 5) if kind == "y" else (2, 1, 4, 0, 3, 5))
            return Gathered(kind, [block[c, p] for c in range(2) for p in range(2)])

        keys, values = held(full_key, "y"), held(full_value, "x")
        queries = held(jnp.concatenate([full_query, full_out[:, :128]], axis=1), "y")
        gates = held(jnp.concatenate([full_gate, full_out[:, 128:]], axis=1), "x")
        feed_weights = feed_weights.reshape(4, 2, 2, -1, TILE)
    coords = grid.coords()

    lengths = seq_lengths[0]
    starts = jnp.cumsum(lengths) - lengths
    begin = seq_index * rows
    begun = (starts <= begin) & (lengths > 0)
    first_token = jnp.max(jnp.where(begun, starts, 0))
    keep = jnp.where(begin == first_token, 0.0, 1.0).astype(f32)[None]
    position = (begin - first_token + jnp.arange(rows, dtype=jnp.int32)).astype(f32)
    frequency = 10000.0 ** (-jnp.arange(HD, dtype=f32) / HD)
    angles = position[:, None] * frequency[None, :]
    cosine, sine = jnp.cos(angles), jnp.sin(angles)
    across = jnp.exp(-decay_rate * CH)
    whole = jnp.exp(-decay_rate * rows)[:, None, None]

    a, a_t = prepare(x)
    if direct:
        order = Order()
        *kv.got, a, a_t = order.point(*kv.got, a, a_t)
        kv.first()
        kv.one, kv.two, feed_block = order.point(kv.one, kv.two, feed_block)
        kv.first_send()
        kv.got = order.point(*kv.got)
        kv.second()
        kv.one, kv.two, *qg.got = order.point(kv.one, kv.two, *qg.got)
        kv.second_send()
        qg.first()
        qg.one, qg.two, feed_block = order.point(qg.one, qg.two, feed_block)
        qg.first_send()
        feed_weights = lax.all_gather(feed_block, "wt", axis=0, tiled=True)
        feed_weights = feed_weights.reshape(4, 2, 2, -1, TILE)
        *kv.got, cosine, sine = order.point(*kv.got, cosine, sine)
        kv.last_send()
        kv.got = order.point(*kv.got)
        keys, values = kv.pairs()
    kraw, v, own_state = key_value(
        decay_rate, across, coords, a, keys, values, cosine, sine, bf16 if direct else f32
    )
    ahead = [(i, i + 1) for i in range(seq_count - 1)]
    if direct:
        own_state, *qg.got = order.point(own_state, *qg.got)
        state_in = lax.ppermute(own_state, "seq", ahead)
        qg.second()
        qg.one, qg.two = order.point(qg.one, qg.two)
        qg.second_send()
        state_in, *qg.got = order.point(state_in, *qg.got)
        qg.last_send()
        queries, gates = qg.pairs()
    else:
        state_in = jnp.zeros_like(own_state)
        for _ in range(seq_count - 1):
            sent = (whole * keep * state_in + own_state).astype(bf16)
            state_in = lax.ppermute(sent, "seq", ahead).astype(f32)
    qraw, u, o, gated = mix(
        decay_rate, across, keep, coords, a, queries, gates, kraw, v, cosine, sine, state_in
    )
    h1, bn, bn_t = residual(coords, x, gated, queries, gates)
    g_early, y_part, dbn_part = feed_start(bn, bn_t, og, feed_weights, early)
    if direct:
        early_share = lax.psum_scatter(
            g_early.reshape(SHARDS, -1, TILE), "wt", scatter_dimension=0, tiled=True
        )[0]
    own_late, other_late, layer_out, dh1, dattn = feed_end(
        coords, h1, bn, bn_t, og, y_part, dbn_part, feed_weights, early
    )
    back_args = (decay_rate, across, keep, qraw, kraw, v)
    weights = (queries, keys, values, gates)
    behind = [(i + 1, i) for i in range(seq_count - 1)]
    gate_args = (decay_rate, across, keep, coords, dattn, queries, gates, o, u, qraw, cosine, sine)
    if direct:
        got_late = grid.over("core", other_late)
        du, do, own_back = gate_back(*gate_args, bf16)
        got_late, du, do, own_back = order.point(got_late, du, do, own_back)
        *sends, own_back, du = order.point(*far([own_late], [got_late]), own_back, du)
        back_in = lax.ppermute(own_back, "seq", behind)
        late_got = grid.corners(sends)
        own_og, other_og = out_gate_grads(coords, a_t, du, gated, dattn)
        own_og, other_og, back_in = order.point(own_og, other_og, back_in)
        got_og = grid.over("core", other_og)
        dq, dk, dv = mix_back(0, *back_args, do, cosine, sine, state_in, back_in)
        late_got[1], got_og, dq, dk, dv = order.point(late_got[1], got_og, dq, dk, dv)
        grads_0 = (dq, dk, dv)
        own_0, other_0 = query_grads(coords, a_t, *grads_0)
        late_got[0], own_0, other_0, do = order.point(late_got[0], own_0, other_0, do)
        got_0 = grid.over("core", other_0)
        dq, dk, dv = mix_back(1, *back_args, do, cosine, sine, state_in, back_in)
        late_got[2], got_0, dq, dk, dv = order.point(late_got[2], got_0, dq, dk, dv)
        z_sends = near([own_late], [got_late], late_got)
        *sends, dq, dk, dv = order.point(
            *z_sends, *far([own_og, own_0], [got_og, got_0]), dq, dk, dv
        )
        middle_got = grid.corners(sends[4:])
        late_got = grid.shifts(sends[:4])
        grads_1 = (dq, dk, dv)
        own_1, other_1 = query_grads(coords, a_t, *grads_1)
        own_1, other_1, du = order.point(own_1, other_1, du)
        got_1 = grid.over("core", other_1)
        partial_sum = input_back(0, coords, (), grads_0, du, weights)
        middle_got[1], got_1, partial_sum, early_share = order.point(
            middle_got[1], got_1, partial_sum, early_share
        )
        *sends, partial_sum, early_share = order.point(
            *far([own_1], [got_1]), partial_sum, early_share
        )
        end_got = grid.corners(sends)
        early_other = grid.over("x", early_share)
        input_grad = input_back(1, coords, (partial_sum, x, dh1), grads_1, du, weights)
        *rest, input_grad = order.point(middle_got[0], middle_got[2], *late_got[1:], input_grad)
        middle_got = [rest[0], middle_got[1], rest[1]]
        late_got = [late_got[0], *rest[2:]]
        sends = order.point(*near([own_og, own_0], [got_og, got_0], middle_got))
        middle_got = grid.shifts(sends)
        end_got = order.point(*end_got)
        sends = order.point(*near([own_1], [got_1], end_got))
        end_got = grid.shifts(sends)
        *middle_got, early_other = order.point(*middle_got, early_other)
        wide = order.point(last(late_got, middle_got))[0]
        wide_other = grid.over("x", wide)
        end_got = order.point(*end_got)
        narrow = order.point(last(end_got))[0]
        narrow_other = grid.over("x", narrow)
        wide_other = order.point(wide_other)[0]
        early_total = early_share.astype(f32) + early_other.astype(f32)
        wide = grid.in_order(grid.x, wide, wide_other, 1).astype(f32)
        narrow = grid.in_order(grid.x, narrow, narrow_other, 1).astype(f32)
        split = own_late.shape[3]
        feed_total = jnp.concatenate([early_total, wide[:split]])[None]
        og_total = wide[None, split : split + 512]
        qkv_total = jnp.concatenate([wide[split + 512 :], narrow])[None]
        shards = 1
    else:
        du, do, own_back = gate_back(*gate_args, f32)
        back_in = jnp.zeros_like(own_back)
        for _ in range(seq_count - 1):
            sent = (keep * whole * back_in + own_back).astype(bf16)
            back_in = lax.ppermute(sent, "seq", behind).astype(f32)
        own_og, other_og = out_gate_grads(coords, a_t, du, gated, dattn)
        parts = [
            mix_back(part, *back_args, do, cosine, sine, state_in, back_in) for part in (0, 1)
        ]
        partial_sum = input_back(0, coords, (), parts[0], du, weights)
        input_grad = input_back(1, coords, (partial_sum, x, dh1), parts[1], du, weights)
        feed_total = jnp.concatenate([g_early, natural(own_late, other_late)], axis=1)
        og_total = natural(own_og, other_og)
        qkv_total = jnp.concatenate(
            [natural(*query_grads(coords, a_t, *part)) for part in parts], axis=1
        )
        shards = SHARDS
    qkv_total = qkv_total.reshape(shards, 4, 3, 64, TILE)
    squares = [qkv_total[:, :, n] for n in range(3)] + [og_total[:, 256:], og_total[:, :256]]
    totals = [square_back(g, shards) for g in squares] + list(feed_back(feed_total, shards))
    if not direct:
        totals = [
            lax.psum(lax.psum_scatter(g, "wt", scatter_dimension=0, tiled=True), "seq").astype(f32)
            for g in totals
        ]
    return (layer_out[None], input_grad[None], *totals)


def solution(mesh):
    weight = P("wt", None)
    tokens = P("wt", "seq", None)
    return jax.shard_map(
        body,
        mesh=mesh,
        in_specs=(tokens,) + (weight,) * 8 + (P(), weight, tokens),
        out_specs=(tokens, tokens) + (weight,) * 8,
        check_vma=False,
    )
```

```python
import functools

import jax
import jax.numpy as jnp
from jax import lax
from jax.experimental import pallas as pl
from jax.experimental.pallas import tpu as pltpu
from jax.sharding import PartitionSpec as P

H = 8
HD = 128
CH = 256
TILE = 256
HALF = 128
SHARDS = 16
MIN_LEN = 1024
VMEM_LIMIT = 60 << 20

epsilon = 1e-06
head_floor = 1.0
bf16 = jnp.bfloat16
f32 = jnp.float32


def nn(left, right):
    return jnp.dot(left, right, preferred_element_type=f32)


def nt(left, right):
    return lax.dot_general(left, right, (((1,), (1,)), ((), ())), preferred_element_type=f32)


def tn(left, right):
    return lax.dot_general(left, right, (((0,), (0,)), ((), ())), preferred_element_type=f32)


def struct(shape, dtype):
    return jax.ShapeDtypeStruct(shape, dtype)


def fixed(shape):
    zeros = (0,) * len(shape)
    return pl.BlockSpec(shape, lambda i: zeros, pipeline_mode=pl.Buffered(1))


def columns(rows, width):
    return pl.BlockSpec((rows, width), lambda i: (0, i))


def row_tiles(height, cols):
    return pl.BlockSpec((height, cols), lambda i: (i, 0))


def smem():
    return pl.BlockSpec(memory_space=pltpu.SMEM)


def params():
    return pltpu.CompilerParams(vmem_limit_bytes=VMEM_LIMIT)


def cost(flops, moved):
    return pl.CostEstimate(flops=flops // 10000, bytes_accessed=moved // 10000, transcendentals=0)


class Gathered:
    def __init__(self, kind, arrays):
        self.kind, self.arrays = kind, arrays

    def specs(self, height, index):
        spec = pl.BlockSpec((2, 4, height, HALF), lambda i: (0, 0, index(i), 0))
        return [spec] * 4


def join(coords, kind, refs, held, rows=slice(None)):
    z0, y0, c0, x0 = coords[0], coords[1], coords[2], coords[3]
    for c_rel in range(2):
        core = c_rel + c0 - 2 * c_rel * c0
        pair = refs[2 * c_rel : 2 * c_rel + 2]
        for y_rel in range(2):
            y = y_rel + y0 - 2 * y_rel * y0
            for z_rel in range(4):
                z = lax.rem(z0 + 4 - z_rel, 4)
                if kind == "y":
                    here, there = pair[0][y_rel, z_rel], pair[1][y_rel, z_rel]
                else:
                    here, there = pair[y_rel][0, z_rel], pair[y_rel][1, z_rel]
                near = jnp.concatenate([here, there], axis=1)
                far = jnp.concatenate([there, here], axis=1)
                held[z, y, core, rows, :] = jnp.where(x0 == 0, near, far)


def emit(coords, stage, own, other, rows):
    z0, y0, c0, x0 = coords[0], coords[1], coords[2], coords[3]
    for x in range(2):
        x_rel = x + x0 - 2 * x * x0
        cols = slice(x * HALF, (x + 1) * HALF)
        for y_rel in range(2):
            y = y_rel + y0 - 2 * y_rel * y0
            for z_rel in range(4):
                z = lax.rem(z0 + z_rel, 4)
                shard = z * 4 + y * 2
                own[x_rel, y_rel, z_rel, rows, :] = stage[shard + c0, :, cols]
                other[x_rel, y_rel, z_rel, rows, :] = stage[shard + 1 - c0, :, cols]


def decay_in_of(rate):
    row = lax.broadcasted_iota(jnp.int32, (CH, HD), 0).astype(f32)
    return jnp.exp(-rate * (row + 1.0))


def decay_out_of(rate):
    row = lax.broadcasted_iota(jnp.int32, (CH, HD), 0).astype(f32)
    return jnp.exp(-rate * (CH - 1.0 - row))


def double(table):
    return jnp.concatenate([table, table], axis=1)


def rotated(heads, cosine, sine):
    return jnp.concatenate([heads * cosine, heads * sine], axis=1)


def swish(raw):
    return raw * jax.nn.sigmoid(raw)


def swish_slope(raw):
    sig = jax.nn.sigmoid(raw)
    return sig * (1.0 + raw * (1.0 - sig))


def head_columns(s):
    return slice(s * HD, (s + 1) * HD)


def head_states():
    return pl.BlockSpec((TILE // HD, HD, 2 * HD), lambda i: (i, 0, 0))


def prepare_kernel(x, a_out, at_out):
    value = x[...].astype(f32)
    low = (value * lax.rsqrt(jnp.mean(value * value, axis=1, keepdims=True) + epsilon)).astype(bf16)
    a_out[...] = low
    at_out[...] = low.T


def prepare(x):
    rows, depth = x.shape
    part = 512
    return pl.pallas_call(
        prepare_kernel,
        grid=(rows // part,),
        in_specs=[row_tiles(part, depth)],
        out_specs=[row_tiles(part, depth), columns(depth, part)],
        out_shape=[struct((rows, depth), bf16), struct((depth, rows), bf16)],
        compiler_params=params(),
        cost_estimate=cost(8 * rows * depth, 6 * rows * depth),
        name="prepare",
    )(x)


def key_value_kernel(
    rates, across, coords, a, cosine, sine, *refs
):
    kraw_out, v_out, state_out, held = refs[8:]
    step = pl.program_id(0)
    rows = a.shape[0]
    join(coords, "y", refs[:4], held.at[0])
    join(coords, "x", refs[4:8], held.at[1])
    kraw = nn(a[...], held[0].reshape(-1, TILE))
    v_out[...] = nn(a[...], held[1].reshape(-1, TILE)).astype(bf16)
    kraw_out[...] = kraw.astype(bf16)
    for s in range(TILE // HD):
        head = step * (TILE // HD) + s
        cols = head_columns(s)
        tail = double(decay_out_of(rates[head]))
        state = jnp.zeros((HD, 2 * HD), f32)
        for c in range(rows // CH):
            span = slice(c * CH, (c + 1) * CH)
            key = swish(kraw[span, cols])
            faded = rotated(key, cosine[span, :], sine[span, :]) * tail
            state = across[head] * state + tn(v_out[span, cols], faded.astype(bf16))
        state_out[s] = state.astype(state_out.dtype)


def key_value(rates, across, coords, a, keys, values, cosine, sine, state_type):
    rows, depth = a.shape
    return pl.pallas_call(
        key_value_kernel,
        grid=(depth // TILE,),
        in_specs=[smem(), smem(), smem(), fixed((rows, depth))]
        + [fixed((rows, HD)), fixed((rows, HD))]
        + keys.specs(64, lambda i: i)
        + values.specs(64, lambda i: i),
        out_specs=[columns(rows, TILE), columns(rows, TILE), head_states()],
        out_shape=[
            struct((rows, depth), bf16),
            struct((rows, depth), bf16),
            struct((H, HD, 2 * HD), state_type),
        ],
        scratch_shapes=[pltpu.VMEM((2, 4, 2, 2, 64, TILE), bf16)],
        compiler_params=params(),
        cost_estimate=cost(5 * rows * depth * depth, 10 * rows * depth),
        name="key_value",
    )(rates, across, coords, a, cosine, sine, *keys.arrays, *values.arrays)


def mix_kernel(rates, across, keep, coords, a, kraw, v, cosine, sine, state_in, *refs):
    qraw_out, u_out, o_out, gated_out, held = refs[8:]
    step = pl.program_id(0)
    rows = a.shape[0]
    join(coords, "y", refs[:4], held.at[0])
    join(coords, "x", refs[4:8], held.at[1])
    qraw = nn(a[...], held[0].reshape(-1, TILE))
    qraw_out[...] = qraw.astype(bf16)
    u_out[...] = nn(a[...], held[1].reshape(-1, TILE)).astype(bf16)
    row = lax.broadcasted_iota(jnp.int32, (CH, CH), 0)
    col = lax.broadcasted_iota(jnp.int32, (CH, CH), 1)
    distance = (row - col).astype(f32)
    for s in range(TILE // HD):
        head = step * (TILE // HD) + s
        cols = head_columns(s)
        rate = rates[head]
        tail = double(decay_out_of(rate))
        lead = decay_in_of(rate)
        mask = jnp.where(distance >= 0, jnp.exp(-rate * jnp.maximum(distance, 0.0)), 0.0)
        state = keep[0] * state_in[s].astype(f32)
        for c in range(rows // CH):
            span = slice(c * CH, (c + 1) * CH)
            cos_c, sin_c = cosine[span, :], sine[span, :]
            query = rotated(swish(qraw[span, cols]), cos_c, sin_c).astype(bf16)
            key_float = rotated(swish(kraw[span, cols].astype(f32)), cos_c, sin_c)
            key = key_float.astype(bf16)
            value = v[span, cols]
            weights = (nt(query, key) * mask).astype(bf16)
            o = nn(weights, value) + lead * nt(query, state.astype(bf16))
            state = across[head] * state + tn(value, (key_float * tail).astype(bf16))
            o_out[span, cols] = o.astype(bf16)
            scale = lax.rsqrt(jnp.mean(o * o, axis=1, keepdims=True) + head_floor)
            gated_out[span, cols] = (o * scale * u_out[span, cols].astype(f32)).astype(bf16)


def mix(rates, across, keep, coords, a, queries, gates, kraw, v, cosine, sine, state_in):
    rows, depth = a.shape
    return pl.pallas_call(
        mix_kernel,
        grid=(depth // TILE,),
        in_specs=[smem(), smem(), smem(), smem(), fixed((rows, depth))]
        + [
            columns(rows, TILE),
            columns(rows, TILE),
            fixed((rows, HD)),
            fixed((rows, HD)),
            head_states(),
        ]
        + queries.specs(64, lambda i: i)
        + gates.specs(64, lambda i: i),
        out_specs=[columns(rows, TILE)] * 4,
        out_shape=[struct((rows, depth), bf16)] * 4,
        scratch_shapes=[pltpu.VMEM((2, 4, 2, 2, 64, TILE), bf16)],
        compiler_params=params(),
        cost_estimate=cost(8 * rows * depth * depth, 18 * rows * depth),
        name="mix",
    )(
        rates,
        across,
        keep,
        coords,
        a,
        kraw,
        v,
        cosine,
        sine,
        state_in,
        *queries.arrays,
        *gates.arrays,
    )


def residual_kernel(coords, x, gated, *refs):
    h1_out, bn_out, bnt_out, held, h1 = refs[8:]

    @pl.when(pl.program_id(0) == 0)
    def _():
        join(coords, "y", refs[:4], held, slice(0, 128))
        join(coords, "x", refs[4:8], held, slice(128, 256))

    for b in range(4):
        cols = slice(b * TILE, (b + 1) * TILE)
        weight = held[:, :, :, b * 64 : (b + 1) * 64, :].reshape(-1, TILE)
        h1[:, cols] = x[:, cols].astype(f32) + nn(gated[...], weight)
    value = h1[...]
    h1_out[...] = value
    normed = value * lax.rsqrt(jnp.mean(value * value, axis=1, keepdims=True) + epsilon)
    low = normed.astype(bf16)
    bn_out[...] = low
    bnt_out[...] = low.T


def residual(coords, x, gated, out_lo, out_hi):
    rows, depth = x.shape
    part = 512
    return pl.pallas_call(
        residual_kernel,
        grid=(rows // part,),
        in_specs=[smem(), row_tiles(part, depth), row_tiles(part, depth)]
        + out_lo.specs(128, lambda i: 2)
        + out_hi.specs(128, lambda i: 2),
        out_specs=[row_tiles(part, depth), row_tiles(part, depth), columns(depth, part)],
        out_shape=[
            struct((rows, depth), f32),
            struct((rows, depth), bf16),
            struct((depth, rows), bf16),
        ],
        scratch_shapes=[
            pltpu.VMEM((4, 2, 2, 256, TILE), bf16),
            pltpu.VMEM((part, depth), f32),
        ],
        compiler_params=params(),
        cost_estimate=cost(2 * rows * depth * depth, 14 * rows * depth),
        name="residual",
    )(coords, x, gated, *out_lo.arrays, *out_hi.arrays)


def feed_tile(bn, bnt, og, held, down, stage, total, dbn):
    w1 = held[:, :, :, 0:64, :].reshape(-1, TILE)
    w2 = held[:, :, :, 64:128, :].reshape(-1, TILE)
    for b in range(4):
        rows = slice(128 + 16 * b, 144 + 16 * b)
        down[:, b * TILE : (b + 1) * TILE] = held[:, :, :, rows, :].reshape(TILE, TILE)
    first = nn(bn[...], w1)
    second = nn(bn[...], w2)
    middle = (first * second).astype(bf16)
    dmid = nt(og[...], down[...])
    total[...] += nn(middle, down[...])
    d_first = (dmid * second).astype(bf16)
    d_second = (dmid * first).astype(bf16)
    dbn[...] += nt(d_first, w1) + nt(d_second, w2)
    stage[:, 0:64, :] = nn(bnt[...], d_first).astype(bf16).reshape(SHARDS, 64, TILE)
    stage[:, 64:128, :] = nn(bnt[...], d_second).astype(bf16).reshape(SHARDS, 64, TILE)
    g_down = tn(middle, og[...]).astype(bf16)
    for b in range(4):
        rows = slice(128 + 16 * b, 144 + 16 * b)
        stage[:, rows, :] = g_down[:, b * TILE : (b + 1) * TILE].reshape(SHARDS, 16, TILE)


def feed_start_kernel(bn, bnt, og, w, g_out, y_out, dbn_out, down, total, dbn):
    step = pl.program_id(0)

    @pl.when(step == 0)
    def _():
        total[...] = jnp.zeros_like(total)
        dbn[...] = jnp.zeros_like(dbn)

    feed_tile(bn, bnt, og, w, down, g_out, total, dbn)

    @pl.when(step == pl.num_programs(0) - 1)
    def _():
        y_out[...] = total[...].astype(bf16)
        dbn_out[...] = dbn[...].astype(bf16)


def feed_tiles(base):
    return pl.BlockSpec((4, 2, 2, 192, TILE), lambda i: (0, 0, 0, base + i, 0))


def feed_start(bn, bnt, og, weights, tiles):
    rows, depth = bn.shape
    return pl.pallas_call(
        feed_start_kernel,
        grid=(tiles,),
        in_specs=[
            fixed((rows, depth)),
            fixed((depth, rows)),
            fixed((rows, depth)),
            feed_tiles(0),
        ],
        out_specs=[
            pl.BlockSpec((SHARDS, 192, TILE), lambda i: (0, i, 0)),
            fixed((rows, depth)),
            fixed((rows, depth)),
        ],
        out_shape=[
            struct((SHARDS, tiles * 192, TILE), bf16),
            struct((rows, depth), bf16),
            struct((rows, depth), bf16),
        ],
        scratch_shapes=[
            pltpu.VMEM((TILE, depth), bf16),
            pltpu.VMEM((rows, depth), f32),
            pltpu.VMEM((rows, depth), f32),
        ],
        compiler_params=params(),
        cost_estimate=cost(
            18 * rows * depth * tiles * TILE, 12 * depth * tiles * TILE + 10 * rows * depth
        ),
        name="feed_start",
    )(bn, bnt, og, weights)


def feed_end_kernel(coords, h1, bn, bnt, og, y_part, dbn_part, w, *refs):
    own_out, other_out, y_out, dh1_out, dattn_out, down, stage, total, dbn = refs
    step = pl.program_id(0)

    @pl.when(step == 0)
    def _():
        total[...] = h1[...] + y_part[...].astype(f32)
        dbn[...] = dbn_part[...].astype(f32)

    feed_tile(bn, bnt, og, w, down, stage, total, dbn)
    emit(coords, stage, own_out, other_out, slice(0, 192))

    @pl.when(step == pl.num_programs(0) - 1)
    def _():
        y_out[...] = total[...].astype(bf16)
        hidden = h1[...]
        scale = lax.rsqrt(jnp.mean(hidden * hidden, axis=1, keepdims=True) + epsilon)
        normed = hidden * scale
        incoming = dbn[...]
        dh1 = og[...].astype(f32) + scale * (
            incoming - normed * jnp.mean(normed * incoming, axis=1, keepdims=True)
        )
        dh1_out[...] = dh1
        dattn_out[...] = dh1.astype(bf16)


def grad_block(height):
    return pl.BlockSpec((2, 2, 4, height, HALF), lambda i: (0, 0, 0, i, 0))


def feed_end(coords, h1, bn, bnt, og, y_part, dbn_part, weights, base):
    rows, depth = bn.shape
    tiles = weights.shape[3] // 192 - base
    grads = struct((2, 2, 4, tiles * 192, HALF), bf16)
    return pl.pallas_call(
        feed_end_kernel,
        grid=(tiles,),
        in_specs=[
            smem(),
            fixed((rows, depth)),
            fixed((rows, depth)),
            fixed((depth, rows)),
            fixed((rows, depth)),
            fixed((rows, depth)),
            fixed((rows, depth)),
            feed_tiles(base),
        ],
        out_specs=[
            grad_block(192),
            grad_block(192),
            fixed((rows, depth)),
            fixed((rows, depth)),
            fixed((rows, depth)),
        ],
        out_shape=[
            grads,
            grads,
            struct((rows, depth), bf16),
            struct((rows, depth), f32),
            struct((rows, depth), bf16),
        ],
        scratch_shapes=[
            pltpu.VMEM((TILE, depth), bf16),
            pltpu.VMEM((SHARDS, 192, TILE), bf16),
            pltpu.VMEM((rows, depth), f32),
            pltpu.VMEM((rows, depth), f32),
        ],
        compiler_params=params(),
        cost_estimate=cost(
            18 * rows * depth * tiles * TILE, 12 * depth * tiles * TILE + 20 * rows * depth
        ),
        name="feed_end",
    )(coords, h1, bn, bnt, og, y_part, dbn_part, weights)


def gate_back_kernel(rates, across, keep, coords, dattn, o_in, u_in, qraw, cosine, sine, *refs):
    du_out, do_out, back_out, held = refs[8:]
    step = pl.program_id(0)
    rows = dattn.shape[0]

    @pl.when(step == 0)
    def _():
        join(coords, "y", refs[:4], held, slice(0, 128))
        join(coords, "x", refs[4:8], held, slice(128, 256))

    dgated = jnp.zeros((rows, TILE), f32)
    for b in range(4):
        weight = held[step, :, :, b * 64 : (b + 1) * 64, :].reshape(TILE, TILE)
        dgated = dgated + nt(dattn[:, b * TILE : (b + 1) * TILE], weight)
    dgated = dgated.astype(bf16).astype(f32)
    for s in range(TILE // HD):
        head = step * (TILE // HD) + s
        cols = head_columns(s)
        lead = double(decay_in_of(rates[head]))
        back = jnp.zeros((HD, 2 * HD), f32)
        for c in reversed(range(rows // CH)):
            span = slice(c * CH, (c + 1) * CH)
            o = o_in[span, cols].astype(f32)
            scale = lax.rsqrt(jnp.mean(o * o, axis=1, keepdims=True) + head_floor)
            normed = o * scale
            incoming = dgated[span, cols]
            du_out[span, cols] = (incoming * normed).astype(bf16)
            spread = incoming * u_in[span, cols].astype(f32)
            do = scale * (spread - normed * jnp.mean(normed * spread, axis=1, keepdims=True))
            low = do.astype(bf16)
            do_out[span, cols] = low
            query = rotated(swish(qraw[span, cols].astype(f32)), cosine[span, :], sine[span, :])
            back = across[head] * back + tn(low, (query * lead).astype(bf16))
        back_out[s] = (keep[0] * back).astype(back_out.dtype)


def gate_back(
    rates, across, keep, coords, dattn, out_lo, out_hi, o_in, u_in, qraw, cosine, sine, back_type
):
    rows, depth = dattn.shape
    return pl.pallas_call(
        gate_back_kernel,
        grid=(depth // TILE,),
        in_specs=[smem(), smem(), smem(), smem(), fixed((rows, depth))]
        + [
            columns(rows, TILE),
            columns(rows, TILE),
            columns(rows, TILE),
            fixed((rows, HD)),
            fixed((rows, HD)),
        ]
        + out_lo.specs(128, lambda i: 2)
        + out_hi.specs(128, lambda i: 2),
        out_specs=[columns(rows, TILE), columns(rows, TILE), head_states()],
        out_shape=[
            struct((rows, depth), bf16),
            struct((rows, depth), bf16),
            struct((H, HD, 2 * HD), back_type),
        ],
        scratch_shapes=[pltpu.VMEM((4, 2, 2, 256, TILE), bf16)],
        compiler_params=params(),
        cost_estimate=cost(3 * rows * depth * depth, 16 * rows * depth),
        name="gate_back",
    )(
        rates,
        across,
        keep,
        coords,
        dattn,
        o_in,
        u_in,
        qraw,
        cosine,
        sine,
        *out_lo.arrays,
        *out_hi.arrays,
    )


def out_gate_grads_kernel(
    coords, a_t, du, gated, dattn, own_out, other_out, stage, stage_out
):
    step = pl.program_id(0)
    z0, y0, c0, x0 = coords[0], coords[1], coords[2], coords[3]
    stage[...] = nn(a_t[...], du[...]).astype(bf16).reshape(SHARDS, 64, TILE)
    rows = pl.ds(pl.multiple_of(256 + step * 64, 64), 64)
    emit(coords, stage, own_out, other_out, rows)
    g = tn(gated[...], dattn[...]).astype(bf16)
    z_rel = lax.rem(step + 4 - z0, 4)
    for b in range(4):
        stage_out[b] = g[:, b * TILE : (b + 1) * TILE].reshape(4, 64, TILE)
        rows = slice(b * 64, (b + 1) * 64)
        for x in range(2):
            x_rel = x + x0 - 2 * x * x0
            cols = slice(x * HALF, (x + 1) * HALF)
            for y_rel in range(2):
                y = y_rel + y0 - 2 * y_rel * y0
                own_out[x_rel, y_rel, z_rel, rows, :] = stage_out[b, 2 * y + c0, :, cols]
                other_out[x_rel, y_rel, z_rel, rows, :] = stage_out[
                    b, 2 * y + 1 - c0, :, cols
                ]


def out_gate_grads(coords, a_t, du, gated, dattn):
    depth, rows = a_t.shape
    grads = struct((2, 2, 4, 512, HALF), bf16)
    return pl.pallas_call(
        out_gate_grads_kernel,
        grid=(depth // TILE,),
        in_specs=[
            smem(),
            fixed((depth, rows)),
            columns(rows, TILE),
            columns(rows, TILE),
            fixed((rows, depth)),
        ],
        out_specs=[fixed(grads.shape), fixed(grads.shape)],
        out_shape=[grads, grads],
        scratch_shapes=[
            pltpu.VMEM((SHARDS, 64, TILE), bf16),
            pltpu.VMEM((4, 4, 64, TILE), bf16),
        ],
        compiler_params=params(),
        cost_estimate=cost(4 * rows * depth * depth, 12 * rows * depth),
        name="out_gate_grads",
    )(coords, a_t, du, gated, dattn)


def mix_back_kernel(
    base,
    rates,
    across,
    keep,
    qraw,
    kraw,
    v,
    do_in,
    cosine,
    sine,
    state_in,
    back_in,
    dq_out,
    dk_out,
    dv_out,
    key_s,
):
    step = base + pl.program_id(0)
    rows = qraw.shape[0]
    count = rows // CH
    row = lax.broadcasted_iota(jnp.int32, (CH, CH), 0)
    col = lax.broadcasted_iota(jnp.int32, (CH, CH), 1)
    distance = (row - col).astype(f32)
    for s in range(TILE // HD):
        head = step * (TILE // HD) + s
        cols = head_columns(s)
        rate = rates[head]
        lead = double(decay_in_of(rate))
        tail = double(decay_out_of(rate))
        mask = jnp.where(distance >= 0, jnp.exp(-rate * jnp.maximum(distance, 0.0)), 0.0)
        mask_t = jnp.where(distance <= 0, jnp.exp(rate * jnp.minimum(distance, 0.0)), 0.0)
        state = keep[0] * state_in[s].astype(f32)
        states = []
        for c in range(count):
            span = slice(c * CH, (c + 1) * CH)
            key_float = rotated(
                swish(kraw[span, cols].astype(f32)), cosine[span, :], sine[span, :]
            )
            key_s[span, :] = key_float.astype(bf16)
            states.append(state.astype(bf16))
            if c < count - 1:
                state = across[head] * state + tn(v[span, cols], (key_float * tail).astype(bf16))
        back = back_in[s].astype(f32)
        for c in reversed(range(count)):
            span = slice(c * CH, (c + 1) * CH)
            cos_c, sin_c = cosine[span, :], sine[span, :]
            query_raw = qraw[span, cols].astype(f32)
            query_float = rotated(swish(query_raw), cos_c, sin_c)
            query = query_float.astype(bf16)
            key = key_s[span, :]
            value = v[span, cols]
            do = do_in[span, cols]
            back_low = back.astype(bf16)
            weights_t = (nt(key, query) * mask_t).astype(bf16)
            dscore = (nt(do, value) * mask).astype(bf16)
            dscore_t = (nt(value, do) * mask_t).astype(bf16)
            dqr = nn(dscore, key) + lead * nn(do, states[c])
            dkr = nn(dscore_t, query) + tail * nn(value, back_low)
            dv = nn(weights_t, do) + tail[:, :HD] * nt(key, back_low)
            back = across[head] * back + tn(do, (query_float * lead).astype(bf16))
            dq = dqr[:, :HD] * cos_c + dqr[:, HD:] * sin_c
            dk = dkr[:, :HD] * cos_c + dkr[:, HD:] * sin_c
            dq_out[span, cols] = (dq * swish_slope(query_raw)).astype(bf16)
            dk_out[span, cols] = (dk * swish_slope(kraw[span, cols].astype(f32))).astype(bf16)
            dv_out[span, cols] = dv.astype(bf16)


def mix_back(part, rates, across, keep, qraw, kraw, v, do_in, cosine, sine, state_in, back_in):
    rows, width = qraw.shape
    count = width // TILE // 2
    base = part * count
    cols = pl.BlockSpec((rows, TILE), lambda i: (0, base + i))
    heads = pl.BlockSpec((TILE // HD, HD, 2 * HD), lambda i: (base + i, 0, 0))
    return pl.pallas_call(
        functools.partial(mix_back_kernel, base),
        grid=(count,),
        in_specs=[smem(), smem(), smem()]
        + [cols] * 4
        + [fixed((rows, HD)), fixed((rows, HD)), heads, heads],
        out_specs=[columns(rows, TILE)] * 3,
        out_shape=[struct((rows, width // 2), bf16)] * 3,
        scratch_shapes=[pltpu.VMEM((rows, 2 * HD), bf16)],
        compiler_params=params(),
        cost_estimate=cost(4 * rows * width * width, 8 * rows * width),
        name="mix_back",
    )(rates, across, keep, qraw, kraw, v, do_in, cosine, sine, state_in, back_in)


def query_grads_kernel(coords, a_t, dq, dk, dv, own_out, other_out, stage):
    for n, incoming in enumerate((dq, dk, dv)):
        stage[:, n * 64 : (n + 1) * 64, :] = (
            nn(a_t[...], incoming[...]).astype(bf16).reshape(SHARDS, 64, TILE)
        )
    emit(coords, stage, own_out, other_out, slice(0, 192))


def query_grads(coords, a_t, dq, dk, dv):
    depth, rows = a_t.shape
    count = dq.shape[1] // TILE
    grads = struct((2, 2, 4, count * 192, HALF), bf16)
    return pl.pallas_call(
        query_grads_kernel,
        grid=(count,),
        in_specs=[smem(), fixed((depth, rows))] + [columns(rows, TILE)] * 3,
        out_specs=[grad_block(192), grad_block(192)],
        out_shape=[grads, grads],
        scratch_shapes=[pltpu.VMEM((SHARDS, 192, TILE), bf16)],
        compiler_params=params(),
        cost_estimate=cost(6 * rows * depth * count * TILE, 10 * rows * depth),
        name="query_grads",
    )(coords, a_t, dq, dk, dv)


def input_part(coords, refs, total, held):
    incoming, weights = refs[:4], refs[4:20]
    part = None
    for n, kind in enumerate(("y", "y", "x", "x")):
        join(coords, kind, weights[4 * n : 4 * n + 4], held.at[n])
        term = nt(incoming[n][...], held[n].reshape(-1, TILE))
        part = term if part is None else part + term
    total[...] += part


def input_start_kernel(coords, *refs):
    out, total, held = refs[20:]
    step = pl.program_id(0)

    @pl.when(step == 0)
    def _():
        total[...] = jnp.zeros_like(total)

    input_part(coords, refs, total, held)

    @pl.when(step == pl.num_programs(0) - 1)
    def _():
        out[...] = total[...].astype(bf16)


def input_end_kernel(coords, start, x, dh1, *refs):
    out, total, held = refs[20:]
    step = pl.program_id(0)

    @pl.when(step == 0)
    def _():
        total[...] = start[...].astype(f32)

    input_part(coords, refs, total, held)

    @pl.when(step == pl.num_programs(0) - 1)
    def _():
        hidden = x[...].astype(f32)
        scale = lax.rsqrt(jnp.mean(hidden * hidden, axis=1, keepdims=True) + epsilon)
        normed = hidden * scale
        incoming = total[...]
        out[...] = (
            dh1[...]
            + scale * (incoming - normed * jnp.mean(normed * incoming, axis=1, keepdims=True))
        ).astype(bf16)


def input_back(part, coords, whole, grads, du, weights):
    rows, depth = du.shape
    count = depth // TILE // 2
    base = part * count
    specs, arrays = [], []
    for weight in weights:
        specs += weight.specs(64, lambda i: base + i)
        arrays += weight.arrays
    return pl.pallas_call(
        input_end_kernel if part else input_start_kernel,
        grid=(count,),
        in_specs=[smem()]
        + [fixed((rows, depth))] * len(whole)
        + [columns(rows, TILE)] * 3
        + [pl.BlockSpec((rows, TILE), lambda i: (0, base + i))]
        + specs,
        out_specs=fixed((rows, depth)),
        out_shape=struct((rows, depth), bf16),
        scratch_shapes=[
            pltpu.VMEM((rows, depth), f32),
            pltpu.VMEM((4, 4, 2, 2, 64, TILE), bf16),
        ],
        compiler_params=params(),
        cost_estimate=cost(4 * rows * depth * depth, 16 * rows * depth),
        name="input_back",
    )(coords, *whole, *grads, du, *arrays)


def square_blocks(w, shards):
    return w.reshape(shards, 64, 4, TILE).transpose(0, 2, 1, 3).reshape(shards, 256, TILE)


def square_back(blocks, shards):
    return blocks.reshape(shards, 4, 64, TILE).transpose(0, 2, 1, 3).reshape(shards * 64, 1024)


def feed_blocks(first, second, down, shards):
    hidden = first.shape[1]
    tiles = hidden // TILE

    def wide(w):
        return w.reshape(shards, 64, SHARDS, tiles, 16).transpose(0, 3, 1, 2, 4).reshape(
            shards, tiles, 64, TILE
        )

    low = down.reshape(shards, tiles, 16, 4, TILE).transpose(0, 1, 3, 2, 4)
    return jnp.concatenate(
        [wide(first), wide(second), low.reshape(shards, tiles, 64, TILE)], axis=2
    ).reshape(shards, tiles * 192, TILE)


def feed_back(blocks, shards):
    tiles = blocks.shape[1] // 192
    blocks = blocks.reshape(shards, tiles, 192, TILE)

    def wide(part):
        return part.reshape(shards, tiles, 64, SHARDS, 16).transpose(0, 2, 3, 1, 4).reshape(
            shards * 64, tiles * TILE
        )

    low = blocks[:, :, 128:].reshape(shards, tiles, 4, 16, TILE).transpose(0, 1, 3, 2, 4)
    return wide(blocks[:, :, :64]), wide(blocks[:, :, 64:128]), low.reshape(-1, 1024)


def halves(x0, own, other):
    near = jnp.concatenate([own, other], axis=1)
    far = jnp.concatenate([other, own], axis=1)
    return jnp.where(x0 == 0, near, far)


def unpack_feed_kernel(
    coords,
    early,
    early_other,
    wide,
    wide_other,
    g1_out,
    g2_out,
    gd_out,
    out_out,
    gate_out,
    offset,
    total,
):
    early_tiles, hidden = early.shape[0] // 192, g1_out.shape[1]
    tiles = hidden // TILE
    unit = lax.broadcasted_iota(jnp.int32, offset.shape, 0)
    target = (unit // 16) * (16 * tiles) + unit % 16
    offset[...] = lax.broadcasted_iota(jnp.int32, offset.shape, 1) - target
    total[...] = jnp.zeros_like(total)

    def rows_of(tile, first, count):
        if tile < early_tiles:
            rows = slice(tile * 192 + first, tile * 192 + first + count)
            return (early[rows, :].astype(f32) + early_other[rows, :].astype(f32)).astype(bf16)
        base = (tile - early_tiles) * 192 + first
        rows = slice(base, base + count)
        return halves(coords[3], wide[rows, :], wide_other[rows, :])

    for tile in range(tiles):
        place = jnp.where(offset[...] == 16 * tile, 1.0, 0.0).astype(bf16)
        total[...] += nn(rows_of(tile, 0, 128), place)
        for b in range(4):
            low = rows_of(tile, 128 + 16 * b, 16).astype(f32)
            gd_out[16 * tile : 16 * tile + 16, b * TILE : (b + 1) * TILE] = low
    g1_out[...] = total[0:64, :]
    g2_out[...] = total[64:128, :]
    base = (tiles - early_tiles) * 192
    for out in (out_out, gate_out):
        for b in range(4):
            rows = slice(base + b * 64, base + b * 64 + 64)
            out[:, b * TILE : (b + 1) * TILE] = halves(
                coords[3], wide[rows, :], wide_other[rows, :]
            ).astype(f32)
        base += 256


def unpack_feed(coords, early, early_other, wide, wide_other):
    tiles = (early.shape[0] + wide.shape[0] - 512 - 384) // 192
    arrays = (early, early_other, wide, wide_other)
    shapes = ((64, tiles * TILE), (64, tiles * TILE), (16 * tiles, 4 * TILE), (64, 1024), (64, 1024))
    return pl.pallas_call(
        unpack_feed_kernel,
        grid=(1,),
        in_specs=[smem()] + [fixed(array.shape) for array in arrays],
        out_specs=[fixed(shape) for shape in shapes],
        out_shape=[struct(shape, f32) for shape in shapes],
        scratch_shapes=[
            pltpu.VMEM((TILE, tiles * TILE), jnp.int32),
            pltpu.VMEM((128, tiles * TILE), f32),
        ],
        compiler_params=params(),
        cost_estimate=cost(0, 0),
        name="unpack_feed",
    )(coords, *arrays)


def unpack_squares_kernel(coords, wide, wide_other, narrow, narrow_other, *outs):
    base = wide.shape[0] - 384
    for n, out in enumerate(outs):
        for b in range(4):
            first = (b % 2) * 192 + n * 64
            if b < 2:
                rows = slice(base + first, base + first + 64)
                block = halves(coords[3], wide[rows, :], wide_other[rows, :])
            else:
                rows = slice(first, first + 64)
                block = halves(coords[3], narrow[rows, :], narrow_other[rows, :])
            out[:, b * TILE : (b + 1) * TILE] = block.astype(f32)


def unpack_squares(coords, wide, wide_other, narrow, narrow_other):
    arrays = (wide, wide_other, narrow, narrow_other)
    return pl.pallas_call(
        unpack_squares_kernel,
        grid=(1,),
        in_specs=[smem()] + [fixed(array.shape) for array in arrays],
        out_specs=[fixed((64, 1024))] * 3,
        out_shape=[struct((64, 1024), f32)] * 3,
        compiler_params=params(),
        cost_estimate=cost(0, 0),
        name="unpack_squares",
    )(coords, *arrays)


class Grid:
    def __init__(self):
        index = lax.axis_index("wt")
        self.z, self.y, self.core = index // 4, (index // 2) % 2, index % 2
        self.x = lax.axis_index("seq")

    def coords(self):
        return jnp.stack([self.z, self.y, self.core, self.x]).astype(jnp.int32)

    def over(self, axis, value):
        if axis == "x":
            return lax.ppermute(value, "seq", [(0, 1), (1, 0)])
        step = {"y": 2, "core": 1}[axis]
        return lax.ppermute(value, "wt", [(i, i ^ step) for i in range(SHARDS)])

    def corners(self, values):
        both = [(s * SHARDS + w, (1 - s) * SHARDS + (w ^ 2)) for s in range(2) for w in range(SHARDS)]
        return [
            self.over("x", values[0]),
            self.over("y", values[1]),
            lax.ppermute(values[2], ("seq", "wt"), both),
        ]

    def shifts(self, values):
        return [values[0]] + [self.shift_z(values[k], k) for k in (1, 2, 3)]

    def shift_z(self, value, k):
        return lax.ppermute(value, "wt", [(i, (i + 4 * k) % SHARDS) for i in range(SHARDS)])

    def in_order(self, flag, own, received, axis):
        near = jnp.concatenate([own, received], axis=axis)
        far = jnp.concatenate([received, own], axis=axis)
        return jnp.where(flag == 0, near, far)


class Gather:
    def __init__(self, grid, one, two):
        self.grid, self.split = grid, one.shape[0]
        both = jnp.concatenate([one, two], axis=0)
        own = lax.dynamic_slice_in_dim(both, grid.x * HALF, HALF, axis=1)
        self.got = [own] + [grid.shift_z(own, k) for k in (1, 2, 3)]

    def first(self):
        both = jnp.stack(self.got)
        self.one, self.two = both[:, : self.split], both[:, self.split :]

    def first_send(self):
        self.got = [self.grid.over("y", self.one), self.grid.over("x", self.two)]

    def second(self):
        self.one = jnp.stack([self.one, self.got[0]])
        self.two = jnp.stack([self.two, self.got[1]])

    def second_send(self):
        self.got = [self.grid.over("x", self.one), self.grid.over("y", self.two)]

    def last_send(self):
        self.one, self.two = [self.one, self.got[0]], [self.two, self.got[1]]
        self.got = [self.grid.over("core", value) for value in (*self.one, *self.two)]

    def pairs(self):
        return Gathered("y", [*self.one, *self.got[:2]]), Gathered("x", [*self.two, *self.got[2:]])


def far_kernel(count, *refs):
    owns, gots, outs = refs[:count], refs[count : 2 * count], refs[2 * count :]
    first = 0
    for own, got in zip(owns, gots):
        rows = slice(first, first + own.shape[3])
        first += own.shape[3]
        for (x_rel, y_rel), out in zip(((1, 0), (0, 1), (1, 1)), outs):
            total = own[x_rel, y_rel].astype(f32) + got[x_rel, y_rel].astype(f32)
            out[:, rows, :] = total.astype(bf16)


def far(owns, gots):
    rows = sum(own.shape[3] for own in owns)

    def spec(array):
        return pl.BlockSpec((2, 2, 1, array.shape[3], HALF), lambda i: (0, 0, i, 0, 0))

    return pl.pallas_call(
        functools.partial(far_kernel, len(owns)),
        grid=(4,),
        in_specs=[spec(array) for array in (*owns, *gots)],
        out_specs=[pl.BlockSpec((1, rows, HALF), lambda i: (i, 0, 0))] * 3,
        out_shape=[struct((4, rows, HALF), bf16)] * 3,
        compiler_params=params(),
        cost_estimate=cost(0, 0),
        name="far",
    )(*owns, *gots)


def near_kernel(count, *refs):
    owns, gots, received = refs[:count], refs[count : 2 * count], refs[2 * count : 2 * count + 3]
    outs = refs[2 * count + 3 :]
    first = 0
    for own, got in zip(owns, gots):
        rows = slice(first, first + own.shape[3])
        first += own.shape[3]
        for z_rel, out in enumerate(outs):
            total = own[0, 0, z_rel].astype(f32) + got[0, 0, z_rel].astype(f32)
            for other in received:
                total = total + other[z_rel, rows, :].astype(f32)
            out[rows, :] = total.astype(bf16)


def near(owns, gots, received):
    rows = received[0].shape[1]

    def spec(array):
        return pl.BlockSpec((1, 1, 4, array.shape[3], HALF), lambda i: (0, 0, 0, 0, 0))

    return pl.pallas_call(
        functools.partial(near_kernel, len(owns)),
        grid=(1,),
        in_specs=[spec(array) for array in (*owns, *gots)] + [fixed((4, rows, HALF))] * 3,
        out_specs=[fixed((rows, HALF))] * 4,
        out_shape=[struct((rows, HALF), bf16)] * 4,
        compiler_params=params(),
        cost_estimate=cost(0, 0),
        name="near",
    )(*owns, *gots, *received)


def last_kernel(*refs):
    *groups, out = refs
    first = 0
    for n in range(0, len(groups), 4):
        rows = slice(first, first + groups[n].shape[0])
        first += groups[n].shape[0]
        out[rows, :] = sum(part[...].astype(f32) for part in groups[n : n + 4]).astype(bf16)


def last(*groups):
    arrays = [array for group in groups for array in group]
    rows = sum(group[0].shape[0] for group in groups)
    return pl.pallas_call(
        last_kernel,
        grid=(1,),
        in_specs=[fixed(array.shape) for array in arrays],
        out_specs=fixed((rows, HALF)),
        out_shape=struct((rows, HALF), bf16),
        compiler_params=params(),
        cost_estimate=cost(0, 0),
        name="last",
    )(*arrays)


class Order:
    def __init__(self):
        self.token = None

    def point(self, *values):
        kept = values if self.token is None else (*values, self.token)
        done = lax.optimization_barrier(kept)
        self.token = done[0]
        return done[: len(values)]


class Plain:
    def coords(self):
        return jnp.zeros((4,), jnp.int32)


def natural(own, other):
    both = jnp.stack([own, other]).transpose(3, 2, 0, 4, 1, 5)
    return both.reshape(SHARDS, own.shape[3], TILE)


def body(
    activations,
    w_query,
    w_key,
    w_value,
    w_gate,
    w_out,
    w_first,
    w_second,
    w_down,
    decay_rate,
    seq_lengths,
    out_grad,
):
    seq_count = lax.axis_size("seq")
    seq_index = lax.axis_index("seq")
    direct = seq_count == 2 and lax.axis_size("wt") == SHARDS
    x = activations[0]
    og = out_grad[0]
    rows = x.shape[0]
    assert MIN_LEN % rows == 0
    tiles = w_first.shape[1] // TILE
    early = (tiles + 1) // 2

    if direct:
        grid = Grid()
        key_block, value_block, query_block, gate_block, out_block = (
            square_blocks(w, 1)[0] for w in (w_key, w_value, w_query, w_gate, w_out)
        )
        feed_block = feed_blocks(w_first, w_second, w_down, 1)[0]
        kv = Gather(grid, key_block, value_block)
        qg = Gather(
            grid,
            jnp.concatenate([query_block, out_block[:128]]),
            jnp.concatenate([gate_block, out_block[128:]]),
        )
    else:
        grid = Plain()
        full_key, full_value, full_query, full_gate, full_out = (
            square_blocks(lax.all_gather(w, "wt", axis=0, tiled=True), SHARDS)
            for w in (w_key, w_value, w_query, w_gate, w_out)
        )
        feed_weights = feed_blocks(
            *(lax.all_gather(w, "wt", axis=0, tiled=True) for w in (w_first, w_second, w_down)),
            SHARDS,
        )

        def held(block, kind):
            block = block.reshape(4, 2, 2, -1, 2, HALF)[jnp.array([0, 3, 2, 1])]
            block = block.transpose((2, 4, 1, 0, 3, 5) if kind == "y" else (2, 1, 4, 0, 3, 5))
            return Gathered(kind, [block[c, p] for c in range(2) for p in range(2)])

        keys, values = held(full_key, "y"), held(full_value, "x")
        queries = held(jnp.concatenate([full_query, full_out[:, :128]], axis=1), "y")
        gates = held(jnp.concatenate([full_gate, full_out[:, 128:]], axis=1), "x")
        feed_weights = feed_weights.reshape(4, 2, 2, -1, TILE)
    coords = grid.coords()

    lengths = seq_lengths[0]
    starts = jnp.cumsum(lengths) - lengths
    begin = seq_index * rows
    begun = (starts <= begin) & (lengths > 0)
    first_token = jnp.max(jnp.where(begun, starts, 0))
    keep = jnp.where(begin == first_token, 0.0, 1.0).astype(f32)[None]
    position = (begin - first_token + jnp.arange(rows, dtype=jnp.int32)).astype(f32)
    frequency = 10000.0 ** (-jnp.arange(HD, dtype=f32) / HD)
    angles = position[:, None] * frequency[None, :]
    cosine, sine = jnp.cos(angles), jnp.sin(angles)
    across = jnp.exp(-decay_rate * CH)
    whole = jnp.exp(-decay_rate * rows)[:, None, None]

    a, a_t = prepare(x)
    if direct:
        order = Order()
        *kv.got, a, a_t = order.point(*kv.got, a, a_t)
        kv.first()
        kv.one, kv.two, feed_block = order.point(kv.one, kv.two, feed_block)
        kv.first_send()
        kv.got = order.point(*kv.got)
        kv.second()
        kv.one, kv.two, *qg.got = order.point(kv.one, kv.two, *qg.got)
        kv.second_send()
        qg.first()
        qg.one, qg.two, feed_block = order.point(qg.one, qg.two, feed_block)
        qg.first_send()
        feed_weights = lax.all_gather(feed_block, "wt", axis=0, tiled=True)
        feed_weights = feed_weights.reshape(4, 2, 2, -1, TILE)
        *kv.got, cosine, sine = order.point(*kv.got, cosine, sine)
        kv.last_send()
        kv.got = order.point(*kv.got)
        keys, values = kv.pairs()
    kraw, v, own_state = key_value(
        decay_rate, across, coords, a, keys, values, cosine, sine, bf16 if direct else f32
    )
    ahead = [(i, i + 1) for i in range(seq_count - 1)]
    if direct:
        own_state, *qg.got = order.point(own_state, *qg.got)
        state_in = lax.ppermute(own_state, "seq", ahead)
        qg.second()
        qg.one, qg.two = order.point(qg.one, qg.two)
        qg.second_send()
        state_in, *qg.got = order.point(state_in, *qg.got)
        qg.last_send()
        queries, gates = qg.pairs()
    else:
        state_in = jnp.zeros_like(own_state)
        for _ in range(seq_count - 1):
            sent = (whole * keep * state_in + own_state).astype(bf16)
            state_in = lax.ppermute(sent, "seq", ahead).astype(f32)
    qraw, u, o, gated = mix(
        decay_rate, across, keep, coords, a, queries, gates, kraw, v, cosine, sine, state_in
    )
    h1, bn, bn_t = residual(coords, x, gated, queries, gates)
    g_early, y_part, dbn_part = feed_start(bn, bn_t, og, feed_weights, early)
    if direct:
        early_share = lax.psum_scatter(
            g_early.reshape(SHARDS, -1, TILE), "wt", scatter_dimension=0, tiled=True
        )[0]
    own_late, other_late, layer_out, dh1, dattn = feed_end(
        coords, h1, bn, bn_t, og, y_part, dbn_part, feed_weights, early
    )
    back_args = (decay_rate, across, keep, qraw, kraw, v)
    weights = (queries, keys, values, gates)
    behind = [(i + 1, i) for i in range(seq_count - 1)]
    gate_args = (decay_rate, across, keep, coords, dattn, queries, gates, o, u, qraw, cosine, sine)
    if direct:
        got_late = grid.over("core", other_late)
        du, do, own_back = gate_back(*gate_args, bf16)
        got_late, du, do, own_back = order.point(got_late, du, do, own_back)
        *sends, own_back, du = order.point(*far([own_late], [got_late]), own_back, du)
        back_in = lax.ppermute(own_back, "seq", behind)
        late_got = grid.corners(sends)
        own_og, other_og = out_gate_grads(coords, a_t, du, gated, dattn)
        own_og, other_og, back_in = order.point(own_og, other_og, back_in)
        got_og = grid.over("core", other_og)
        dq, dk, dv = mix_back(0, *back_args, do, cosine, sine, state_in, back_in)
        late_got[1], dq, dk, dv = order.point(late_got[1], dq, dk, dv)
        grads_0 = (dq, dk, dv)
        own_0, other_0 = query_grads(coords, a_t, *grads_0)
        late_got[0], own_0, other_0, do = order.point(late_got[0], own_0, other_0, do)
        got_0 = grid.over("core", other_0)
        got_og, got_0, do = order.point(got_og, got_0, do)
        *sends, do = order.point(*far([own_og, own_0], [got_og, got_0]), do)
        middle_got = grid.corners(sends)
        dq, dk, dv = mix_back(1, *back_args, do, cosine, sine, state_in, back_in)
        late_got[2], dq, dk, dv = order.point(late_got[2], dq, dk, dv)
        *sends, dq, dk, dv = order.point(*near([own_late], [got_late], late_got), dq, dk, dv)
        late_got = grid.shifts(sends)
        grads_1 = (dq, dk, dv)
        own_1, other_1 = query_grads(coords, a_t, *grads_1)
        middle_got[1], own_1, other_1, du = order.point(middle_got[1], own_1, other_1, du)
        got_1 = grid.over("core", other_1)
        got_1, du = order.point(got_1, du)
        *sends, du = order.point(*far([own_1], [got_1]), du)
        end_got = grid.corners(sends)
        partial_sum = input_back(0, coords, (), grads_0, du, weights)
        middle_got[0], partial_sum = order.point(middle_got[0], partial_sum)
        input_grad = input_back(1, coords, (partial_sum, x, dh1), grads_1, du, weights)
        middle_got[2], input_grad, *rest = order.point(
            middle_got[2], input_grad, *late_got[1:]
        )
        late_got = [late_got[0], *rest]
        sends = order.point(*near([own_og, own_0], [got_og, got_0], middle_got))
        middle_got = grid.shifts(sends)
        early_share, *end_got = order.point(early_share, *end_got)
        early_other = grid.over("x", early_share)
        sends = order.point(*near([own_1], [got_1], end_got))
        end_got = grid.shifts(sends)
        middle_got = order.point(*middle_got)
        wide = order.point(last(late_got, middle_got))[0]
        wide_other = grid.over("x", wide)
        wide, wide_other, early_share, early_other = order.point(
            wide, wide_other, early_share, early_other
        )
        feed_grads = unpack_feed(coords, early_share, early_other, wide, wide_other)
        end_got = order.point(*end_got)
        narrow = order.point(last(end_got))[0]
        narrow_other = grid.over("x", narrow)
        g_first, g_second, g_down, g_out, g_gate = feed_grads
        squares = unpack_squares(coords, wide, wide_other, narrow, narrow_other)
        return (
            layer_out[None],
            input_grad[None],
            *squares,
            g_gate,
            g_out,
            g_first,
            g_second,
            g_down,
        )
    else:
        du, do, own_back = gate_back(*gate_args, f32)
        back_in = jnp.zeros_like(own_back)
        for _ in range(seq_count - 1):
            sent = (keep * whole * back_in + own_back).astype(bf16)
            back_in = lax.ppermute(sent, "seq", behind).astype(f32)
        own_og, other_og = out_gate_grads(coords, a_t, du, gated, dattn)
        parts = [
            mix_back(part, *back_args, do, cosine, sine, state_in, back_in) for part in (0, 1)
        ]
        partial_sum = input_back(0, coords, (), parts[0], du, weights)
        input_grad = input_back(1, coords, (partial_sum, x, dh1), parts[1], du, weights)
        feed_total = jnp.concatenate([g_early, natural(own_late, other_late)], axis=1)
        og_total = natural(own_og, other_og)
        qkv_total = jnp.concatenate(
            [natural(*query_grads(coords, a_t, *part)) for part in parts], axis=1
        )
    qkv_total = qkv_total.reshape(SHARDS, 4, 3, 64, TILE)
    squares = [qkv_total[:, :, n] for n in range(3)] + [og_total[:, 256:], og_total[:, :256]]
    totals = [square_back(g, SHARDS) for g in squares] + list(feed_back(feed_total, SHARDS))
    totals = [
        lax.psum(lax.psum_scatter(g, "wt", scatter_dimension=0, tiled=True), "seq").astype(f32)
        for g in totals
    ]
    return (layer_out[None], input_grad[None], *totals)


def solution(mesh):
    weight = P("wt", None)
    tokens = P("wt", "seq", None)
    return jax.shard_map(
        body,
        mesh=mesh,
        in_specs=(tokens,) + (weight,) * 8 + (P(), weight, tokens),
        out_specs=(tokens, tokens) + (weight,) * 8,
        check_vma=False,
    )
```

```python
import functools

import jax
import jax.numpy as jnp
from jax import lax
from jax.experimental import pallas as pl
from jax.experimental.pallas import tpu as pltpu
from jax.sharding import PartitionSpec as P

H = 8
HD = 128
CH = 256
TILE = 256
HALF = 128
SHARDS = 16
MIN_LEN = 1024
VMEM_LIMIT = 60 << 20

epsilon = 1e-06
head_floor = 1.0
bf16 = jnp.bfloat16
f32 = jnp.float32


def nn(left, right):
    return jnp.dot(left, right, preferred_element_type=f32)


def nt(left, right):
    return lax.dot_general(left, right, (((1,), (1,)), ((), ())), preferred_element_type=f32)


def tn(left, right):
    return lax.dot_general(left, right, (((0,), (0,)), ((), ())), preferred_element_type=f32)


def struct(shape, dtype):
    return jax.ShapeDtypeStruct(shape, dtype)


def fixed(shape):
    zeros = (0,) * len(shape)
    return pl.BlockSpec(shape, lambda i: zeros, pipeline_mode=pl.Buffered(1))


def columns(rows, width):
    return pl.BlockSpec((rows, width), lambda i: (0, i))


def row_tiles(height, cols):
    return pl.BlockSpec((height, cols), lambda i: (i, 0))


def smem():
    return pl.BlockSpec(memory_space=pltpu.SMEM)


def params():
    return pltpu.CompilerParams(vmem_limit_bytes=VMEM_LIMIT)


def cost(flops, moved):
    return pl.CostEstimate(flops=flops // 10000, bytes_accessed=moved // 10000, transcendentals=0)


class Gathered:
    def __init__(self, kind, arrays):
        self.kind, self.arrays = kind, arrays

    def specs(self, height, index):
        spec = pl.BlockSpec((2, 4, height, HALF), lambda i: (0, 0, index(i), 0))
        return [spec] * 4


def join(coords, kind, refs, held, rows=slice(None)):
    z0, y0, c0, x0 = coords[0], coords[1], coords[2], coords[3]
    for c_rel in range(2):
        core = c_rel + c0 - 2 * c_rel * c0
        pair = refs[2 * c_rel : 2 * c_rel + 2]
        for y_rel in range(2):
            y = y_rel + y0 - 2 * y_rel * y0
            for z_rel in range(4):
                z = lax.rem(z0 + 4 - z_rel, 4)
                if kind == "y":
                    here, there = pair[0][y_rel, z_rel], pair[1][y_rel, z_rel]
                else:
                    here, there = pair[y_rel][0, z_rel], pair[y_rel][1, z_rel]
                near = jnp.concatenate([here, there], axis=1)
                far = jnp.concatenate([there, here], axis=1)
                held[z, y, core, rows, :] = jnp.where(x0 == 0, near, far)


def emit(coords, stage, own, other, rows):
    z0, y0, c0, x0 = coords[0], coords[1], coords[2], coords[3]
    for x in range(2):
        x_rel = x + x0 - 2 * x * x0
        cols = slice(x * HALF, (x + 1) * HALF)
        for y_rel in range(2):
            y = y_rel + y0 - 2 * y_rel * y0
            for z_rel in range(4):
                z = lax.rem(z0 + z_rel, 4)
                shard = z * 4 + y * 2
                own[x_rel, y_rel, z_rel, rows, :] = stage[shard + c0, :, cols]
                other[x_rel, y_rel, z_rel, rows, :] = stage[shard + 1 - c0, :, cols]


def decay_in_of(rate):
    row = lax.broadcasted_iota(jnp.int32, (CH, HD), 0).astype(f32)
    return jnp.exp(-rate * (row + 1.0))


def decay_out_of(rate):
    row = lax.broadcasted_iota(jnp.int32, (CH, HD), 0).astype(f32)
    return jnp.exp(-rate * (CH - 1.0 - row))


def double(table):
    return jnp.concatenate([table, table], axis=1)


def rotated(heads, cosine, sine):
    return jnp.concatenate([heads * cosine, heads * sine], axis=1)


def swish(raw):
    return raw * jax.nn.sigmoid(raw)


def swish_slope(raw):
    sig = jax.nn.sigmoid(raw)
    return sig * (1.0 + raw * (1.0 - sig))


def head_columns(s):
    return slice(s * HD, (s + 1) * HD)


def head_states():
    return pl.BlockSpec((TILE // HD, HD, 2 * HD), lambda i: (i, 0, 0))


def prepare_kernel(x, a_out, at_out):
    value = x[...].astype(f32)
    low = (value * lax.rsqrt(jnp.mean(value * value, axis=1, keepdims=True) + epsilon)).astype(bf16)
    a_out[...] = low
    at_out[...] = low.T


def prepare(x):
    rows, depth = x.shape
    part = 512
    return pl.pallas_call(
        prepare_kernel,
        grid=(rows // part,),
        in_specs=[row_tiles(part, depth)],
        out_specs=[row_tiles(part, depth), columns(depth, part)],
        out_shape=[struct((rows, depth), bf16), struct((depth, rows), bf16)],
        compiler_params=params(),
        cost_estimate=cost(8 * rows * depth, 6 * rows * depth),
        name="prepare",
    )(x)


def key_value_kernel(
    rates, across, coords, a, cosine, sine, *refs
):
    kraw_out, v_out, state_out, held = refs[8:]
    step = pl.program_id(0)
    rows = a.shape[0]
    join(coords, "y", refs[:4], held.at[0])
    join(coords, "x", refs[4:8], held.at[1])
    kraw = nn(a[...], held[0].reshape(-1, TILE))
    v_out[...] = nn(a[...], held[1].reshape(-1, TILE)).astype(bf16)
    kraw_out[...] = kraw.astype(bf16)
    for s in range(TILE // HD):
        head = step * (TILE // HD) + s
        cols = head_columns(s)
        tail = double(decay_out_of(rates[head]))
        state = jnp.zeros((HD, 2 * HD), f32)
        for c in range(rows // CH):
            span = slice(c * CH, (c + 1) * CH)
            key = swish(kraw[span, cols])
            faded = rotated(key, cosine[span, :], sine[span, :]) * tail
            state = across[head] * state + tn(v_out[span, cols], faded.astype(bf16))
        state_out[s] = state.astype(state_out.dtype)


def key_value(rates, across, coords, a, keys, values, cosine, sine, state_type):
    rows, depth = a.shape
    return pl.pallas_call(
        key_value_kernel,
        grid=(depth // TILE,),
        in_specs=[smem(), smem(), smem(), fixed((rows, depth))]
        + [fixed((rows, HD)), fixed((rows, HD))]
        + keys.specs(64, lambda i: i)
        + values.specs(64, lambda i: i),
        out_specs=[columns(rows, TILE), columns(rows, TILE), head_states()],
        out_shape=[
            struct((rows, depth), bf16),
            struct((rows, depth), bf16),
            struct((H, HD, 2 * HD), state_type),
        ],
        scratch_shapes=[pltpu.VMEM((2, 4, 2, 2, 64, TILE), bf16)],
        compiler_params=params(),
        cost_estimate=cost(5 * rows * depth * depth, 10 * rows * depth),
        name="key_value",
    )(rates, across, coords, a, cosine, sine, *keys.arrays, *values.arrays)


def mix_kernel(rates, across, keep, coords, a, kraw, v, cosine, sine, state_in, *refs):
    qraw_out, u_out, o_out, gated_out, held = refs[8:]
    step = pl.program_id(0)
    rows = a.shape[0]
    join(coords, "y", refs[:4], held.at[0])
    join(coords, "x", refs[4:8], held.at[1])
    qraw = nn(a[...], held[0].reshape(-1, TILE))
    qraw_out[...] = qraw.astype(bf16)
    u_out[...] = nn(a[...], held[1].reshape(-1, TILE)).astype(bf16)
    row = lax.broadcasted_iota(jnp.int32, (CH, CH), 0)
    col = lax.broadcasted_iota(jnp.int32, (CH, CH), 1)
    distance = (row - col).astype(f32)
    for s in range(TILE // HD):
        head = step * (TILE // HD) + s
        cols = head_columns(s)
        rate = rates[head]
        tail = double(decay_out_of(rate))
        lead = decay_in_of(rate)
        mask = jnp.where(distance >= 0, jnp.exp(-rate * jnp.maximum(distance, 0.0)), 0.0)
        state = keep[0] * state_in[s].astype(f32)
        for c in range(rows // CH):
            span = slice(c * CH, (c + 1) * CH)
            cos_c, sin_c = cosine[span, :], sine[span, :]
            query = rotated(swish(qraw[span, cols]), cos_c, sin_c).astype(bf16)
            key_float = rotated(swish(kraw[span, cols].astype(f32)), cos_c, sin_c)
            key = key_float.astype(bf16)
            value = v[span, cols]
            weights = (nt(query, key) * mask).astype(bf16)
            o = nn(weights, value) + lead * nt(query, state.astype(bf16))
            state = across[head] * state + tn(value, (key_float * tail).astype(bf16))
            o_out[span, cols] = o.astype(bf16)
            scale = lax.rsqrt(jnp.mean(o * o, axis=1, keepdims=True) + head_floor)
            gated_out[span, cols] = (o * scale * u_out[span, cols].astype(f32)).astype(bf16)


def mix(rates, across, keep, coords, a, queries, gates, kraw, v, cosine, sine, state_in):
    rows, depth = a.shape
    return pl.pallas_call(
        mix_kernel,
        grid=(depth // TILE,),
        in_specs=[smem(), smem(), smem(), smem(), fixed((rows, depth))]
        + [
            columns(rows, TILE),
            columns(rows, TILE),
            fixed((rows, HD)),
            fixed((rows, HD)),
            head_states(),
        ]
        + queries.specs(64, lambda i: i)
        + gates.specs(64, lambda i: i),
        out_specs=[columns(rows, TILE)] * 4,
        out_shape=[struct((rows, depth), bf16)] * 4,
        scratch_shapes=[pltpu.VMEM((2, 4, 2, 2, 64, TILE), bf16)],
        compiler_params=params(),
        cost_estimate=cost(8 * rows * depth * depth, 18 * rows * depth),
        name="mix",
    )(
        rates,
        across,
        keep,
        coords,
        a,
        kraw,
        v,
        cosine,
        sine,
        state_in,
        *queries.arrays,
        *gates.arrays,
    )


def residual_kernel(coords, x, gated, *refs):
    h1_out, bn_out, bnt_out, held, h1 = refs[8:]

    @pl.when(pl.program_id(0) == 0)
    def _():
        join(coords, "y", refs[:4], held, slice(0, 128))
        join(coords, "x", refs[4:8], held, slice(128, 256))

    for b in range(4):
        cols = slice(b * TILE, (b + 1) * TILE)
        weight = held[:, :, :, b * 64 : (b + 1) * 64, :].reshape(-1, TILE)
        h1[:, cols] = x[:, cols].astype(f32) + nn(gated[...], weight)
    value = h1[...]
    h1_out[...] = value
    normed = value * lax.rsqrt(jnp.mean(value * value, axis=1, keepdims=True) + epsilon)
    low = normed.astype(bf16)
    bn_out[...] = low
    bnt_out[...] = low.T


def residual(coords, x, gated, out_lo, out_hi):
    rows, depth = x.shape
    part = 512
    return pl.pallas_call(
        residual_kernel,
        grid=(rows // part,),
        in_specs=[smem(), row_tiles(part, depth), row_tiles(part, depth)]
        + out_lo.specs(128, lambda i: 2)
        + out_hi.specs(128, lambda i: 2),
        out_specs=[row_tiles(part, depth), row_tiles(part, depth), columns(depth, part)],
        out_shape=[
            struct((rows, depth), f32),
            struct((rows, depth), bf16),
            struct((depth, rows), bf16),
        ],
        scratch_shapes=[
            pltpu.VMEM((4, 2, 2, 256, TILE), bf16),
            pltpu.VMEM((part, depth), f32),
        ],
        compiler_params=params(),
        cost_estimate=cost(2 * rows * depth * depth, 14 * rows * depth),
        name="residual",
    )(coords, x, gated, *out_lo.arrays, *out_hi.arrays)


def feed_tile(bn, bnt, og, held, down, stage, total, dbn):
    w1 = held[:, :, :, 0:64, :].reshape(-1, TILE)
    w2 = held[:, :, :, 64:128, :].reshape(-1, TILE)
    for b in range(4):
        rows = slice(128 + 16 * b, 144 + 16 * b)
        down[:, b * TILE : (b + 1) * TILE] = held[:, :, :, rows, :].reshape(TILE, TILE)
    first = nn(bn[...], w1)
    second = nn(bn[...], w2)
    middle = (first * second).astype(bf16)
    dmid = nt(og[...], down[...])
    total[...] += nn(middle, down[...])
    d_first = (dmid * second).astype(bf16)
    d_second = (dmid * first).astype(bf16)
    dbn[...] += nt(d_first, w1) + nt(d_second, w2)
    stage[:, 0:64, :] = nn(bnt[...], d_first).astype(bf16).reshape(SHARDS, 64, TILE)
    stage[:, 64:128, :] = nn(bnt[...], d_second).astype(bf16).reshape(SHARDS, 64, TILE)
    g_down = tn(middle, og[...]).astype(bf16)
    for b in range(4):
        rows = slice(128 + 16 * b, 144 + 16 * b)
        stage[:, rows, :] = g_down[:, b * TILE : (b + 1) * TILE].reshape(SHARDS, 16, TILE)


def feed_start_kernel(bn, bnt, og, w, g_out, y_out, dbn_out, down, total, dbn):
    step = pl.program_id(0)

    @pl.when(step == 0)
    def _():
        total[...] = jnp.zeros_like(total)
        dbn[...] = jnp.zeros_like(dbn)

    feed_tile(bn, bnt, og, w, down, g_out, total, dbn)

    @pl.when(step == pl.num_programs(0) - 1)
    def _():
        y_out[...] = total[...].astype(bf16)
        dbn_out[...] = dbn[...].astype(bf16)


def feed_tiles(base):
    return pl.BlockSpec((4, 2, 2, 192, TILE), lambda i: (0, 0, 0, base + i, 0))


def feed_start(bn, bnt, og, weights, tiles):
    rows, depth = bn.shape
    return pl.pallas_call(
        feed_start_kernel,
        grid=(tiles,),
        in_specs=[
            fixed((rows, depth)),
            fixed((depth, rows)),
            fixed((rows, depth)),
            feed_tiles(0),
        ],
        out_specs=[
            pl.BlockSpec((SHARDS, 192, TILE), lambda i: (0, i, 0)),
            fixed((rows, depth)),
            fixed((rows, depth)),
        ],
        out_shape=[
            struct((SHARDS, tiles * 192, TILE), bf16),
            struct((rows, depth), bf16),
            struct((rows, depth), bf16),
        ],
        scratch_shapes=[
            pltpu.VMEM((TILE, depth), bf16),
            pltpu.VMEM((rows, depth), f32),
            pltpu.VMEM((rows, depth), f32),
        ],
        compiler_params=params(),
        cost_estimate=cost(
            18 * rows * depth * tiles * TILE, 12 * depth * tiles * TILE + 10 * rows * depth
        ),
        name="feed_start",
    )(bn, bnt, og, weights)


def feed_end_kernel(coords, h1, bn, bnt, og, y_part, dbn_part, w, *refs):
    own_out, other_out, y_out, dh1_out, dattn_out, down, stage, total, dbn = refs
    step = pl.program_id(0)

    @pl.when(step == 0)
    def _():
        total[...] = h1[...] + y_part[...].astype(f32)
        dbn[...] = dbn_part[...].astype(f32)

    feed_tile(bn, bnt, og, w, down, stage, total, dbn)
    emit(coords, stage, own_out, other_out, slice(0, 192))

    @pl.when(step == pl.num_programs(0) - 1)
    def _():
        y_out[...] = total[...].astype(bf16)
        hidden = h1[...]
        scale = lax.rsqrt(jnp.mean(hidden * hidden, axis=1, keepdims=True) + epsilon)
        normed = hidden * scale
        incoming = dbn[...]
        dh1 = og[...].astype(f32) + scale * (
            incoming - normed * jnp.mean(normed * incoming, axis=1, keepdims=True)
        )
        dh1_out[...] = dh1
        dattn_out[...] = dh1.astype(bf16)


def grad_block(height):
    return pl.BlockSpec((2, 2, 4, height, HALF), lambda i: (0, 0, 0, i, 0))


def feed_end(coords, h1, bn, bnt, og, y_part, dbn_part, weights, base):
    rows, depth = bn.shape
    tiles = weights.shape[3] // 192 - base
    grads = struct((2, 2, 4, tiles * 192, HALF), bf16)
    return pl.pallas_call(
        feed_end_kernel,
        grid=(tiles,),
        in_specs=[
            smem(),
            fixed((rows, depth)),
            fixed((rows, depth)),
            fixed((depth, rows)),
            fixed((rows, depth)),
            fixed((rows, depth)),
            fixed((rows, depth)),
            feed_tiles(base),
        ],
        out_specs=[
            grad_block(192),
            grad_block(192),
            fixed((rows, depth)),
            fixed((rows, depth)),
            fixed((rows, depth)),
        ],
        out_shape=[
            grads,
            grads,
            struct((rows, depth), bf16),
            struct((rows, depth), f32),
            struct((rows, depth), bf16),
        ],
        scratch_shapes=[
            pltpu.VMEM((TILE, depth), bf16),
            pltpu.VMEM((SHARDS, 192, TILE), bf16),
            pltpu.VMEM((rows, depth), f32),
            pltpu.VMEM((rows, depth), f32),
        ],
        compiler_params=params(),
        cost_estimate=cost(
            18 * rows * depth * tiles * TILE, 12 * depth * tiles * TILE + 20 * rows * depth
        ),
        name="feed_end",
    )(coords, h1, bn, bnt, og, y_part, dbn_part, weights)


def gate_back_kernel(rates, across, keep, coords, dattn, o_in, u_in, qraw, cosine, sine, *refs):
    du_out, do_out, back_out, held = refs[8:]
    step = pl.program_id(0)
    rows = dattn.shape[0]

    @pl.when(step == 0)
    def _():
        join(coords, "y", refs[:4], held, slice(0, 128))
        join(coords, "x", refs[4:8], held, slice(128, 256))

    dgated = jnp.zeros((rows, TILE), f32)
    for b in range(4):
        weight = held[step, :, :, b * 64 : (b + 1) * 64, :].reshape(TILE, TILE)
        dgated = dgated + nt(dattn[:, b * TILE : (b + 1) * TILE], weight)
    dgated = dgated.astype(bf16).astype(f32)
    for s in range(TILE // HD):
        head = step * (TILE // HD) + s
        cols = head_columns(s)
        lead = double(decay_in_of(rates[head]))
        back = jnp.zeros((HD, 2 * HD), f32)
        for c in reversed(range(rows // CH)):
            span = slice(c * CH, (c + 1) * CH)
            o = o_in[span, cols].astype(f32)
            scale = lax.rsqrt(jnp.mean(o * o, axis=1, keepdims=True) + head_floor)
            normed = o * scale
            incoming = dgated[span, cols]
            du_out[span, cols] = (incoming * normed).astype(bf16)
            spread = incoming * u_in[span, cols].astype(f32)
            do = scale * (spread - normed * jnp.mean(normed * spread, axis=1, keepdims=True))
            low = do.astype(bf16)
            do_out[span, cols] = low
            query = rotated(swish(qraw[span, cols].astype(f32)), cosine[span, :], sine[span, :])
            back = across[head] * back + tn(low, (query * lead).astype(bf16))
        back_out[s] = (keep[0] * back).astype(back_out.dtype)


def gate_back(
    rates, across, keep, coords, dattn, out_lo, out_hi, o_in, u_in, qraw, cosine, sine, back_type
):
    rows, depth = dattn.shape
    return pl.pallas_call(
        gate_back_kernel,
        grid=(depth // TILE,),
        in_specs=[smem(), smem(), smem(), smem(), fixed((rows, depth))]
        + [
            columns(rows, TILE),
            columns(rows, TILE),
            columns(rows, TILE),
            fixed((rows, HD)),
            fixed((rows, HD)),
        ]
        + out_lo.specs(128, lambda i: 2)
        + out_hi.specs(128, lambda i: 2),
        out_specs=[columns(rows, TILE), columns(rows, TILE), head_states()],
        out_shape=[
            struct((rows, depth), bf16),
            struct((rows, depth), bf16),
            struct((H, HD, 2 * HD), back_type),
        ],
        scratch_shapes=[pltpu.VMEM((4, 2, 2, 256, TILE), bf16)],
        compiler_params=params(),
        cost_estimate=cost(3 * rows * depth * depth, 16 * rows * depth),
        name="gate_back",
    )(
        rates,
        across,
        keep,
        coords,
        dattn,
        o_in,
        u_in,
        qraw,
        cosine,
        sine,
        *out_lo.arrays,
        *out_hi.arrays,
    )


def out_gate_grads_kernel(
    coords, a_t, du, gated, dattn, own_out, other_out, stage, stage_out
):
    step = pl.program_id(0)
    z0, y0, c0, x0 = coords[0], coords[1], coords[2], coords[3]
    stage[...] = nn(a_t[...], du[...]).astype(bf16).reshape(SHARDS, 64, TILE)
    rows = pl.ds(pl.multiple_of(256 + step * 64, 64), 64)
    emit(coords, stage, own_out, other_out, rows)
    g = tn(gated[...], dattn[...]).astype(bf16)
    z_rel = lax.rem(step + 4 - z0, 4)
    for b in range(4):
        stage_out[b] = g[:, b * TILE : (b + 1) * TILE].reshape(4, 64, TILE)
        rows = slice(b * 64, (b + 1) * 64)
        for x in range(2):
            x_rel = x + x0 - 2 * x * x0
            cols = slice(x * HALF, (x + 1) * HALF)
            for y_rel in range(2):
                y = y_rel + y0 - 2 * y_rel * y0
                own_out[x_rel, y_rel, z_rel, rows, :] = stage_out[b, 2 * y + c0, :, cols]
                other_out[x_rel, y_rel, z_rel, rows, :] = stage_out[
                    b, 2 * y + 1 - c0, :, cols
                ]


def out_gate_grads(coords, a_t, du, gated, dattn):
    depth, rows = a_t.shape
    grads = struct((2, 2, 4, 512, HALF), bf16)
    return pl.pallas_call(
        out_gate_grads_kernel,
        grid=(depth // TILE,),
        in_specs=[
            smem(),
            fixed((depth, rows)),
            columns(rows, TILE),
            columns(rows, TILE),
            fixed((rows, depth)),
        ],
        out_specs=[fixed(grads.shape), fixed(grads.shape)],
        out_shape=[grads, grads],
        scratch_shapes=[
            pltpu.VMEM((SHARDS, 64, TILE), bf16),
            pltpu.VMEM((4, 4, 64, TILE), bf16),
        ],
        compiler_params=params(),
        cost_estimate=cost(4 * rows * depth * depth, 12 * rows * depth),
        name="out_gate_grads",
    )(coords, a_t, du, gated, dattn)


def mix_back_kernel(
    base,
    rates,
    across,
    keep,
    qraw,
    kraw,
    v,
    do_in,
    cosine,
    sine,
    state_in,
    back_in,
    dq_out,
    dk_out,
    dv_out,
    key_s,
):
    step = base + pl.program_id(0)
    rows = qraw.shape[0]
    count = rows // CH
    row = lax.broadcasted_iota(jnp.int32, (CH, CH), 0)
    col = lax.broadcasted_iota(jnp.int32, (CH, CH), 1)
    distance = (row - col).astype(f32)
    for s in range(TILE // HD):
        head = step * (TILE // HD) + s
        cols = head_columns(s)
        rate = rates[head]
        lead = double(decay_in_of(rate))
        tail = double(decay_out_of(rate))
        mask = jnp.where(distance >= 0, jnp.exp(-rate * jnp.maximum(distance, 0.0)), 0.0)
        mask_t = jnp.where(distance <= 0, jnp.exp(rate * jnp.minimum(distance, 0.0)), 0.0)
        state = keep[0] * state_in[s].astype(f32)
        states = []
        for c in range(count):
            span = slice(c * CH, (c + 1) * CH)
            key_float = rotated(
                swish(kraw[span, cols].astype(f32)), cosine[span, :], sine[span, :]
            )
            key_s[span, :] = key_float.astype(bf16)
            states.append(state.astype(bf16))
            if c < count - 1:
                state = across[head] * state + tn(v[span, cols], (key_float * tail).astype(bf16))
        back = back_in[s].astype(f32)
        for c in reversed(range(count)):
            span = slice(c * CH, (c + 1) * CH)
            cos_c, sin_c = cosine[span, :], sine[span, :]
            query_raw = qraw[span, cols].astype(f32)
            query_float = rotated(swish(query_raw), cos_c, sin_c)
            query = query_float.astype(bf16)
            key = key_s[span, :]
            value = v[span, cols]
            do = do_in[span, cols]
            back_low = back.astype(bf16)
            weights_t = (nt(key, query) * mask_t).astype(bf16)
            dscore = (nt(do, value) * mask).astype(bf16)
            dscore_t = (nt(value, do) * mask_t).astype(bf16)
            dqr = nn(dscore, key) + lead * nn(do, states[c])
            dkr = nn(dscore_t, query) + tail * nn(value, back_low)
            dv = nn(weights_t, do) + tail[:, :HD] * nt(key, back_low)
            back = across[head] * back + tn(do, (query_float * lead).astype(bf16))
            dq = dqr[:, :HD] * cos_c + dqr[:, HD:] * sin_c
            dk = dkr[:, :HD] * cos_c + dkr[:, HD:] * sin_c
            dq_out[span, cols] = (dq * swish_slope(query_raw)).astype(bf16)
            dk_out[span, cols] = (dk * swish_slope(kraw[span, cols].astype(f32))).astype(bf16)
            dv_out[span, cols] = dv.astype(bf16)


def mix_back(part, rates, across, keep, qraw, kraw, v, do_in, cosine, sine, state_in, back_in):
    rows, width = qraw.shape
    count = width // TILE // 2
    base = part * count
    cols = pl.BlockSpec((rows, TILE), lambda i: (0, base + i))
    heads = pl.BlockSpec((TILE // HD, HD, 2 * HD), lambda i: (base + i, 0, 0))
    return pl.pallas_call(
        functools.partial(mix_back_kernel, base),
        grid=(count,),
        in_specs=[smem(), smem(), smem()]
        + [cols] * 4
        + [fixed((rows, HD)), fixed((rows, HD)), heads, heads],
        out_specs=[columns(rows, TILE)] * 3,
        out_shape=[struct((rows, width // 2), bf16)] * 3,
        scratch_shapes=[pltpu.VMEM((rows, 2 * HD), bf16)],
        compiler_params=params(),
        cost_estimate=cost(4 * rows * width * width, 8 * rows * width),
        name="mix_back",
    )(rates, across, keep, qraw, kraw, v, do_in, cosine, sine, state_in, back_in)


def query_grads_kernel(coords, a_t, dq, dk, dv, own_out, other_out, stage):
    for n, incoming in enumerate((dq, dk, dv)):
        stage[:, n * 64 : (n + 1) * 64, :] = (
            nn(a_t[...], incoming[...]).astype(bf16).reshape(SHARDS, 64, TILE)
        )
    emit(coords, stage, own_out, other_out, slice(0, 192))


def query_grads(coords, a_t, dq, dk, dv):
    depth, rows = a_t.shape
    count = dq.shape[1] // TILE
    grads = struct((2, 2, 4, count * 192, HALF), bf16)
    return pl.pallas_call(
        query_grads_kernel,
        grid=(count,),
        in_specs=[smem(), fixed((depth, rows))] + [columns(rows, TILE)] * 3,
        out_specs=[grad_block(192), grad_block(192)],
        out_shape=[grads, grads],
        scratch_shapes=[pltpu.VMEM((SHARDS, 192, TILE), bf16)],
        compiler_params=params(),
        cost_estimate=cost(6 * rows * depth * count * TILE, 10 * rows * depth),
        name="query_grads",
    )(coords, a_t, dq, dk, dv)


def input_part(coords, refs, total, held):
    incoming, weights = refs[:4], refs[4:20]
    part = None
    for n, kind in enumerate(("y", "y", "x", "x")):
        join(coords, kind, weights[4 * n : 4 * n + 4], held.at[n])
        term = nt(incoming[n][...], held[n].reshape(-1, TILE))
        part = term if part is None else part + term
    total[...] += part


def input_start_kernel(coords, *refs):
    out, total, held = refs[20:]
    step = pl.program_id(0)

    @pl.when(step == 0)
    def _():
        total[...] = jnp.zeros_like(total)

    input_part(coords, refs, total, held)

    @pl.when(step == pl.num_programs(0) - 1)
    def _():
        out[...] = total[...].astype(bf16)


def input_end_kernel(coords, start, x, dh1, *refs):
    out, total, held = refs[20:]
    step = pl.program_id(0)

    @pl.when(step == 0)
    def _():
        total[...] = start[...].astype(f32)

    input_part(coords, refs, total, held)

    @pl.when(step == pl.num_programs(0) - 1)
    def _():
        hidden = x[...].astype(f32)
        scale = lax.rsqrt(jnp.mean(hidden * hidden, axis=1, keepdims=True) + epsilon)
        normed = hidden * scale
        incoming = total[...]
        out[...] = (
            dh1[...]
            + scale * (incoming - normed * jnp.mean(normed * incoming, axis=1, keepdims=True))
        ).astype(bf16)


def input_back(part, coords, whole, grads, du, weights):
    rows, depth = du.shape
    count = depth // TILE // 2
    base = part * count
    specs, arrays = [], []
    for weight in weights:
        specs += weight.specs(64, lambda i: base + i)
        arrays += weight.arrays
    return pl.pallas_call(
        input_end_kernel if part else input_start_kernel,
        grid=(count,),
        in_specs=[smem()]
        + [fixed((rows, depth))] * len(whole)
        + [columns(rows, TILE)] * 3
        + [pl.BlockSpec((rows, TILE), lambda i: (0, base + i))]
        + specs,
        out_specs=fixed((rows, depth)),
        out_shape=struct((rows, depth), bf16),
        scratch_shapes=[
            pltpu.VMEM((rows, depth), f32),
            pltpu.VMEM((4, 4, 2, 2, 64, TILE), bf16),
        ],
        compiler_params=params(),
        cost_estimate=cost(4 * rows * depth * depth, 16 * rows * depth),
        name="input_back",
    )(coords, *whole, *grads, du, *arrays)


def square_blocks(w, shards):
    return w.reshape(shards, 64, 4, TILE).transpose(0, 2, 1, 3).reshape(shards, 256, TILE)


def square_back(blocks, shards):
    return blocks.reshape(shards, 4, 64, TILE).transpose(0, 2, 1, 3).reshape(shards * 64, 1024)


def feed_blocks(first, second, down, shards):
    hidden = first.shape[1]
    tiles = hidden // TILE

    def wide(w):
        return w.reshape(shards, 64, SHARDS, tiles, 16).transpose(0, 3, 1, 2, 4).reshape(
            shards, tiles, 64, TILE
        )

    low = down.reshape(shards, tiles, 16, 4, TILE).transpose(0, 1, 3, 2, 4)
    return jnp.concatenate(
        [wide(first), wide(second), low.reshape(shards, tiles, 64, TILE)], axis=2
    ).reshape(shards, tiles * 192, TILE)


def feed_back(blocks, shards):
    tiles = blocks.shape[1] // 192
    blocks = blocks.reshape(shards, tiles, 192, TILE)

    def wide(part):
        return part.reshape(shards, tiles, 64, SHARDS, 16).transpose(0, 2, 3, 1, 4).reshape(
            shards * 64, tiles * TILE
        )

    low = blocks[:, :, 128:].reshape(shards, tiles, 4, 16, TILE).transpose(0, 1, 3, 2, 4)
    return wide(blocks[:, :, :64]), wide(blocks[:, :, 64:128]), low.reshape(-1, 1024)


def halves(x0, own, other):
    near = jnp.concatenate([own, other], axis=1)
    far = jnp.concatenate([other, own], axis=1)
    return jnp.where(x0 == 0, near, far)


def unpack_feed_kernel(
    coords,
    early,
    early_other,
    wide,
    wide_other,
    g1_out,
    g2_out,
    gd_out,
    out_out,
    gate_out,
    offset,
    total,
):
    early_tiles, hidden = early.shape[0] // 192, g1_out.shape[1]
    tiles = hidden // TILE
    unit = lax.broadcasted_iota(jnp.int32, offset.shape, 0)
    target = (unit // 16) * (16 * tiles) + unit % 16
    offset[...] = lax.broadcasted_iota(jnp.int32, offset.shape, 1) - target
    total[...] = jnp.zeros_like(total)

    def rows_of(tile, first, count):
        if tile < early_tiles:
            rows = slice(tile * 192 + first, tile * 192 + first + count)
            return (early[rows, :].astype(f32) + early_other[rows, :].astype(f32)).astype(bf16)
        base = (tile - early_tiles) * 192 + first
        rows = slice(base, base + count)
        return halves(coords[3], wide[rows, :], wide_other[rows, :])

    for tile in range(tiles):
        place = jnp.where(offset[...] == 16 * tile, 1.0, 0.0).astype(bf16)
        total[...] += nn(rows_of(tile, 0, 128), place)
        for b in range(4):
            low = rows_of(tile, 128 + 16 * b, 16).astype(f32)
            gd_out[16 * tile : 16 * tile + 16, b * TILE : (b + 1) * TILE] = low
    g1_out[...] = total[0:64, :]
    g2_out[...] = total[64:128, :]
    base = (tiles - early_tiles) * 192
    for out in (out_out, gate_out):
        for b in range(4):
            rows = slice(base + b * 64, base + b * 64 + 64)
            out[:, b * TILE : (b + 1) * TILE] = halves(
                coords[3], wide[rows, :], wide_other[rows, :]
            ).astype(f32)
        base += 256


def unpack_feed(coords, early, early_other, wide, wide_other):
    tiles = (early.shape[0] + wide.shape[0] - 512 - 384) // 192
    arrays = (early, early_other, wide, wide_other)
    shapes = ((64, tiles * TILE), (64, tiles * TILE), (16 * tiles, 4 * TILE), (64, 1024), (64, 1024))
    return pl.pallas_call(
        unpack_feed_kernel,
        grid=(1,),
        in_specs=[smem()] + [fixed(array.shape) for array in arrays],
        out_specs=[fixed(shape) for shape in shapes],
        out_shape=[struct(shape, f32) for shape in shapes],
        scratch_shapes=[
            pltpu.VMEM((TILE, tiles * TILE), jnp.int32),
            pltpu.VMEM((128, tiles * TILE), f32),
        ],
        compiler_params=params(),
        cost_estimate=cost(0, 0),
        name="unpack_feed",
    )(coords, *arrays)


def unpack_squares_kernel(coords, wide, wide_other, narrow, narrow_other, *outs):
    base = wide.shape[0] - 384
    for n, out in enumerate(outs):
        for b in range(4):
            first = (b % 2) * 192 + n * 64
            if b < 2:
                rows = slice(base + first, base + first + 64)
                block = halves(coords[3], wide[rows, :], wide_other[rows, :])
            else:
                rows = slice(first, first + 64)
                block = halves(coords[3], narrow[rows, :], narrow_other[rows, :])
            out[:, b * TILE : (b + 1) * TILE] = block.astype(f32)


def unpack_squares(coords, wide, wide_other, narrow, narrow_other):
    arrays = (wide, wide_other, narrow, narrow_other)
    return pl.pallas_call(
        unpack_squares_kernel,
        grid=(1,),
        in_specs=[smem()] + [fixed(array.shape) for array in arrays],
        out_specs=[fixed((64, 1024))] * 3,
        out_shape=[struct((64, 1024), f32)] * 3,
        compiler_params=params(),
        cost_estimate=cost(0, 0),
        name="unpack_squares",
    )(coords, *arrays)


class Grid:
    def __init__(self):
        index = lax.axis_index("wt")
        self.z, self.y, self.core = index // 4, (index // 2) % 2, index % 2
        self.x = lax.axis_index("seq")

    def coords(self):
        return jnp.stack([self.z, self.y, self.core, self.x]).astype(jnp.int32)

    def over(self, axis, value):
        if axis == "x":
            return lax.ppermute(value, "seq", [(0, 1), (1, 0)])
        step = {"y": 2, "core": 1}[axis]
        return lax.ppermute(value, "wt", [(i, i ^ step) for i in range(SHARDS)])

    def corners(self, values):
        both = [(s * SHARDS + w, (1 - s) * SHARDS + (w ^ 2)) for s in range(2) for w in range(SHARDS)]
        return [
            self.over("x", values[0]),
            self.over("y", values[1]),
            lax.ppermute(values[2], ("seq", "wt"), both),
        ]

    def shifts(self, values):
        return [values[0]] + [self.shift_z(values[k], k) for k in (1, 2, 3)]

    def shift_z(self, value, k):
        return lax.ppermute(value, "wt", [(i, (i + 4 * k) % SHARDS) for i in range(SHARDS)])

    def in_order(self, flag, own, received, axis):
        near = jnp.concatenate([own, received], axis=axis)
        far = jnp.concatenate([received, own], axis=axis)
        return jnp.where(flag == 0, near, far)


class Gather:
    def __init__(self, grid, one, two):
        self.grid, self.split = grid, one.shape[0]
        both = jnp.concatenate([one, two], axis=0)
        own = lax.dynamic_slice_in_dim(both, grid.x * HALF, HALF, axis=1)
        self.got = [own] + [grid.shift_z(own, k) for k in (1, 2, 3)]

    def first(self):
        both = jnp.stack(self.got)
        self.one, self.two = both[:, : self.split], both[:, self.split :]

    def first_send(self):
        self.got = [self.grid.over("y", self.one), self.grid.over("x", self.two)]

    def second(self):
        self.one = jnp.stack([self.one, self.got[0]])
        self.two = jnp.stack([self.two, self.got[1]])

    def second_send(self):
        self.got = [self.grid.over("x", self.one), self.grid.over("y", self.two)]

    def last_send(self):
        self.one, self.two = [self.one, self.got[0]], [self.two, self.got[1]]
        self.got = [self.grid.over("core", value) for value in (*self.one, *self.two)]

    def pairs(self):
        return Gathered("y", [*self.one, *self.got[:2]]), Gathered("x", [*self.two, *self.got[2:]])


def far_kernel(count, *refs):
    owns, gots, outs = refs[:count], refs[count : 2 * count], refs[2 * count :]
    first = 0
    for own, got in zip(owns, gots):
        rows = slice(first, first + own.shape[3])
        first += own.shape[3]
        for (x_rel, y_rel), out in zip(((1, 0), (0, 1), (1, 1)), outs):
            total = own[x_rel, y_rel].astype(f32) + got[x_rel, y_rel].astype(f32)
            out[:, rows, :] = total.astype(bf16)


def far(owns, gots):
    rows = sum(own.shape[3] for own in owns)

    def spec(array):
        return pl.BlockSpec((2, 2, 1, array.shape[3], HALF), lambda i: (0, 0, i, 0, 0))

    return pl.pallas_call(
        functools.partial(far_kernel, len(owns)),
        grid=(4,),
        in_specs=[spec(array) for array in (*owns, *gots)],
        out_specs=[pl.BlockSpec((1, rows, HALF), lambda i: (i, 0, 0))] * 3,
        out_shape=[struct((4, rows, HALF), bf16)] * 3,
        compiler_params=params(),
        cost_estimate=cost(0, 0),
        name="far",
    )(*owns, *gots)


def near_kernel(count, *refs):
    owns, gots, received = refs[:count], refs[count : 2 * count], refs[2 * count : 2 * count + 3]
    outs = refs[2 * count + 3 :]
    first = 0
    for own, got in zip(owns, gots):
        rows = slice(first, first + own.shape[3])
        first += own.shape[3]
        for z_rel, out in enumerate(outs):
            total = own[0, 0, z_rel].astype(f32) + got[0, 0, z_rel].astype(f32)
            for other in received:
                total = total + other[z_rel, rows, :].astype(f32)
            out[rows, :] = total.astype(bf16)


def near(owns, gots, received):
    rows = received[0].shape[1]

    def spec(array):
        return pl.BlockSpec((1, 1, 4, array.shape[3], HALF), lambda i: (0, 0, 0, 0, 0))

    return pl.pallas_call(
        functools.partial(near_kernel, len(owns)),
        grid=(1,),
        in_specs=[spec(array) for array in (*owns, *gots)] + [fixed((4, rows, HALF))] * 3,
        out_specs=[fixed((rows, HALF))] * 4,
        out_shape=[struct((rows, HALF), bf16)] * 4,
        compiler_params=params(),
        cost_estimate=cost(0, 0),
        name="near",
    )(*owns, *gots, *received)


def last_kernel(*refs):
    *groups, out = refs
    first = 0
    for n in range(0, len(groups), 4):
        rows = slice(first, first + groups[n].shape[0])
        first += groups[n].shape[0]
        out[rows, :] = sum(part[...].astype(f32) for part in groups[n : n + 4]).astype(bf16)


def last(*groups):
    arrays = [array for group in groups for array in group]
    rows = sum(group[0].shape[0] for group in groups)
    return pl.pallas_call(
        last_kernel,
        grid=(1,),
        in_specs=[fixed(array.shape) for array in arrays],
        out_specs=fixed((rows, HALF)),
        out_shape=struct((rows, HALF), bf16),
        compiler_params=params(),
        cost_estimate=cost(0, 0),
        name="last",
    )(*arrays)


class Order:
    def __init__(self):
        self.token = None

    def point(self, *values):
        kept = values if self.token is None else (*values, self.token)
        done = lax.optimization_barrier(kept)
        self.token = done[0]
        return done[: len(values)]


class Plain:
    def coords(self):
        return jnp.zeros((4,), jnp.int32)


def natural(own, other):
    both = jnp.stack([own, other]).transpose(3, 2, 0, 4, 1, 5)
    return both.reshape(SHARDS, own.shape[3], TILE)


def body(
    activations,
    w_query,
    w_key,
    w_value,
    w_gate,
    w_out,
    w_first,
    w_second,
    w_down,
    decay_rate,
    seq_lengths,
    out_grad,
):
    seq_count = lax.axis_size("seq")
    seq_index = lax.axis_index("seq")
    direct = seq_count == 2 and lax.axis_size("wt") == SHARDS
    x = activations[0]
    og = out_grad[0]
    rows = x.shape[0]
    assert MIN_LEN % rows == 0
    tiles = w_first.shape[1] // TILE
    early = (tiles + 1) // 2

    if direct:
        grid = Grid()
        key_block, value_block, query_block, gate_block, out_block = (
            square_blocks(w, 1)[0] for w in (w_key, w_value, w_query, w_gate, w_out)
        )
        feed_block = feed_blocks(w_first, w_second, w_down, 1)[0]
        kv = Gather(grid, key_block, value_block)
        qg = Gather(
            grid,
            jnp.concatenate([query_block, out_block[:128]]),
            jnp.concatenate([gate_block, out_block[128:]]),
        )
    else:
        grid = Plain()
        full_key, full_value, full_query, full_gate, full_out = (
            square_blocks(lax.all_gather(w, "wt", axis=0, tiled=True), SHARDS)
            for w in (w_key, w_value, w_query, w_gate, w_out)
        )
        feed_weights = feed_blocks(
            *(lax.all_gather(w, "wt", axis=0, tiled=True) for w in (w_first, w_second, w_down)),
            SHARDS,
        )

        def held(block, kind):
            block = block.reshape(4, 2, 2, -1, 2, HALF)[jnp.array([0, 3, 2, 1])]
            block = block.transpose((2, 4, 1, 0, 3, 5) if kind == "y" else (2, 1, 4, 0, 3, 5))
            return Gathered(kind, [block[c, p] for c in range(2) for p in range(2)])

        keys, values = held(full_key, "y"), held(full_value, "x")
        queries = held(jnp.concatenate([full_query, full_out[:, :128]], axis=1), "y")
        gates = held(jnp.concatenate([full_gate, full_out[:, 128:]], axis=1), "x")
        feed_weights = feed_weights.reshape(4, 2, 2, -1, TILE)
    coords = grid.coords()

    lengths = seq_lengths[0]
    starts = jnp.cumsum(lengths) - lengths
    begin = seq_index * rows
    begun = (starts <= begin) & (lengths > 0)
    first_token = jnp.max(jnp.where(begun, starts, 0))
    keep = jnp.where(begin == first_token, 0.0, 1.0).astype(f32)[None]
    position = (begin - first_token + jnp.arange(rows, dtype=jnp.int32)).astype(f32)
    frequency = 10000.0 ** (-jnp.arange(HD, dtype=f32) / HD)
    angles = position[:, None] * frequency[None, :]
    cosine, sine = jnp.cos(angles), jnp.sin(angles)
    across = jnp.exp(-decay_rate * CH)
    whole = jnp.exp(-decay_rate * rows)[:, None, None]

    a, a_t = prepare(x)
    if direct:
        order = Order()
        *kv.got, a, a_t = order.point(*kv.got, a, a_t)
        kv.first()
        kv.one, kv.two, feed_block = order.point(kv.one, kv.two, feed_block)
        kv.first_send()
        kv.got = order.point(*kv.got)
        kv.second()
        kv.one, kv.two, *qg.got = order.point(kv.one, kv.two, *qg.got)
        kv.second_send()
        qg.first()
        qg.one, qg.two, feed_block = order.point(qg.one, qg.two, feed_block)
        qg.first_send()
        feed_weights = lax.all_gather(feed_block, "wt", axis=0, tiled=True)
        feed_weights = feed_weights.reshape(4, 2, 2, -1, TILE)
        *kv.got, cosine, sine = order.point(*kv.got, cosine, sine)
        kv.last_send()
        kv.got = order.point(*kv.got)
        keys, values = kv.pairs()
    kraw, v, own_state = key_value(
        decay_rate, across, coords, a, keys, values, cosine, sine, bf16 if direct else f32
    )
    ahead = [(i, i + 1) for i in range(seq_count - 1)]
    if direct:
        own_state, *qg.got = order.point(own_state, *qg.got)
        state_in = lax.ppermute(own_state, "seq", ahead)
        qg.second()
        qg.one, qg.two = order.point(qg.one, qg.two)
        qg.second_send()
        state_in, *qg.got = order.point(state_in, *qg.got)
        qg.last_send()
        queries, gates = qg.pairs()
    else:
        state_in = jnp.zeros_like(own_state)
        for _ in range(seq_count - 1):
            sent = (whole * keep * state_in + own_state).astype(bf16)
            state_in = lax.ppermute(sent, "seq", ahead).astype(f32)
    qraw, u, o, gated = mix(
        decay_rate, across, keep, coords, a, queries, gates, kraw, v, cosine, sine, state_in
    )
    h1, bn, bn_t = residual(coords, x, gated, queries, gates)
    g_early, y_part, dbn_part = feed_start(bn, bn_t, og, feed_weights, early)
    if direct:
        early_share = lax.psum_scatter(
            g_early.reshape(SHARDS, -1, TILE), "wt", scatter_dimension=0, tiled=True
        )[0]
    own_late, other_late, layer_out, dh1, dattn = feed_end(
        coords, h1, bn, bn_t, og, y_part, dbn_part, feed_weights, early
    )
    back_args = (decay_rate, across, keep, qraw, kraw, v)
    weights = (queries, keys, values, gates)
    behind = [(i + 1, i) for i in range(seq_count - 1)]
    gate_args = (decay_rate, across, keep, coords, dattn, queries, gates, o, u, qraw, cosine, sine)
    if direct:
        got_late = grid.over("core", other_late)
        du, do, own_back = gate_back(*gate_args, bf16)
        got_late, du, do, own_back = order.point(got_late, du, do, own_back)
        *sends, own_back, du = order.point(*far([own_late], [got_late]), own_back, du)
        back_in = lax.ppermute(own_back, "seq", behind)
        late_got = grid.corners(sends)
        own_og, other_og = out_gate_grads(coords, a_t, du, gated, dattn)
        own_og, other_og, back_in = order.point(own_og, other_og, back_in)
        got_og = grid.over("core", other_og)
        dq, dk, dv = mix_back(0, *back_args, do, cosine, sine, state_in, back_in)
        late_got[1], dq, dk, dv = order.point(late_got[1], dq, dk, dv)
        grads_0 = (dq, dk, dv)
        own_0, other_0 = query_grads(coords, a_t, *grads_0)
        late_got[0], own_0, other_0, do = order.point(late_got[0], own_0, other_0, do)
        got_0 = grid.over("core", other_0)
        got_og, got_0, do = order.point(got_og, got_0, do)
        *sends, do = order.point(*far([own_og, own_0], [got_og, got_0]), do)
        middle_got = grid.corners(sends)
        dq, dk, dv = mix_back(1, *back_args, do, cosine, sine, state_in, back_in)
        late_got[2], dq, dk, dv = order.point(late_got[2], dq, dk, dv)
        *sends, dq, dk, dv = order.point(*near([own_late], [got_late], late_got), dq, dk, dv)
        late_got = grid.shifts(sends)
        grads_1 = (dq, dk, dv)
        own_1, other_1 = query_grads(coords, a_t, *grads_1)
        middle_got[1], own_1, other_1, du = order.point(middle_got[1], own_1, other_1, du)
        got_1 = grid.over("core", other_1)
        got_1, du = order.point(got_1, du)
        *sends, du = order.point(*far([own_1], [got_1]), du)
        end_got = grid.corners(sends)
        partial_sum = input_back(0, coords, (), grads_0, du, weights)
        middle_got[0], middle_got[2], partial_sum, *rest = order.point(
            middle_got[0], middle_got[2], partial_sum, *late_got[1:]
        )
        late_got = [late_got[0], *rest]
        *sends, partial_sum, early_share = order.point(
            *near([own_og, own_0], [got_og, got_0], middle_got), partial_sum, early_share
        )
        middle_got = grid.shifts(sends)
        early_other = grid.over("x", early_share)
        input_grad = input_back(1, coords, (partial_sum, x, dh1), grads_1, du, weights)
        input_grad = order.point(input_grad)[0]
        end_got = order.point(*end_got)
        sends = order.point(*near([own_1], [got_1], end_got))
        end_got = grid.shifts(sends)
        middle_got = order.point(*middle_got)
        wide = order.point(last(late_got, middle_got))[0]
        wide_other = grid.over("x", wide)
        end_got = order.point(*end_got)
        narrow = order.point(last(end_got))[0]
        narrow_other = grid.over("x", narrow)
        feed_grads = unpack_feed(coords, early_share, early_other, wide, wide_other)
        g_first, g_second, g_down, g_out, g_gate = feed_grads
        squares = unpack_squares(coords, wide, wide_other, narrow, narrow_other)
        return (
            layer_out[None],
            input_grad[None],
            *squares,
            g_gate,
            g_out,
            g_first,
            g_second,
            g_down,
        )
    else:
        du, do, own_back = gate_back(*gate_args, f32)
        back_in = jnp.zeros_like(own_back)
        for _ in range(seq_count - 1):
            sent = (keep * whole * back_in + own_back).astype(bf16)
            back_in = lax.ppermute(sent, "seq", behind).astype(f32)
        own_og, other_og = out_gate_grads(coords, a_t, du, gated, dattn)
        parts = [
            mix_back(part, *back_args, do, cosine, sine, state_in, back_in) for part in (0, 1)
        ]
        partial_sum = input_back(0, coords, (), parts[0], du, weights)
        input_grad = input_back(1, coords, (partial_sum, x, dh1), parts[1], du, weights)
        feed_total = jnp.concatenate([g_early, natural(own_late, other_late)], axis=1)
        og_total = natural(own_og, other_og)
        qkv_total = jnp.concatenate(
            [natural(*query_grads(coords, a_t, *part)) for part in parts], axis=1
        )
    qkv_total = qkv_total.reshape(SHARDS, 4, 3, 64, TILE)
    squares = [qkv_total[:, :, n] for n in range(3)] + [og_total[:, 256:], og_total[:, :256]]
    totals = [square_back(g, SHARDS) for g in squares] + list(feed_back(feed_total, SHARDS))
    totals = [
        lax.psum(lax.psum_scatter(g, "wt", scatter_dimension=0, tiled=True), "seq").astype(f32)
        for g in totals
    ]
    return (layer_out[None], input_grad[None], *totals)


def solution(mesh):
    weight = P("wt", None)
    tokens = P("wt", "seq", None)
    return jax.shard_map(
        body,
        mesh=mesh,
        in_specs=(tokens,) + (weight,) * 8 + (P(), weight, tokens),
        out_specs=(tokens, tokens) + (weight,) * 8,
        check_vma=False,
    )
```
